32 devices in a mesh: lat: 4 (over z), lon: 4 (over y, core), buf: 2 (over x).
Axes of the slice: x: 2, y: 2, z: 4, core: 2. Of those that a mesh axis runs over, the one named last changes fastest.
Arguments:
- store: bfloat16 [8, 64, 64, 1725], P('buf', ('lat', 'lon')), may hold values from -6 to 6
- sample_index: int32 [6], replicated, may hold values from 0 to 7, as said below
- region_ids: int32 [64, 64], replicated, may hold values from 0 to 2
- w_embed: bfloat16 [1725, 512], replicated, may hold values from -0.15625 to 0.15625
- attn_gain: float32 [512], replicated, may hold values from 0.1 to 1.9
- w_qkv: bfloat16 [512, 1536], replicated, may hold values from -8 to 8
- w_out: bfloat16 [512, 512], replicated, may hold values from -0.25 to 0.25
- out_gain: float32 [512], replicated, may hold values from 0.1 to 1.9
- w_dec: bfloat16 [512, 1725], replicated, may hold values from -0.25 to 0.25
Outputs:
- new_store: bfloat16 [8, 64, 64, 1725], P('buf', ('lat', 'lon'))
The draws below stay inside these ranges and needn't reach their ends.
Inputs may be any that keep to these rules, and one draw needn't show every extreme that they name: `sample_index`: distinct slot numbers.
All inputs are finite; a program needn't handle non-finite values.
Results may differ from the reference program's by a relative error of at most 0.007.
Values may be sent and summed in bfloat16 or wider, within the bound.
A program may use at most 128 MiB of HBM per device.

```python
import math
import jax
import jax.numpy as jnp
from jax import lax

D = 512
HEADS = 8
HDIM = 64
CPP = 1725
WIN = 8
SLOTS = 8
B = 6
HT = 64
WT = 64


def draw_sample_index(key, part):
    order = jax.random.permutation(jax.random.fold_in(key, 21), SLOTS)
    return order[:B].astype(jnp.int32)


def draw_w_qkv(key, part):
    entries = jax.random.normal(jax.random.fold_in(key, 11), (D, 3 * D), jnp.float32)
    entries = jnp.clip(entries, -6.0, 6.0) * D ** (-0.5)
    return jnp.clip(entries, -8.0, 8.0).astype(jnp.bfloat16)


def touch_ends(result, stream_key, least, top_value):
    longest = result.shape.index(max(result.shape))
    spots = []
    for shift in (0, 1):
        where = [jax.random.randint(jax.random.fold_in(stream_key, axis), (), 0, length) for axis, length in enumerate(result.shape)]
        where[longest] = (where[longest] + shift) % result.shape[longest]
        spots.append(tuple(where))
    return result.at[spots[0]].set(least).at[spots[1]].set(top_value)


def shard_levels(own_key, shape, split, low, largest):
    factor_of, own = 1.0, jax.random.fold_in(own_key, 6)
    for dim, shards_of in split:
        heights = jnp.exp(jax.random.uniform(jax.random.fold_in(own, dim), (shards_of,), jnp.float32, low / len(split), largest / len(split)))
        factor_of = factor_of * jnp.repeat(heights, shape[dim] // shards_of).reshape([-1 if axis == dim else 1 for axis in range(len(shape))])
    return factor_of


def gaussian(stream_key, dims, width, most, cuts=(), kind=jnp.bfloat16):
    array = jax.random.normal(stream_key, dims, jnp.float32) * width
    if len(cuts) > 0:
        array = shard_levels(stream_key, dims, cuts, -0.22, 0.18) * array
    return jnp.clip(array, min=-most, max=most).astype(kind)


def setup_inputs(seed: int = 0) -> dict:
    streams_of = jax.random.split(jax.random.key(seed), 10)
    store = gaussian(streams_of[0], (SLOTS, HT, WT, CPP), 1.0, 6.0, ((0, 2), (1, 16)))
    sample_index = draw_sample_index(jax.random.fold_in(streams_of[9], 71), 0)
    region_ids = touch_ends(jax.random.randint(streams_of[2], (HT, WT), 0, 3), jax.random.fold_in(streams_of[2], 1), 0, 2).astype(jnp.int32)
    w_embed = gaussian(streams_of[3], (CPP, D), CPP ** -0.5, 0.15625)
    attn_gain = jnp.clip(1.0 + 0.18 * jax.random.normal(streams_of[4], (D,), jnp.float32), 0.1, 1.9)
    w_qkv = draw_w_qkv(jax.random.fold_in(streams_of[9], 71), 0)
    w_out = gaussian(streams_of[6], (D, D), D ** -0.5, 0.25)
    out_gain = jnp.clip(1.0 + 0.18 * jax.random.normal(streams_of[7], (D,), jnp.float32), 0.1, 1.9)
    w_dec = gaussian(streams_of[8], (D, CPP), D ** -0.5, 0.25)
    return dict(store=store, sample_index=sample_index, region_ids=region_ids, w_embed=w_embed, attn_gain=attn_gain, w_qkv=w_qkv, w_out=w_out, out_gain=out_gain, w_dec=w_dec)


def layer_norm(values, gain_row):
    center = lax.optimization_barrier(jnp.mean(values, axis=-1, keepdims=True))
    spread = lax.optimization_barrier(jnp.mean(jnp.square(values - center), axis=-1, keepdims=True))
    return (values - center) * lax.rsqrt(spread + 1e-05) * gain_row

def window_attention(windows, regions):
    queries = windows[:, :, 0].astype(jnp.float32)
    keys_all = windows[:, :, 1].astype(jnp.float32)
    values_all = windows[:, :, 2].astype(jnp.float32)
    scores = jnp.einsum('wqhd,wkhd->whqk', queries, keys_all) / math.sqrt(HDIM)
    visible = (regions[:, :, None] == regions[:, None, :])[:, None]
    scores = jnp.where(visible, scores, -1e+30)
    highest = lax.optimization_barrier(jnp.max(scores, axis=-1, keepdims=True))
    expo_terms = jnp.where(visible, jnp.exp(scores - highest), 0.0)
    weights = (expo_terms / lax.optimization_barrier(jnp.sum(expo_terms, axis=-1, keepdims=True))).astype(jnp.bfloat16)
    mixed_heads = jnp.einsum('whqk,wkhd->wqhd', weights.astype(jnp.float32), values_all)
    return mixed_heads.astype(jnp.bfloat16).reshape(windows.shape[0], WIN * WIN, D)

def reference(store, sample_index, region_ids, w_embed, attn_gain, w_qkv, w_out, out_gain, w_dec):
    half_win = WIN // 2
    rolled_regions = jnp.roll(region_ids, (-half_win, -half_win), axis=(0, 1))
    region_windows = rolled_regions.reshape(HT // WIN, WIN, WT // WIN, WIN).transpose(0, 2, 1, 3).reshape(-1, WIN * WIN)

    def one_sample(slot_number):
        state_grid = lax.dynamic_index_in_dim(store, slot_number, 0, keepdims=False)
        patches = state_grid.reshape(HT * WT, CPP)
        embedded = jnp.dot(patches, w_embed, preferred_element_type=jnp.float32).astype(jnp.bfloat16)
        normed = layer_norm(embedded.astype(jnp.float32), attn_gain).astype(jnp.bfloat16)
        projected = jnp.dot(normed, w_qkv, preferred_element_type=jnp.float32).astype(jnp.bfloat16)
        rolled = jnp.roll(projected.reshape(HT, WT, 3 * D), (-half_win, -half_win), axis=(0, 1))
        windows = rolled.reshape(HT // WIN, WIN, WT // WIN, WIN, 3, HEADS, HDIM)
        windows = windows.transpose(0, 2, 1, 3, 4, 5, 6).reshape(-1, WIN * WIN, 3, HEADS, HDIM)
        mixed_heads = window_attention(windows, region_windows)
        placed = mixed_heads.reshape(HT // WIN, WT // WIN, WIN, WIN, D).transpose(0, 2, 1, 3, 4).reshape(HT, WT, D)
        placed = jnp.roll(placed, (half_win, half_win), axis=(0, 1)).reshape(HT * WT, D)
        updated = embedded.astype(jnp.float32) + jnp.dot(placed, w_out, preferred_element_type=jnp.float32)
        final_norm = layer_norm(updated, out_gain).astype(jnp.bfloat16)
        predicted = (patches.astype(jnp.float32) + jnp.dot(final_norm, w_dec, preferred_element_type=jnp.float32)).astype(jnp.bfloat16)
        return predicted.reshape(HT, WT, CPP)
    predictions = lax.map(one_sample, sample_index)
    return store.at[sample_index].set(predictions)
```

```python
import math

import jax
import jax.numpy as jnp
from jax import lax
from jax.experimental import pallas as pl
from jax.experimental.pallas import tpu as pltpu
from jax.sharding import PartitionSpec as P

D = 512
HEADS = 8
HDIM = 64
WIN = 8
HALF = WIN // 2
VMEM_LIMIT = 40 * 1024 * 1024
LAST_LIMIT = 40 * 1024 * 1024
FIRST_LIMIT = 56 * 1024 * 1024


def with_halo(array, sides, width):
    for axis, dim in sides:
        devices, length = (lax.axis_size(axis), array.shape[dim])
        up = [(i, (i + 1) % devices) for i in range(devices)]
        down = [(j, i) for i, j in up]
        last = lax.slice_in_dim(array, length - width, length, axis=dim)
        leading = lax.slice_in_dim(array, 0, width, axis=dim)
        before = lax.ppermute(last, axis, up)
        after = lax.ppermute(leading, axis, down)
        array = jnp.concatenate([before, array, after], axis=dim)
    return array


def layer_norm(values, gain_row):
    center = jnp.mean(values, axis=-1, keepdims=True)
    spread = jnp.mean(jnp.square(values - center), axis=-1, keepdims=True)
    return (values - center) * lax.rsqrt(spread + 1e-05) * gain_row


def window_mix(windows, regions):
    scores = jnp.einsum(
        "bwqhd,bwkhd->bwhqk",
        windows[:, :, :, 0],
        windows[:, :, :, 1],
        preferred_element_type=jnp.float32,
    ) / math.sqrt(HDIM)
    visible = (regions[:, :, None] == regions[:, None, :])[None, :, None]
    scores = jnp.where(visible, scores, -1e30)
    highest = jnp.max(scores, axis=-1, keepdims=True)
    expo_terms = jnp.where(visible, jnp.exp(scores - highest), 0.0)
    weights = (expo_terms / jnp.sum(expo_terms, axis=-1, keepdims=True)).astype(jnp.bfloat16)
    return jnp.einsum(
        "bwhqk,bwkhd->bwqhd", weights, windows[:, :, :, 2], preferred_element_type=jnp.float32
    ).astype(jnp.bfloat16)


def local_tiles(store, sample_index, region_ids, w_embed, attn_gain, w_qkv, w_out, out_gain, w_dec):
    lon_count = lax.axis_size("lon")
    slots_here, rows_here, width_all, patch_len = store.shape
    patch_cols = width_all // lon_count
    patch_rows = rows_here * lon_count
    half_win = WIN // 2
    ext_rows = patch_rows + WIN
    ext_cols = patch_cols + WIN
    own_slots = lax.axis_index("buf") * slots_here + jnp.arange(slots_here, dtype=jnp.int32)
    matches = own_slots[:, None] == sample_index[None, :]
    occupied = jnp.any(matches, axis=1)
    local_rows = store.reshape(slots_here, 1, rows_here, lon_count, patch_cols, patch_len)
    tile_data = lax.all_to_all(local_rows, "lon", split_axis=3, concat_axis=1, tiled=True)
    patches = tile_data.reshape(-1, patch_len)
    embedded = jnp.dot(patches, w_embed, preferred_element_type=jnp.float32).astype(jnp.bfloat16)
    normed = layer_norm(embedded.astype(jnp.float32), attn_gain).astype(jnp.bfloat16)
    normed = normed.reshape(slots_here, patch_rows, patch_cols, D)
    widened = with_halo(normed, (("lat", 1), ("lon", 2)), half_win)
    projected = jnp.dot(widened.reshape(-1, D), w_qkv, preferred_element_type=jnp.float32).astype(
        jnp.bfloat16
    )
    windows = projected.reshape(
        slots_here, ext_rows // WIN, WIN, ext_cols // WIN, WIN, 3, HEADS, HDIM
    )
    windows = windows.transpose(0, 1, 3, 2, 4, 5, 6, 7).reshape(
        slots_here, -1, WIN * WIN, 3, HEADS, HDIM
    )
    total_rows, total_cols = region_ids.shape
    row_pick = (
        lax.axis_index("lat") * patch_rows - half_win + jnp.arange(ext_rows, dtype=jnp.int32)
    ) % total_rows
    col_pick = (
        lax.axis_index("lon") * patch_cols - half_win + jnp.arange(ext_cols, dtype=jnp.int32)
    ) % total_cols
    local_regions = jnp.take(jnp.take(region_ids, row_pick, axis=0), col_pick, axis=1)
    region_windows = (
        local_regions.reshape(ext_rows // WIN, WIN, ext_cols // WIN, WIN)
        .transpose(0, 2, 1, 3)
        .reshape(-1, WIN * WIN)
    )
    mixed_heads = window_mix(windows, region_windows)
    placed = mixed_heads.reshape(slots_here, ext_rows // WIN, ext_cols // WIN, WIN, WIN, D)
    placed = placed.transpose(0, 1, 3, 2, 4, 5).reshape(slots_here, ext_rows, ext_cols, D)
    placed = placed[:, half_win : half_win + patch_rows, half_win : half_win + patch_cols].reshape(
        -1, D
    )
    updated = embedded.astype(jnp.float32) + jnp.dot(
        placed, w_out, preferred_element_type=jnp.float32
    )
    final_norm = layer_norm(updated, out_gain).astype(jnp.bfloat16)
    predicted = (
        patches.astype(jnp.float32) + jnp.dot(final_norm, w_dec, preferred_element_type=jnp.float32)
    ).astype(jnp.bfloat16)
    outgoing = predicted.reshape(slots_here, lon_count, rows_here, 1, patch_cols, patch_len)
    returned = lax.all_to_all(outgoing, "lon", split_axis=1, concat_axis=3, tiled=True)
    strip_data = returned.reshape(slots_here, rows_here, width_all, patch_len)
    return jnp.where(occupied[:, None, None, None], strip_data, store)


def to_windows(values):
    rows, cols = HALF, values.shape[0] // HALF
    parts = [pltpu.roll(values[cols * i : cols * (i + 1)], cols - HALF, 0) for i in range(rows)]
    return jnp.concatenate(
        [parts[i][WIN * c : WIN * (c + 1)] for c in range(cols // WIN) for i in range(rows)], axis=0
    )


def from_windows(values):
    rows, cols = HALF, values.shape[0] // HALF
    parts = []
    for i in range(rows):
        line = jnp.concatenate(
            [
                values[WIN * (rows * c + i) : WIN * (rows * c + i + 1)]
                for c in range(cols // WIN)
            ],
            axis=0,
        )
        parts.append(pltpu.roll(line, HALF, 0))
    return jnp.concatenate(parts, axis=0)


def embed_slot(patches, w_embed, gain):
    embedded = jnp.dot(patches, w_embed, preferred_element_type=jnp.float32).astype(jnp.bfloat16)
    embedded = to_windows(embedded.astype(jnp.float32))
    normed = layer_norm(embedded, gain).astype(jnp.bfloat16)
    return embedded.astype(jnp.bfloat16), normed


NT = (((1,), (1,)), ((), ()))
TN = (((0,), (0,)), ((), ()))
GROUP = 4
WIDE = GROUP * HDIM
PER = WIN * HALF


def attend_slot(query, kv_own, kv_other, q_regions, k_regions):
    shape = (GROUP * PER, WIDE)
    pick = (
        lax.broadcasted_iota(jnp.int32, shape, 0) // PER
        == lax.broadcasted_iota(jnp.int32, shape, 1) // HDIM
    )
    head_mask = jnp.where(pick, 1.0, 0.0).astype(jnp.bfloat16)
    windows = query.shape[0] // PER
    kvs, scores, weights, mixed = [], [], [], []
    for c in range(windows):
        at = slice(PER * c, PER * (c + 1))
        kvs.append(jnp.concatenate([kv_own[at], kv_other[at]], axis=0))
        for g in range(HEADS // GROUP):
            cols = slice(WIDE * g, WIDE * (g + 1))
            queries = jnp.concatenate([query[at, cols]] * GROUP, axis=0) * head_mask
            scores.append(
                lax.dot_general(kvs[c][:, cols], queries, NT, preferred_element_type=jnp.float32)
            )
    for c in range(windows):
        seen = k_regions[:, c : c + 1] == q_regions[c : c + 1, :]
        for g in range(HEADS // GROUP):
            part = jnp.where(seen, scores[2 * c + g], -1e30)
            expo = jnp.exp(part - jnp.max(part, axis=0, keepdims=True))
            total = jnp.sum(expo, axis=0, keepdims=True)
            weights.append((expo * (1.0 / total)).astype(jnp.bfloat16))
    for c in range(windows):
        groups = []
        for g in range(HEADS // GROUP):
            heads = lax.dot_general(
                weights[2 * c + g],
                kvs[c][:, D + WIDE * g : D + WIDE * (g + 1)],
                TN,
                preferred_element_type=jnp.float32,
            )
            heads = jnp.where(pick, heads, 0.0)
            total = heads[:PER]
            for h in range(1, GROUP):
                total = total + heads[PER * h : PER * (h + 1)]
            groups.append(total)
        mixed.append(jnp.concatenate(groups, axis=1).astype(jnp.bfloat16))
    return jnp.concatenate(mixed, axis=0)


def region_tables(own, far):
    rows, cols = own.shape
    windows = cols // WIN
    lines = [own[i : i + 1] for i in range(rows)] + [far[i : i + 1] for i in range(rows)]
    wide = jnp.concatenate([jnp.broadcast_to(line, (WIN, cols)) for line in lines], axis=0)
    row = lax.broadcasted_iota(jnp.int32, wide.shape, 0)
    col = lax.broadcasted_iota(jnp.int32, wide.shape, 1)
    kept = jnp.where((col + WIN - HALF) % WIN == row % WIN, wide, 0.0).astype(jnp.bfloat16)
    place = (lax.broadcasted_iota(jnp.int32, (windows, cols), 1) + cols - HALF) % cols // WIN
    here = place == lax.broadcasted_iota(jnp.int32, (windows, cols), 0)
    here = jnp.where(here, 1.0, 0.0).astype(jnp.bfloat16)
    k_regions = lax.dot_general(kept, here, NT, preferred_element_type=jnp.float32)
    q_rows = jnp.concatenate([kept[:PER]] * GROUP, axis=0)
    q_regions = lax.dot_general(here, q_rows, NT, preferred_element_type=jnp.float32)
    return q_regions, k_regions


def finish_part(embedded, mixed, w_out, gain):
    updated = embedded.astype(jnp.float32) + jnp.dot(
        mixed, w_out, preferred_element_type=jnp.float32
    )
    return layer_norm(updated, gain)


def decode_slot(patches, final, w_dec_t):
    return (
        patches.astype(jnp.float32)
        + lax.dot_general(
            final, w_dec_t, (((1,), (1,)), ((), ())), preferred_element_type=jnp.float32
        )
    ).astype(jnp.bfloat16)


MESH = pl.DeviceIdType.MESH
UNIT_A, UNIT_C, UNIT_D, UNIT_B = range(4)


def slot_order(sample_ref, slots):
    first = lax.axis_index("buf") * slots
    taken = []
    for s in range(slots):
        hit = sample_ref[0] == first + s
        for b in range(1, sample_ref.shape[0]):
            hit = jnp.logical_or(hit, sample_ref[b] == first + s)
        taken.append(hit.astype(jnp.int32))
    count = sum(taken)
    places, before = [], jnp.int32(0)
    for s in range(slots):
        places.append(jnp.where(taken[s] == 1, before, count + s - before))
        before = before + taken[s]
    order = [
        sum(jnp.where(places[s] == j, jnp.int32(s), 0) for s in range(slots)) for j in range(slots)
    ]
    return [order[j] for j in (0, 2, 3, 1)], count


def first_kernel(
    sample_ref, gain_ref, store_ref, w_embed_ref, w_embed, grabbed, embedded, own, sems
):
    slots, rows_here, cols, patch_len = store_ref.shape
    order, _ = slot_order(sample_ref, slots)
    weight = pltpu.make_async_copy(w_embed_ref, w_embed, sems.at[0])
    fetch_a = pltpu.make_async_copy(store_ref.at[order[UNIT_A]], grabbed.at[0], sems.at[1])
    fetch_d = pltpu.make_async_copy(store_ref.at[order[UNIT_D]], grabbed.at[1], sems.at[2])
    weight.start()
    fetch_a.start()
    fetch_d.start()
    weight.wait()
    fetch_a.wait()
    flat = grabbed[0].reshape(rows_here * cols, patch_len)
    embedded[...], own[...] = embed_slot(flat, w_embed[...], gain_ref[...])
    fetch_d.wait()


def exchange_kernel(
    sample_ref,
    region_ref,
    a_gain_ref,
    o_gain_ref,
    w_embed,
    grabbed,
    embedded_a,
    own_a,
    store_ref,
    w_qkv_ref,
    w_out_ref,
    w_dec_ref,
    result,
    w_qkv,
    w_out,
    w_dec,
    last_qkv,
    last_far,
    last_embedded,
    last_final,
    q_table,
    k_table,
    patches,
    embedded,
    own,
    outgoing,
    relay,
    far,
    own_qkv,
    finals,
    slot_sems,
    weight_sems,
    relay_send_sems,
    relay_recv_sems,
    send_sems,
    recv_sems,
):
    slots, rows_here, cols, patch_len = store_ref.shape
    lon_count = lax.axis_size("lon")
    strips = lax.axis_size("lat") * lon_count
    mine = lax.axis_index("lat") * lon_count + lax.axis_index("lon")
    other = lax.rem(mine + 2 * lax.rem(mine, 2) - 1 + strips, strips)
    partner = {"lat": lax.div(other, lon_count), "lon": lax.rem(other, lon_count)}
    peer = {"buf": 1 - lax.axis_index("buf")}
    tokens = rows_here * cols
    half = tokens // 2
    halves = [pl.ds(half * h, half) for h in range(2)]
    windows = tokens // PER

    barrier = pltpu.get_barrier_semaphore()
    for device in (partner, peer):
        pl.semaphore_signal(barrier, inc=1, device_id=device, device_id_type=MESH)

    fetches = [
        pltpu.make_async_copy(store_ref.at[s], patches.at[s], slot_sems.at[s])
        for s in range(slots)
    ]
    for copy in fetches:
        copy.start()
    weights = [
        pltpu.make_async_copy(src, dst, weight_sems.at[i])
        for i, (src, dst) in enumerate(
            ((w_qkv_ref, w_qkv), (w_out_ref, w_out), (w_dec_ref, w_dec))
        )
    ]
    order, count = slot_order(sample_ref, slots)

    def send(k, h, src, device):
        return pltpu.make_async_remote_copy(
            src_ref=src,
            dst_ref=far.at[k, halves[h]],
            send_sem=send_sems.at[k, h],
            recv_sem=recv_sems.at[k, h],
            device_id=device,
            device_id_type=MESH,
        )

    def send_half(k, h):
        src = own_a if k == UNIT_A else outgoing if k == UNIT_C else own.at[UNIT_B]
        return send(k, h, src.at[halves[h]], partner)

    def arrival(k, h):
        return send(k, h, far.at[k, halves[h]], partner)

    def forward(h):
        return send(UNIT_D, h, far.at[UNIT_C, halves[h]], peer)

    def relay_half(h):
        return pltpu.make_async_remote_copy(
            src_ref=own.at[UNIT_D, halves[h]],
            dst_ref=relay.at[halves[h]],
            send_sem=relay_send_sems.at[h],
            recv_sem=relay_recv_sems.at[h],
            device_id=peer,
            device_id_type=MESH,
        )

    def embed(k, values):
        flat = values.reshape(tokens, patch_len)
        embedded[k], own[k] = embed_slot(flat, w_embed[...], a_gain_ref[...])

    pl.semaphore_wait(barrier, 2)
    for h in range(2):
        send_half(UNIT_A, h).start()
    embed(UNIT_D, grabbed[1])
    for h in range(2):
        relay_half(h).start()
    embedded[UNIT_A] = embedded_a[...]
    own[UNIT_A] = own_a[...]
    q_regions, k_regions = region_tables(
        region_ref[pl.ds(mine * HALF, HALF), :].astype(jnp.float32),
        region_ref[pl.ds(other * HALF, HALF), :].astype(jnp.float32),
    )
    q_table[...] = q_regions
    k_table[...] = k_regions
    for copy in fetches:
        copy.wait()
    for copy in weights:
        copy.start()
    embed(UNIT_C, patches[order[UNIT_C]])
    embed(UNIT_B, patches[order[UNIT_B]])
    result[UNIT_B] = patches[order[UNIT_B]]

    for h in range(2):
        relay_half(h).wait_recv()
        at = slice(half * h, half * (h + 1))
        outgoing[at] = jnp.where(count >= 3, own[UNIT_C, at], relay[at])
        send_half(UNIT_C, h).start()
    for h in range(2):
        send_half(UNIT_B, h).start()

    weights[0].wait()

    @pl.loop(0, slots)
    def _(k):
        query = jnp.dot(own[k], w_qkv[:, :D], preferred_element_type=jnp.float32)
        own_qkv[k, :, :D] = (query * (1.0 / math.sqrt(HDIM))).astype(jnp.bfloat16)
        own_qkv[k, :, D:] = jnp.dot(
            own[k], w_qkv[:, D:], preferred_element_type=jnp.float32
        ).astype(jnp.bfloat16)

    weights[1].wait()
    weights[2].wait()

    def mix_half(k, h):
        at = slice(half * h, half * (h + 1))
        here = slice(windows // 2 * h, windows // 2 * (h + 1))
        kv_other = jnp.dot(far[k, at], w_qkv[:, D:], preferred_element_type=jnp.float32)
        mixed = attend_slot(
            own_qkv[k, at, :D],
            own_qkv[k, at, D:],
            kv_other.astype(jnp.bfloat16),
            q_table[here, :],
            k_table[:, here],
        )
        return finish_part(embedded[k, at], mixed, w_out[...], o_gain_ref[...])

    @pl.loop(0, UNIT_B)
    def _(k):
        for h in range(2):
            arrival(k, h).wait_recv()

            @pl.when(k == UNIT_C)
            def _():
                forward(h).start()

            finals[half * h : half * (h + 1)] = mix_half(k, h)
        final = from_windows(finals[...]).astype(jnp.bfloat16)
        needed = jnp.where(k == UNIT_A, 1, jnp.where(k == UNIT_C, 3, 4))
        final = jnp.where(count >= needed, final, jnp.zeros_like(final))
        place = jnp.where(
            k == UNIT_A, order[UNIT_A], jnp.where(k == UNIT_C, order[UNIT_C], order[UNIT_D])
        )
        flat = patches[place].reshape(tokens, patch_len)
        result[k] = decode_slot(flat, final, w_dec[...]).reshape(rows_here, cols, patch_len)

    arrival(UNIT_B, 0).wait_recv()
    last_final[...] = mix_half(UNIT_B, 0)
    last_qkv[...] = own_qkv[UNIT_B, half:]
    last_embedded[...] = embedded[UNIT_B, half:]
    for h in range(2):
        relay_half(h).wait_send()
        send_half(UNIT_A, h).wait_send()
        send_half(UNIT_C, h).wait_send()
        send_half(UNIT_B, h).wait_send()
        forward(h).wait_send()
    arrival(UNIT_B, 1).wait_recv()
    last_far[...] = far[UNIT_B, half:]


def last_kernel(
    sample_ref,
    o_gain_ref,
    result,
    w_qkv,
    w_out,
    w_dec,
    last_qkv,
    last_far,
    last_embedded,
    last_final,
    q_table,
    k_table,
    new_ref,
    decoded,
    finals,
    sems,
    row_sems,
):
    slots, rows_here, cols, patch_len = result.shape
    order, _ = slot_order(sample_ref, slots)
    copies = [
        pltpu.make_async_copy(result.at[k], new_ref.at[order[k]], sems.at[k])
        for k in (UNIT_A, UNIT_C, UNIT_D)
    ]
    for copy in copies:
        copy.start()
    tokens = rows_here * cols
    half = tokens // 2
    windows = tokens // PER
    kv_other = jnp.dot(last_far[...], w_qkv[:, D:], preferred_element_type=jnp.float32)
    mixed = attend_slot(
        last_qkv[:, :D],
        last_qkv[:, D:],
        kv_other.astype(jnp.bfloat16),
        q_table[windows // 2 :, :],
        k_table[:, windows // 2 :],
    )
    finals[:half] = last_final[...]
    finals[half:] = finish_part(last_embedded[...], mixed, w_out[...], o_gain_ref[...])
    final = from_windows(finals[...]).astype(jnp.bfloat16)
    rows = rows_here // 2
    for h in range(2):
        here = slice(rows * h, rows * (h + 1))
        decoded[here] = decode_slot(
            result[UNIT_B, here].reshape(half, patch_len),
            final[half * h : half * (h + 1)],
            w_dec[...],
        ).reshape(rows, cols, patch_len)
        copies.append(
            pltpu.make_async_copy(
                decoded.at[here], new_ref.at[order[UNIT_B], here], row_sems.at[h]
            )
        )
        copies[-1].start()
    for copy in copies:
        copy.wait()


def local_strips(
    store, sample_index, region_ids, w_embed, attn_gain, w_qkv, w_out, out_gain, w_dec
):
    slots, rows_here, cols, patch_len = store.shape
    tokens = rows_here * cols
    half = tokens // 2
    windows = tokens // PER
    held = lambda *shape: pltpu.VMEM(shape, jnp.bfloat16)
    wide = lambda *shape: pltpu.VMEM(shape, jnp.float32)
    vmem = pl.BlockSpec(memory_space=pltpu.VMEM)
    smem = pl.BlockSpec(memory_space=pltpu.SMEM)
    hbm = pl.BlockSpec(memory_space=pltpu.HBM)
    in_hbm = lambda array: pltpu.with_memory_space_constraint(array, pltpu.HBM)
    store, w_embed, w_qkv, w_out = (in_hbm(array) for array in (store, w_embed, w_qkv, w_out))
    w_dec_t = in_hbm(w_dec.T)
    w_embed_held, grabbed, embedded_a, own_a = pl.pallas_call(
        first_kernel,
        in_specs=[smem, vmem, hbm, hbm],
        out_specs=[vmem] * 4,
        out_shape=[
            held(*w_embed.shape),
            held(2, *store.shape[1:]),
            held(tokens, D),
            held(tokens, D),
        ],
        scratch_shapes=[pltpu.SemaphoreType.DMA((3,))],
        compiler_params=pltpu.CompilerParams(vmem_limit_bytes=FIRST_LIMIT),
    )(sample_index, attn_gain[None], store, w_embed)
    carried = pl.pallas_call(
        exchange_kernel,
        in_specs=[smem] + [vmem] * 7 + [hbm] * 4,
        out_specs=[vmem] * 10,
        out_shape=[
            held(*store.shape),
            held(*w_qkv.shape),
            held(*w_out.shape),
            held(*w_dec_t.shape),
            held(half, 3 * D),
            held(half, D),
            held(half, D),
            wide(half, D),
            wide(windows, GROUP * PER),
            wide(2 * PER, windows),
        ],
        scratch_shapes=[
            held(*store.shape),
            held(slots, tokens, D),
            held(slots, tokens, D),
            held(tokens, D),
            held(tokens, D),
            held(slots, tokens, D),
            held(slots, tokens, 3 * D),
            wide(tokens, D),
            pltpu.SemaphoreType.DMA((slots,)),
            pltpu.SemaphoreType.DMA((3,)),
            pltpu.SemaphoreType.DMA((2,)),
            pltpu.SemaphoreType.DMA((2,)),
            pltpu.SemaphoreType.DMA((slots, 2)),
            pltpu.SemaphoreType.DMA((slots, 2)),
        ],
        compiler_params=pltpu.CompilerParams(
            vmem_limit_bytes=VMEM_LIMIT, collective_id=0, has_side_effects=True
        ),
    )(
        sample_index,
        region_ids,
        attn_gain[None],
        out_gain[None],
        w_embed_held,
        grabbed,
        embedded_a,
        own_a,
        store,
        w_qkv,
        w_out,
        w_dec_t,
    )
    return pl.pallas_call(
        last_kernel,
        in_specs=[smem] + [vmem] * 11,
        out_specs=hbm,
        out_shape=jax.ShapeDtypeStruct(store.shape, store.dtype),
        scratch_shapes=[
            held(*store.shape[1:]),
            wide(tokens, D),
            pltpu.SemaphoreType.DMA((slots,)),
            pltpu.SemaphoreType.DMA((2,)),
        ],
        compiler_params=pltpu.CompilerParams(vmem_limit_bytes=LAST_LIMIT),
    )(sample_index, out_gain[None], *carried)


def local(store, sample_index, *rest):
    slots, rows_here = store.shape[:2]
    strips = (
        rows_here == HALF
        and slots == 4
        and lax.axis_size("buf") == 2
        and sample_index.shape[0] == 6
    )
    return (local_strips if strips else local_tiles)(store, sample_index, *rest)


def solution(mesh):
    return jax.shard_map(
        local,
        mesh=mesh,
        in_specs=(P("buf", ("lat", "lon"), None, None), P(), P(), P(), P(), P(), P(), P(), P()),
        out_specs=P("buf", ("lat", "lon"), None, None),
        check_vma=False,
    )
```

```python
import math

import jax
import jax.numpy as jnp
from jax import lax
from jax.experimental import pallas as pl
from jax.experimental.pallas import tpu as pltpu
from jax.sharding import PartitionSpec as P

D = 512
HEADS = 8
HDIM = 64
WIN = 8
HALF = WIN // 2
VMEM_LIMIT = 40 * 1024 * 1024
LAST_LIMIT = 40 * 1024 * 1024
FIRST_LIMIT = 56 * 1024 * 1024


def with_halo(array, sides, width):
    for axis, dim in sides:
        devices, length = (lax.axis_size(axis), array.shape[dim])
        up = [(i, (i + 1) % devices) for i in range(devices)]
        down = [(j, i) for i, j in up]
        last = lax.slice_in_dim(array, length - width, length, axis=dim)
        leading = lax.slice_in_dim(array, 0, width, axis=dim)
        before = lax.ppermute(last, axis, up)
        after = lax.ppermute(leading, axis, down)
        array = jnp.concatenate([before, array, after], axis=dim)
    return array


def layer_norm(values, gain_row):
    center = jnp.mean(values, axis=-1, keepdims=True)
    spread = jnp.mean(jnp.square(values - center), axis=-1, keepdims=True)
    return (values - center) * lax.rsqrt(spread + 1e-05) * gain_row


def window_mix(windows, regions):
    scores = jnp.einsum(
        "bwqhd,bwkhd->bwhqk",
        windows[:, :, :, 0],
        windows[:, :, :, 1],
        preferred_element_type=jnp.float32,
    ) / math.sqrt(HDIM)
    visible = (regions[:, :, None] == regions[:, None, :])[None, :, None]
    scores = jnp.where(visible, scores, -1e30)
    highest = jnp.max(scores, axis=-1, keepdims=True)
    expo_terms = jnp.where(visible, jnp.exp(scores - highest), 0.0)
    weights = (expo_terms / jnp.sum(expo_terms, axis=-1, keepdims=True)).astype(jnp.bfloat16)
    return jnp.einsum(
        "bwhqk,bwkhd->bwqhd", weights, windows[:, :, :, 2], preferred_element_type=jnp.float32
    ).astype(jnp.bfloat16)


def local_tiles(store, sample_index, region_ids, w_embed, attn_gain, w_qkv, w_out, out_gain, w_dec):
    lon_count = lax.axis_size("lon")
    slots_here, rows_here, width_all, patch_len = store.shape
    patch_cols = width_all // lon_count
    patch_rows = rows_here * lon_count
    half_win = WIN // 2
    ext_rows = patch_rows + WIN
    ext_cols = patch_cols + WIN
    own_slots = lax.axis_index("buf") * slots_here + jnp.arange(slots_here, dtype=jnp.int32)
    matches = own_slots[:, None] == sample_index[None, :]
    occupied = jnp.any(matches, axis=1)
    local_rows = store.reshape(slots_here, 1, rows_here, lon_count, patch_cols, patch_len)
    tile_data = lax.all_to_all(local_rows, "lon", split_axis=3, concat_axis=1, tiled=True)
    patches = tile_data.reshape(-1, patch_len)
    embedded = jnp.dot(patches, w_embed, preferred_element_type=jnp.float32).astype(jnp.bfloat16)
    normed = layer_norm(embedded.astype(jnp.float32), attn_gain).astype(jnp.bfloat16)
    normed = normed.reshape(slots_here, patch_rows, patch_cols, D)
    widened = with_halo(normed, (("lat", 1), ("lon", 2)), half_win)
    projected = jnp.dot(widened.reshape(-1, D), w_qkv, preferred_element_type=jnp.float32).astype(
        jnp.bfloat16
    )
    windows = projected.reshape(
        slots_here, ext_rows // WIN, WIN, ext_cols // WIN, WIN, 3, HEADS, HDIM
    )
    windows = windows.transpose(0, 1, 3, 2, 4, 5, 6, 7).reshape(
        slots_here, -1, WIN * WIN, 3, HEADS, HDIM
    )
    total_rows, total_cols = region_ids.shape
    row_pick = (
        lax.axis_index("lat") * patch_rows - half_win + jnp.arange(ext_rows, dtype=jnp.int32)
    ) % total_rows
    col_pick = (
        lax.axis_index("lon") * patch_cols - half_win + jnp.arange(ext_cols, dtype=jnp.int32)
    ) % total_cols
    local_regions = jnp.take(jnp.take(region_ids, row_pick, axis=0), col_pick, axis=1)
    region_windows = (
        local_regions.reshape(ext_rows // WIN, WIN, ext_cols // WIN, WIN)
        .transpose(0, 2, 1, 3)
        .reshape(-1, WIN * WIN)
    )
    mixed_heads = window_mix(windows, region_windows)
    placed = mixed_heads.reshape(slots_here, ext_rows // WIN, ext_cols // WIN, WIN, WIN, D)
    placed = placed.transpose(0, 1, 3, 2, 4, 5).reshape(slots_here, ext_rows, ext_cols, D)
    placed = placed[:, half_win : half_win + patch_rows, half_win : half_win + patch_cols].reshape(
        -1, D
    )
    updated = embedded.astype(jnp.float32) + jnp.dot(
        placed, w_out, preferred_element_type=jnp.float32
    )
    final_norm = layer_norm(updated, out_gain).astype(jnp.bfloat16)
    predicted = (
        patches.astype(jnp.float32) + jnp.dot(final_norm, w_dec, preferred_element_type=jnp.float32)
    ).astype(jnp.bfloat16)
    outgoing = predicted.reshape(slots_here, lon_count, rows_here, 1, patch_cols, patch_len)
    returned = lax.all_to_all(outgoing, "lon", split_axis=1, concat_axis=3, tiled=True)
    strip_data = returned.reshape(slots_here, rows_here, width_all, patch_len)
    return jnp.where(occupied[:, None, None, None], strip_data, store)


def to_windows(values):
    rows, cols = HALF, values.shape[0] // HALF
    parts = [pltpu.roll(values[cols * i : cols * (i + 1)], cols - HALF, 0) for i in range(rows)]
    return jnp.concatenate(
        [parts[i][WIN * c : WIN * (c + 1)] for c in range(cols // WIN) for i in range(rows)], axis=0
    )


def from_windows(values):
    rows, cols = HALF, values.shape[0] // HALF
    parts = []
    for i in range(rows):
        line = jnp.concatenate(
            [
                values[WIN * (rows * c + i) : WIN * (rows * c + i + 1)]
                for c in range(cols // WIN)
            ],
            axis=0,
        )
        parts.append(pltpu.roll(line, HALF, 0))
    return jnp.concatenate(parts, axis=0)


def embed_slot(patches, w_embed, gain):
    embedded = jnp.dot(patches, w_embed, preferred_element_type=jnp.float32).astype(jnp.bfloat16)
    embedded = to_windows(embedded.astype(jnp.float32))
    normed = layer_norm(embedded, gain).astype(jnp.bfloat16)
    return embedded.astype(jnp.bfloat16), normed


NT = (((1,), (1,)), ((), ()))
TN = (((0,), (0,)), ((), ()))
GROUP = 4
WIDE = GROUP * HDIM
PER = WIN * HALF


def attend_slot(query, kv_own, kv_other, q_regions, k_regions):
    shape = (GROUP * PER, WIDE)
    pick = (
        lax.broadcasted_iota(jnp.int32, shape, 0) // PER
        == lax.broadcasted_iota(jnp.int32, shape, 1) // HDIM
    )
    head_mask = jnp.where(pick, 1.0, 0.0).astype(jnp.bfloat16)
    windows = query.shape[0] // PER
    kvs, scores, weights, mixed = [], [], [], []
    for c in range(windows):
        at = slice(PER * c, PER * (c + 1))
        kvs.append(jnp.concatenate([kv_own[at], kv_other[at]], axis=0))
        for g in range(HEADS // GROUP):
            cols = slice(WIDE * g, WIDE * (g + 1))
            queries = jnp.concatenate([query[at, cols]] * GROUP, axis=0) * head_mask
            scores.append(
                lax.dot_general(kvs[c][:, cols], queries, NT, preferred_element_type=jnp.float32)
            )
    for c in range(windows):
        seen = k_regions[:, c : c + 1] == q_regions[c : c + 1, :]
        for g in range(HEADS // GROUP):
            part = jnp.where(seen, scores[2 * c + g], -1e30)
            expo = jnp.exp(part - jnp.max(part, axis=0, keepdims=True))
            total = jnp.sum(expo, axis=0, keepdims=True)
            weights.append((expo * (1.0 / total)).astype(jnp.bfloat16))
    for c in range(windows):
        groups = []
        for g in range(HEADS // GROUP):
            heads = lax.dot_general(
                weights[2 * c + g],
                kvs[c][:, D + WIDE * g : D + WIDE * (g + 1)],
                TN,
                preferred_element_type=jnp.float32,
            )
            heads = jnp.where(pick, heads, 0.0)
            total = heads[:PER]
            for h in range(1, GROUP):
                total = total + heads[PER * h : PER * (h + 1)]
            groups.append(total)
        mixed.append(jnp.concatenate(groups, axis=1).astype(jnp.bfloat16))
    return jnp.concatenate(mixed, axis=0)


def region_tables(own, far):
    rows, cols = own.shape
    windows = cols // WIN
    lines = [own[i : i + 1] for i in range(rows)] + [far[i : i + 1] for i in range(rows)]
    wide = jnp.concatenate([jnp.broadcast_to(line, (WIN, cols)) for line in lines], axis=0)
    row = lax.broadcasted_iota(jnp.int32, wide.shape, 0)
    col = lax.broadcasted_iota(jnp.int32, wide.shape, 1)
    kept = jnp.where((col + WIN - HALF) % WIN == row % WIN, wide, 0.0).astype(jnp.bfloat16)
    place = (lax.broadcasted_iota(jnp.int32, (windows, cols), 1) + cols - HALF) % cols // WIN
    here = place == lax.broadcasted_iota(jnp.int32, (windows, cols), 0)
    here = jnp.where(here, 1.0, 0.0).astype(jnp.bfloat16)
    k_regions = lax.dot_general(kept, here, NT, preferred_element_type=jnp.float32)
    q_rows = jnp.concatenate([kept[:PER]] * GROUP, axis=0)
    q_regions = lax.dot_general(here, q_rows, NT, preferred_element_type=jnp.float32)
    return q_regions, k_regions


def finish_part(embedded, mixed, w_out, gain):
    updated = embedded.astype(jnp.float32) + jnp.dot(
        mixed, w_out, preferred_element_type=jnp.float32
    )
    return layer_norm(updated, gain)


def decode_slot(patches, final, w_dec_t):
    return (
        patches.astype(jnp.float32)
        + lax.dot_general(
            final, w_dec_t, (((1,), (1,)), ((), ())), preferred_element_type=jnp.float32
        )
    ).astype(jnp.bfloat16)


MESH = pl.DeviceIdType.MESH
UNIT_A, UNIT_C, UNIT_D, UNIT_B = range(4)


def slot_order(sample_ref, slots):
    first = lax.axis_index("buf") * slots
    taken = []
    for s in range(slots):
        hit = sample_ref[0] == first + s
        for b in range(1, sample_ref.shape[0]):
            hit = jnp.logical_or(hit, sample_ref[b] == first + s)
        taken.append(hit.astype(jnp.int32))
    count = sum(taken)
    places, before = [], jnp.int32(0)
    for s in range(slots):
        places.append(jnp.where(taken[s] == 1, before, count + s - before))
        before = before + taken[s]
    order = [
        sum(jnp.where(places[s] == j, jnp.int32(s), 0) for s in range(slots)) for j in range(slots)
    ]
    return [order[j] for j in (0, 2, 3, 1)], count


def first_kernel(
    sample_ref, gain_ref, store_ref, w_embed_ref, w_embed, grabbed, embedded, own, sample, gain, sems
):
    slots, rows_here, cols, patch_len = store_ref.shape
    weight = pltpu.make_async_copy(w_embed_ref, w_embed, sems.at[0])
    sample_in = pltpu.make_async_copy(sample_ref, sample, sems.at[3])
    gain_in = pltpu.make_async_copy(gain_ref, gain, sems.at[4])
    sample_in.start()
    weight.start()
    gain_in.start()
    sample_in.wait()
    order, _ = slot_order(sample, slots)
    fetch_a = pltpu.make_async_copy(store_ref.at[order[UNIT_A]], grabbed.at[0], sems.at[1])
    fetch_d = pltpu.make_async_copy(store_ref.at[order[UNIT_D]], grabbed.at[1], sems.at[2])
    fetch_a.start()
    gain_in.wait()
    weight.wait()
    fetch_d.start()
    fetch_a.wait()
    flat = grabbed[0].reshape(rows_here * cols, patch_len)
    embedded[...], own[...] = embed_slot(flat, w_embed[...], gain[...])
    fetch_d.wait()


def exchange_kernel(
    sample_ref,
    region_ref,
    a_gain_ref,
    o_gain_ref,
    w_embed,
    grabbed,
    embedded_a,
    own_a,
    store_ref,
    w_qkv_ref,
    w_out_ref,
    w_dec_ref,
    result,
    w_qkv,
    w_out,
    w_dec,
    last_qkv,
    last_far,
    last_embedded,
    last_final,
    q_table,
    k_table,
    patches,
    embedded,
    own,
    outgoing,
    relay,
    far,
    own_qkv,
    slot_sems,
    weight_sems,
    relay_send_sems,
    relay_recv_sems,
    send_sems,
    recv_sems,
):
    slots, rows_here, cols, patch_len = store_ref.shape
    lon_count = lax.axis_size("lon")
    strips = lax.axis_size("lat") * lon_count
    mine = lax.axis_index("lat") * lon_count + lax.axis_index("lon")
    other = lax.rem(mine + 2 * lax.rem(mine, 2) - 1 + strips, strips)
    partner = {"lat": lax.div(other, lon_count), "lon": lax.rem(other, lon_count)}
    peer = {"buf": 1 - lax.axis_index("buf")}
    near = lax.div(other, lon_count) == lax.axis_index("lat")
    tokens = rows_here * cols
    half = tokens // 2
    windows = tokens // PER

    def part(h):
        return pl.ds(half * h if isinstance(h, int) else pl.multiple_of(half * h, half), half)

    barrier = pltpu.get_barrier_semaphore()
    for device in (partner, peer):
        pl.semaphore_signal(barrier, inc=1, device_id=device, device_id_type=MESH)

    fetches = [
        pltpu.make_async_copy(store_ref.at[s], patches.at[s], slot_sems.at[s])
        for s in range(slots)
    ]
    for copy in fetches:
        copy.start()
    weights = [
        pltpu.make_async_copy(src, dst, weight_sems.at[i])
        for i, (src, dst) in enumerate(
            ((w_qkv_ref, w_qkv), (w_out_ref, w_out), (w_dec_ref, w_dec))
        )
    ]
    order, count = slot_order(sample_ref, slots)

    def send(k, h, src, device):
        return pltpu.make_async_remote_copy(
            src_ref=src,
            dst_ref=far.at[k, part(h)],
            send_sem=send_sems.at[k, h],
            recv_sem=recv_sems.at[k, h],
            device_id=device,
            device_id_type=MESH,
        )

    def send_half(k, h):
        src = own_a if k == UNIT_A else outgoing if k == UNIT_C else own.at[UNIT_B]
        return send(k, h, src.at[part(h)], partner)

    def arrival(k, h):
        return send(k, h, far.at[k, part(h)], partner)

    def forward(h):
        return send(UNIT_D, h, far.at[UNIT_C, part(h)], peer)

    def relay_half(h):
        return pltpu.make_async_remote_copy(
            src_ref=own.at[UNIT_D, part(h)],
            dst_ref=relay.at[part(h)],
            send_sem=relay_send_sems.at[h],
            recv_sem=relay_recv_sems.at[h],
            device_id=peer,
            device_id_type=MESH,
        )

    def embed(k, values):
        flat = values.reshape(tokens, patch_len)
        embedded[k], own[k] = embed_slot(flat, w_embed[...], a_gain_ref[...])

    pl.semaphore_wait(barrier, 2)
    for h in range(2):
        send_half(UNIT_A, h).start()
    embed(UNIT_D, grabbed[1])
    for h in range(2):
        relay_half(h).start()
    embedded[UNIT_A] = embedded_a[...]
    own[UNIT_A] = own_a[...]
    q_regions, k_regions = region_tables(
        region_ref[pl.ds(mine * HALF, HALF), :].astype(jnp.float32),
        region_ref[pl.ds(other * HALF, HALF), :].astype(jnp.float32),
    )
    q_table[...] = q_regions
    k_table[...] = k_regions
    for copy in fetches:
        copy.wait()
    for copy in weights:
        copy.start()
    embed(UNIT_C, patches[order[UNIT_C]])
    embed(UNIT_B, patches[order[UNIT_B]])
    result[UNIT_B] = patches[order[UNIT_B]]

    weights[0].wait()

    def project(k):
        query = jnp.dot(own[k], w_qkv[:, :D], preferred_element_type=jnp.float32)
        own_qkv[k, :, :D] = (query * (1.0 / math.sqrt(HDIM))).astype(jnp.bfloat16)
        own_qkv[k, :, D:] = jnp.dot(
            own[k], w_qkv[:, D:], preferred_element_type=jnp.float32
        ).astype(jnp.bfloat16)

    @pl.loop(0, 2)
    def _(h):
        project(2 * h)
        project(2 * h + 1)
        relay_half(h).wait_recv()
        at = part(h)
        outgoing[at] = jnp.where(count >= 3, own[UNIT_C, at], relay[at])
        send_half(UNIT_C, h).start()

    @pl.when(near)
    def _():
        for h in range(2):
            send_half(UNIT_B, h).start()

    weights[1].wait()
    weights[2].wait()

    def mix(k, at, here):
        kv_other = jnp.dot(far[k, at], w_qkv[:, D:], preferred_element_type=jnp.float32)
        mixed = attend_slot(
            own_qkv[k, at, :D],
            own_qkv[k, at, D:],
            kv_other.astype(jnp.bfloat16),
            q_table[here, :],
            k_table[:, here],
        )
        return finish_part(embedded[k, at], mixed, w_out[...], o_gain_ref[...])

    @pl.loop(0, UNIT_B)
    def _(k):
        for h in range(2):
            arrival(k, h).wait_recv()

            @pl.when(k == UNIT_C)
            def _():
                forward(h).start()

        final = from_windows(mix(k, slice(0, tokens), slice(0, windows))).astype(jnp.bfloat16)
        needed = jnp.where(k == UNIT_A, 1, jnp.where(k == UNIT_C, 3, 4))
        final = jnp.where(count >= needed, final, jnp.zeros_like(final))
        place = jnp.where(
            k == UNIT_A, order[UNIT_A], jnp.where(k == UNIT_C, order[UNIT_C], order[UNIT_D])
        )
        flat = patches[place].reshape(tokens, patch_len)
        result[k] = decode_slot(flat, final, w_dec[...]).reshape(rows_here, cols, patch_len)

        @pl.when(jnp.logical_and(k == UNIT_A, jnp.logical_not(near)))
        def _():
            for h in range(2):
                send_half(UNIT_B, h).start()

        @pl.when(k == UNIT_C)
        def _():
            arrival(UNIT_B, 0).wait_recv()
            last_final[...] = mix(UNIT_B, slice(0, half), slice(0, windows // 2))

    last_qkv[...] = own_qkv[UNIT_B, half:]
    last_embedded[...] = embedded[UNIT_B, half:]
    for h in range(2):
        relay_half(h).wait_send()
        send_half(UNIT_A, h).wait_send()
        send_half(UNIT_C, h).wait_send()
        send_half(UNIT_B, h).wait_send()
        forward(h).wait_send()
    arrival(UNIT_B, 1).wait_recv()
    last_far[...] = far[UNIT_B, half:]


def last_kernel(
    sample_ref,
    o_gain_ref,
    result,
    w_qkv,
    w_out,
    w_dec,
    last_qkv,
    last_far,
    last_embedded,
    last_final,
    q_table,
    k_table,
    new_ref,
    decoded,
    finals,
    sems,
    row_sems,
):
    slots, rows_here, cols, patch_len = result.shape
    order, _ = slot_order(sample_ref, slots)
    copies = [
        pltpu.make_async_copy(result.at[k], new_ref.at[order[k]], sems.at[k])
        for k in (UNIT_A, UNIT_C, UNIT_D)
    ]
    for copy in copies:
        copy.start()
    tokens = rows_here * cols
    half = tokens // 2
    windows = tokens // PER
    kv_other = jnp.dot(last_far[...], w_qkv[:, D:], preferred_element_type=jnp.float32)
    mixed = attend_slot(
        last_qkv[:, :D],
        last_qkv[:, D:],
        kv_other.astype(jnp.bfloat16),
        q_table[windows // 2 :, :],
        k_table[:, windows // 2 :],
    )
    finals[:half] = last_final[...]
    finals[half:] = finish_part(last_embedded[...], mixed, w_out[...], o_gain_ref[...])
    final = from_windows(finals[...]).astype(jnp.bfloat16)
    rows = rows_here // 2
    for h in range(2):
        here = slice(rows * h, rows * (h + 1))
        decoded[here] = decode_slot(
            result[UNIT_B, here].reshape(half, patch_len),
            final[half * h : half * (h + 1)],
            w_dec[...],
        ).reshape(rows, cols, patch_len)
        copies.append(
            pltpu.make_async_copy(
                decoded.at[here], new_ref.at[order[UNIT_B], here], row_sems.at[h]
            )
        )
        copies[-1].start()
    for copy in copies:
        copy.wait()


def local_strips(
    store, sample_index, region_ids, w_embed, attn_gain, w_qkv, w_out, out_gain, w_dec
):
    slots, rows_here, cols, patch_len = store.shape
    tokens = rows_here * cols
    half = tokens // 2
    windows = tokens // PER
    held = lambda *shape: pltpu.VMEM(shape, jnp.bfloat16)
    wide = lambda *shape: pltpu.VMEM(shape, jnp.float32)
    vmem = pl.BlockSpec(memory_space=pltpu.VMEM)
    smem = pl.BlockSpec(memory_space=pltpu.SMEM)
    hbm = pl.BlockSpec(memory_space=pltpu.HBM)
    in_hbm = lambda array: pltpu.with_memory_space_constraint(array, pltpu.HBM)
    store, w_embed, w_qkv, w_out = (in_hbm(array) for array in (store, w_embed, w_qkv, w_out))
    w_dec_t = in_hbm(w_dec.T)
    w_embed_held, grabbed, embedded_a, own_a = pl.pallas_call(
        first_kernel,
        in_specs=[hbm] * 4,
        out_specs=[vmem] * 4,
        out_shape=[
            held(*w_embed.shape),
            held(2, *store.shape[1:]),
            held(tokens, D),
            held(tokens, D),
        ],
        scratch_shapes=[
            pltpu.SMEM(sample_index.shape, jnp.int32),
            wide(1, D),
            pltpu.SemaphoreType.DMA((5,)),
        ],
        compiler_params=pltpu.CompilerParams(vmem_limit_bytes=FIRST_LIMIT),
    )(in_hbm(sample_index), in_hbm(attn_gain[None]), store, w_embed)
    carried = pl.pallas_call(
        exchange_kernel,
        in_specs=[smem] + [vmem] * 7 + [hbm] * 4,
        out_specs=[vmem] * 10,
        out_shape=[
            held(*store.shape),
            held(*w_qkv.shape),
            held(*w_out.shape),
            held(*w_dec_t.shape),
            held(half, 3 * D),
            held(half, D),
            held(half, D),
            wide(half, D),
            wide(windows, GROUP * PER),
            wide(2 * PER, windows),
        ],
        scratch_shapes=[
            held(*store.shape),
            held(slots, tokens, D),
            held(slots, tokens, D),
            held(tokens, D),
            held(tokens, D),
            held(slots, tokens, D),
            held(slots, tokens, 3 * D),
            pltpu.SemaphoreType.DMA((slots,)),
            pltpu.SemaphoreType.DMA((3,)),
            pltpu.SemaphoreType.DMA((2,)),
            pltpu.SemaphoreType.DMA((2,)),
            pltpu.SemaphoreType.DMA((slots, 2)),
            pltpu.SemaphoreType.DMA((slots, 2)),
        ],
        compiler_params=pltpu.CompilerParams(
            vmem_limit_bytes=VMEM_LIMIT, collective_id=0, has_side_effects=True
        ),
    )(
        sample_index,
        region_ids,
        attn_gain[None],
        out_gain[None],
        w_embed_held,
        grabbed,
        embedded_a,
        own_a,
        store,
        w_qkv,
        w_out,
        w_dec_t,
    )
    return pl.pallas_call(
        last_kernel,
        in_specs=[smem] + [vmem] * 11,
        out_specs=hbm,
        out_shape=jax.ShapeDtypeStruct(store.shape, store.dtype),
        scratch_shapes=[
            held(*store.shape[1:]),
            wide(tokens, D),
            pltpu.SemaphoreType.DMA((slots,)),
            pltpu.SemaphoreType.DMA((2,)),
        ],
        compiler_params=pltpu.CompilerParams(vmem_limit_bytes=LAST_LIMIT),
    )(sample_index, out_gain[None], *carried)


def local(store, sample_index, *rest):
    slots, rows_here = store.shape[:2]
    strips = (
        rows_here == HALF
        and slots == 4
        and lax.axis_size("buf") == 2
        and sample_index.shape[0] == 6
    )
    return (local_strips if strips else local_tiles)(store, sample_index, *rest)


def solution(mesh):
    return jax.shard_map(
        local,
        mesh=mesh,
        in_specs=(P("buf", ("lat", "lon"), None, None), P(), P(), P(), P(), P(), P(), P(), P()),
        out_specs=P("buf", ("lat", "lon"), None, None),
        check_vma=False,
    )
```

```python
import math

import jax
import jax.numpy as jnp
from jax import lax
from jax.experimental import pallas as pl
from jax.experimental.pallas import tpu as pltpu
from jax.sharding import PartitionSpec as P

D = 512
HEADS = 8
HDIM = 64
WIN = 8
HALF = WIN // 2
VMEM_LIMIT = 40 * 1024 * 1024
LAST_LIMIT = 40 * 1024 * 1024
FIRST_LIMIT = 56 * 1024 * 1024


def with_halo(array, sides, width):
    for axis, dim in sides:
        devices, length = (lax.axis_size(axis), array.shape[dim])
        up = [(i, (i + 1) % devices) for i in range(devices)]
        down = [(j, i) for i, j in up]
        last = lax.slice_in_dim(array, length - width, length, axis=dim)
        leading = lax.slice_in_dim(array, 0, width, axis=dim)
        before = lax.ppermute(last, axis, up)
        after = lax.ppermute(leading, axis, down)
        array = jnp.concatenate([before, array, after], axis=dim)
    return array


def layer_norm(values, gain_row):
    center = jnp.mean(values, axis=-1, keepdims=True)
    spread = jnp.mean(jnp.square(values - center), axis=-1, keepdims=True)
    return (values - center) * lax.rsqrt(spread + 1e-05) * gain_row


def window_mix(windows, regions):
    scores = jnp.einsum(
        "bwqhd,bwkhd->bwhqk",
        windows[:, :, :, 0],
        windows[:, :, :, 1],
        preferred_element_type=jnp.float32,
    ) / math.sqrt(HDIM)
    visible = (regions[:, :, None] == regions[:, None, :])[None, :, None]
    scores = jnp.where(visible, scores, -1e30)
    highest = jnp.max(scores, axis=-1, keepdims=True)
    expo_terms = jnp.where(visible, jnp.exp(scores - highest), 0.0)
    weights = (expo_terms / jnp.sum(expo_terms, axis=-1, keepdims=True)).astype(jnp.bfloat16)
    return jnp.einsum(
        "bwhqk,bwkhd->bwqhd", weights, windows[:, :, :, 2], preferred_element_type=jnp.float32
    ).astype(jnp.bfloat16)


def local_tiles(store, sample_index, region_ids, w_embed, attn_gain, w_qkv, w_out, out_gain, w_dec):
    lon_count = lax.axis_size("lon")
    slots_here, rows_here, width_all, patch_len = store.shape
    patch_cols = width_all // lon_count
    patch_rows = rows_here * lon_count
    half_win = WIN // 2
    ext_rows = patch_rows + WIN
    ext_cols = patch_cols + WIN
    own_slots = lax.axis_index("buf") * slots_here + jnp.arange(slots_here, dtype=jnp.int32)
    matches = own_slots[:, None] == sample_index[None, :]
    occupied = jnp.any(matches, axis=1)
    local_rows = store.reshape(slots_here, 1, rows_here, lon_count, patch_cols, patch_len)
    tile_data = lax.all_to_all(local_rows, "lon", split_axis=3, concat_axis=1, tiled=True)
    patches = tile_data.reshape(-1, patch_len)
    embedded = jnp.dot(patches, w_embed, preferred_element_type=jnp.float32).astype(jnp.bfloat16)
    normed = layer_norm(embedded.astype(jnp.float32), attn_gain).astype(jnp.bfloat16)
    normed = normed.reshape(slots_here, patch_rows, patch_cols, D)
    widened = with_halo(normed, (("lat", 1), ("lon", 2)), half_win)
    projected = jnp.dot(widened.reshape(-1, D), w_qkv, preferred_element_type=jnp.float32).astype(
        jnp.bfloat16
    )
    windows = projected.reshape(
        slots_here, ext_rows // WIN, WIN, ext_cols // WIN, WIN, 3, HEADS, HDIM
    )
    windows = windows.transpose(0, 1, 3, 2, 4, 5, 6, 7).reshape(
        slots_here, -1, WIN * WIN, 3, HEADS, HDIM
    )
    total_rows, total_cols = region_ids.shape
    row_pick = (
        lax.axis_index("lat") * patch_rows - half_win + jnp.arange(ext_rows, dtype=jnp.int32)
    ) % total_rows
    col_pick = (
        lax.axis_index("lon") * patch_cols - half_win + jnp.arange(ext_cols, dtype=jnp.int32)
    ) % total_cols
    local_regions = jnp.take(jnp.take(region_ids, row_pick, axis=0), col_pick, axis=1)
    region_windows = (
        local_regions.reshape(ext_rows // WIN, WIN, ext_cols // WIN, WIN)
        .transpose(0, 2, 1, 3)
        .reshape(-1, WIN * WIN)
    )
    mixed_heads = window_mix(windows, region_windows)
    placed = mixed_heads.reshape(slots_here, ext_rows // WIN, ext_cols // WIN, WIN, WIN, D)
    placed = placed.transpose(0, 1, 3, 2, 4, 5).reshape(slots_here, ext_rows, ext_cols, D)
    placed = placed[:, half_win : half_win + patch_rows, half_win : half_win + patch_cols].reshape(
        -1, D
    )
    updated = embedded.astype(jnp.float32) + jnp.dot(
        placed, w_out, preferred_element_type=jnp.float32
    )
    final_norm = layer_norm(updated, out_gain).astype(jnp.bfloat16)
    predicted = (
        patches.astype(jnp.float32) + jnp.dot(final_norm, w_dec, preferred_element_type=jnp.float32)
    ).astype(jnp.bfloat16)
    outgoing = predicted.reshape(slots_here, lon_count, rows_here, 1, patch_cols, patch_len)
    returned = lax.all_to_all(outgoing, "lon", split_axis=1, concat_axis=3, tiled=True)
    strip_data = returned.reshape(slots_here, rows_here, width_all, patch_len)
    return jnp.where(occupied[:, None, None, None], strip_data, store)


def to_windows(values):
    rows, cols = HALF, values.shape[0] // HALF
    parts = [pltpu.roll(values[cols * i : cols * (i + 1)], cols - HALF, 0) for i in range(rows)]
    return jnp.concatenate(
        [parts[i][WIN * c : WIN * (c + 1)] for c in range(cols // WIN) for i in range(rows)], axis=0
    )


def from_windows(values):
    rows, cols = HALF, values.shape[0] // HALF
    parts = []
    for i in range(rows):
        line = jnp.concatenate(
            [
                values[WIN * (rows * c + i) : WIN * (rows * c + i + 1)]
                for c in range(cols // WIN)
            ],
            axis=0,
        )
        parts.append(pltpu.roll(line, HALF, 0))
    return jnp.concatenate(parts, axis=0)


def embed_slot(patches, w_embed, gain):
    embedded = jnp.dot(patches, w_embed, preferred_element_type=jnp.float32).astype(jnp.bfloat16)
    embedded = to_windows(embedded.astype(jnp.float32))
    normed = layer_norm(embedded, gain).astype(jnp.bfloat16)
    return embedded.astype(jnp.bfloat16), normed


NT = (((1,), (1,)), ((), ()))
TN = (((0,), (0,)), ((), ()))
GROUP = 4
WIDE = GROUP * HDIM
PER = WIN * HALF


def attend_slot(query, kv_own, kv_other, q_regions, k_regions):
    shape = (GROUP * PER, WIDE)
    pick = (
        lax.broadcasted_iota(jnp.int32, shape, 0) // PER
        == lax.broadcasted_iota(jnp.int32, shape, 1) // HDIM
    )
    head_mask = jnp.where(pick, 1.0, 0.0).astype(jnp.bfloat16)
    windows = query.shape[0] // PER
    kvs, scores, weights, mixed = [], [], [], []
    for c in range(windows):
        at = slice(PER * c, PER * (c + 1))
        kvs.append(jnp.concatenate([kv_own[at], kv_other[at]], axis=0))
        for g in range(HEADS // GROUP):
            cols = slice(WIDE * g, WIDE * (g + 1))
            queries = jnp.concatenate([query[at, cols]] * GROUP, axis=0) * head_mask
            scores.append(
                lax.dot_general(kvs[c][:, cols], queries, NT, preferred_element_type=jnp.float32)
            )
    for c in range(windows):
        seen = k_regions[:, c : c + 1] == q_regions[c : c + 1, :]
        for g in range(HEADS // GROUP):
            part = jnp.where(seen, scores[2 * c + g], -1e30)
            expo = jnp.exp(part - jnp.max(part, axis=0, keepdims=True))
            total = jnp.sum(expo, axis=0, keepdims=True)
            weights.append((expo * (1.0 / total)).astype(jnp.bfloat16))
    for c in range(windows):
        groups = []
        for g in range(HEADS // GROUP):
            heads = lax.dot_general(
                weights[2 * c + g],
                kvs[c][:, D + WIDE * g : D + WIDE * (g + 1)],
                TN,
                preferred_element_type=jnp.float32,
            )
            heads = jnp.where(pick, heads, 0.0)
            total = heads[:PER]
            for h in range(1, GROUP):
                total = total + heads[PER * h : PER * (h + 1)]
            groups.append(total)
        mixed.append(jnp.concatenate(groups, axis=1).astype(jnp.bfloat16))
    return jnp.concatenate(mixed, axis=0)


def region_tables(own, far):
    rows, cols = own.shape
    windows = cols // WIN
    lines = [own[i : i + 1] for i in range(rows)] + [far[i : i + 1] for i in range(rows)]
    wide = jnp.concatenate([jnp.broadcast_to(line, (WIN, cols)) for line in lines], axis=0)
    row = lax.broadcasted_iota(jnp.int32, wide.shape, 0)
    col = lax.broadcasted_iota(jnp.int32, wide.shape, 1)
    kept = jnp.where((col + WIN - HALF) % WIN == row % WIN, wide, 0.0).astype(jnp.bfloat16)
    place = (lax.broadcasted_iota(jnp.int32, (windows, cols), 1) + cols - HALF) % cols // WIN
    here = place == lax.broadcasted_iota(jnp.int32, (windows, cols), 0)
    here = jnp.where(here, 1.0, 0.0).astype(jnp.bfloat16)
    k_regions = lax.dot_general(kept, here, NT, preferred_element_type=jnp.float32)
    q_rows = jnp.concatenate([kept[:PER]] * GROUP, axis=0)
    q_regions = lax.dot_general(here, q_rows, NT, preferred_element_type=jnp.float32)
    return q_regions, k_regions


def finish_part(embedded, mixed, w_out, gain):
    updated = embedded.astype(jnp.float32) + jnp.dot(
        mixed, w_out, preferred_element_type=jnp.float32
    )
    return layer_norm(updated, gain)


def decode_slot(patches, final, w_dec_t):
    return (
        patches.astype(jnp.float32)
        + lax.dot_general(
            final, w_dec_t, (((1,), (1,)), ((), ())), preferred_element_type=jnp.float32
        )
    ).astype(jnp.bfloat16)


MESH = pl.DeviceIdType.MESH
UNIT_A, UNIT_C, UNIT_D, UNIT_B = range(4)


def slot_order(sample_ref, slots):
    first = lax.axis_index("buf") * slots
    taken = []
    samples = len(sample_ref) if isinstance(sample_ref, list) else sample_ref.shape[0]
    for s in range(slots):
        hit = sample_ref[0] == first + s
        for b in range(1, samples):
            hit = jnp.logical_or(hit, sample_ref[b] == first + s)
        taken.append(hit.astype(jnp.int32))
    count = sum(taken)
    places, before = [], jnp.int32(0)
    for s in range(slots):
        places.append(jnp.where(taken[s] == 1, before, count + s - before))
        before = before + taken[s]
    order = [
        sum(jnp.where(places[s] == j, jnp.int32(s), 0) for s in range(slots)) for j in range(slots)
    ]
    return [order[j] for j in (0, 2, 3, 1)], count


def first_kernel(
    sample_ref, gain_ref, store_ref, w_embed_ref, w_embed, grabbed, embedded, own, sample, gain, sems
):
    slots, rows_here, cols, patch_len = store_ref.shape
    weight = pltpu.make_async_copy(w_embed_ref, w_embed, sems.at[0])
    sample_in = pltpu.make_async_copy(sample_ref, sample, sems.at[3])
    gain_in = pltpu.make_async_copy(gain_ref, gain, sems.at[4])
    sample_in.start()
    weight.start()
    gain_in.start()
    sample_in.wait()
    order, _ = slot_order(sample, slots)
    fetch_a = pltpu.make_async_copy(store_ref.at[order[UNIT_A]], grabbed.at[0], sems.at[1])
    fetch_d = pltpu.make_async_copy(store_ref.at[order[UNIT_D]], grabbed.at[1], sems.at[2])
    fetch_a.start()
    gain_in.wait()
    weight.wait()
    fetch_d.start()
    fetch_a.wait()
    flat = grabbed[0].reshape(rows_here * cols, patch_len)
    embedded[...], own[...] = embed_slot(flat, w_embed[...], gain[...])
    fetch_d.wait()


def exchange_kernel(
    sample_in,
    region_ref,
    a_gain_ref,
    o_gain_ref,
    w_embed,
    grabbed,
    embedded_a,
    own_a,
    store_ref,
    w_qkv_ref,
    w_out_ref,
    w_dec_ref,
    result,
    w_dec,
    finals,
    sample,
    w_qkv,
    w_out,
    q_table,
    k_table,
    q_parts,
    k_parts,
    patches,
    embedded,
    own,
    outgoing,
    relay,
    far,
    own_qkv,
    slot_sems,
    weight_sems,
    relay_send_sems,
    relay_recv_sems,
    send_sems,
    recv_sems,
):
    slots, rows_here, cols, patch_len = store_ref.shape
    lon_count = lax.axis_size("lon")
    strips = lax.axis_size("lat") * lon_count
    mine = lax.axis_index("lat") * lon_count + lax.axis_index("lon")
    other = lax.rem(mine + 2 * lax.rem(mine, 2) - 1 + strips, strips)
    partner = {"lat": lax.div(other, lon_count), "lon": lax.rem(other, lon_count)}
    peer = {"buf": 1 - lax.axis_index("buf")}
    near = lax.div(other, lon_count) == lax.axis_index("lat")
    tokens = rows_here * cols
    half = tokens // 2
    windows = tokens // PER

    def part(h):
        return pl.ds(half * h if isinstance(h, int) else pl.multiple_of(half * h, half), half)

    barrier = pltpu.get_barrier_semaphore()
    for device in (partner, peer):
        pl.semaphore_signal(barrier, inc=1, device_id=device, device_id_type=MESH)

    fetches = [
        pltpu.make_async_copy(store_ref.at[s], patches.at[s], slot_sems.at[s])
        for s in range(slots)
    ]
    fetches.append(pltpu.make_async_copy(sample_in, sample, slot_sems.at[slots]))
    for copy in reversed(fetches):
        copy.start()
    weights = [
        pltpu.make_async_copy(src, dst, weight_sems.at[i])
        for i, (src, dst) in enumerate(
            ((w_qkv_ref, w_qkv), (w_out_ref, w_out), (w_dec_ref, w_dec))
        )
    ]
    def send(k, h, at, src, device):
        return pltpu.make_async_remote_copy(
            src_ref=src.at[at],
            dst_ref=far.at[k, at],
            send_sem=send_sems.at[k, h],
            recv_sem=recv_sems.at[k, h],
            device_id=device,
            device_id_type=MESH,
        )

    def send_half(k, h):
        return send(k, h, part(h), own_a if k == UNIT_A else outgoing, partner)

    def send_piece(q):
        return send(UNIT_B, q, part(q), own.at[UNIT_B], partner)

    def arrival(k, h):
        return send(k, h, part(h), far.at[k], partner)

    def forward(h):
        return send(UNIT_D, h, part(h), far.at[UNIT_C], peer)

    def relay_half(h):
        return pltpu.make_async_remote_copy(
            src_ref=own.at[UNIT_D, part(h)],
            dst_ref=relay.at[part(h)],
            send_sem=relay_send_sems.at[h],
            recv_sem=relay_recv_sems.at[h],
            device_id=peer,
            device_id_type=MESH,
        )

    def embed(k, values):
        flat = values.reshape(tokens, patch_len)
        embedded[k], own[k] = embed_slot(flat, w_embed[...], a_gain_ref[...])

    pl.semaphore_wait(barrier, 2)
    for h in range(2):
        send_half(UNIT_A, h).start()
    embed(UNIT_D, grabbed[1])
    for h in range(2):
        relay_half(h).start()
    embedded[UNIT_A] = embedded_a[...]
    own[UNIT_A] = own_a[...]
    q_regions, k_regions = region_tables(
        region_ref[pl.ds(mine * HALF, HALF), :].astype(jnp.float32),
        region_ref[pl.ds(other * HALF, HALF), :].astype(jnp.float32),
    )
    q_table[...] = q_regions
    k_table[...] = k_regions
    each = windows // 2
    for q in range(2):
        q_parts[q] = q_regions[each * q : each * (q + 1)]
        k_parts[q] = k_regions[:, each * q : each * (q + 1)]
    for copy in fetches:
        copy.wait()
    for copy in weights:
        copy.start()
    order, count = slot_order(sample, slots)
    embed(UNIT_C, patches[order[UNIT_C]])
    embed(UNIT_B, patches[order[UNIT_B]])
    result[UNIT_B] = patches[order[UNIT_B]]

    weights[0].wait()

    def project(k):
        query = jnp.dot(own[k], w_qkv[:, :D], preferred_element_type=jnp.float32)
        own_qkv[k, :, :D] = (query * (1.0 / math.sqrt(HDIM))).astype(jnp.bfloat16)
        own_qkv[k, :, D:] = jnp.dot(
            own[k], w_qkv[:, D:], preferred_element_type=jnp.float32
        ).astype(jnp.bfloat16)

    @pl.loop(0, 2)
    def _(h):
        project(2 * h)
        project(2 * h + 1)
        relay_half(h).wait_recv()
        at = part(h)
        outgoing[at] = jnp.where(count >= 3, own[UNIT_C, at], relay[at])
        send_half(UNIT_C, h).start()

    @pl.when(near)
    def _():
        for q in range(2):
            send_piece(q).start()

    weights[1].wait()
    weights[2].wait()

    def mix(k, at, q_regions, k_regions):
        kv_other = jnp.dot(far[k, at], w_qkv[:, D:], preferred_element_type=jnp.float32)
        mixed = attend_slot(
            own_qkv[k, at, :D],
            own_qkv[k, at, D:],
            kv_other.astype(jnp.bfloat16),
            q_regions,
            k_regions,
        )
        return finish_part(embedded[k, at], mixed, w_out[...], o_gain_ref[...])

    @pl.loop(0, 5)
    def _(step):
        whole = jnp.logical_or(step < 2, step == 3)

        @pl.when(whole)
        def _():
            k = jnp.minimum(step, UNIT_D)
            for h in range(2):
                arrival(k, h).wait_recv()

                @pl.when(k == UNIT_C)
                def _():
                    forward(h).start()

            mixed = mix(k, pl.ds(0, tokens), q_table[...], k_table[...])
            final = from_windows(mixed).astype(jnp.bfloat16)
            needed = jnp.where(k == UNIT_A, 1, jnp.where(k == UNIT_C, 3, 4))
            final = jnp.where(count >= needed, final, jnp.zeros_like(final))
            place = jnp.where(
                k == UNIT_A, order[UNIT_A], jnp.where(k == UNIT_C, order[UNIT_C], order[UNIT_D])
            )
            flat = patches[place].reshape(tokens, patch_len)
            result[k] = decode_slot(flat, final, w_dec[...]).reshape(rows_here, cols, patch_len)

            @pl.when(jnp.logical_and(k == UNIT_A, jnp.logical_not(near)))
            def _():
                for q in range(2):
                    send_piece(q).start()

        @pl.when(jnp.logical_not(whole))
        def _():
            q = (step - 2) // 2
            send_piece(q).wait_recv()
            finals[part(q)] = mix(UNIT_B, part(q), q_parts[q], k_parts[q])

    for h in range(2):
        relay_half(h).wait_send()
        send_half(UNIT_A, h).wait_send()
        send_half(UNIT_C, h).wait_send()
        forward(h).wait_send()
    for q in range(2):
        send_piece(q).wait_send()


def last_kernel(sample_ref, result, w_dec, finals, new_ref, decoded, sems, row_sems):
    slots, rows_here, cols, patch_len = result.shape
    samples = sample_ref[...]
    order, _ = slot_order([samples[0, b] for b in range(samples.shape[1])], slots)
    copies = [
        pltpu.make_async_copy(result.at[k], new_ref.at[order[k]], sems.at[k])
        for k in (UNIT_A, UNIT_C, UNIT_D)
    ]
    for copy in copies:
        copy.start()
    half = rows_here * cols // 2
    final = from_windows(finals[...]).astype(jnp.bfloat16)
    rows = rows_here // 2
    for h in range(2):
        here = slice(rows * h, rows * (h + 1))
        decoded[here] = decode_slot(
            result[UNIT_B, here].reshape(half, patch_len),
            final[half * h : half * (h + 1)],
            w_dec[...],
        ).reshape(rows, cols, patch_len)
        copies.append(
            pltpu.make_async_copy(
                decoded.at[here], new_ref.at[order[UNIT_B], here], row_sems.at[h]
            )
        )
        copies[-1].start()
    for copy in copies:
        copy.wait()


def local_strips(
    store, sample_index, region_ids, w_embed, attn_gain, w_qkv, w_out, out_gain, w_dec
):
    slots, rows_here, cols, patch_len = store.shape
    tokens = rows_here * cols
    windows = tokens // PER
    held = lambda *shape: pltpu.VMEM(shape, jnp.bfloat16)
    wide = lambda *shape: pltpu.VMEM(shape, jnp.float32)
    vmem = pl.BlockSpec(memory_space=pltpu.VMEM)
    hbm = pl.BlockSpec(memory_space=pltpu.HBM)
    in_hbm = lambda array: pltpu.with_memory_space_constraint(array, pltpu.HBM)
    samples, sample_index, store = sample_index, in_hbm(sample_index), in_hbm(store)
    w_embed, w_qkv, w_out = in_hbm(w_embed), in_hbm(w_qkv), in_hbm(w_out)
    w_dec_t = in_hbm(w_dec.T)
    w_embed_held, grabbed, embedded_a, own_a = pl.pallas_call(
        first_kernel,
        in_specs=[hbm] * 4,
        out_specs=[vmem] * 4,
        out_shape=[
            held(*w_embed.shape),
            held(2, *store.shape[1:]),
            held(tokens, D),
            held(tokens, D),
        ],
        scratch_shapes=[
            pltpu.SMEM(sample_index.shape, jnp.int32),
            wide(1, D),
            pltpu.SemaphoreType.DMA((5,)),
        ],
        compiler_params=pltpu.CompilerParams(vmem_limit_bytes=FIRST_LIMIT),
    )(sample_index, in_hbm(attn_gain[None]), store, w_embed)
    carried = pl.pallas_call(
        exchange_kernel,
        in_specs=[hbm] + [vmem] * 7 + [hbm] * 4,
        out_specs=[vmem] * 3,
        out_shape=[
            held(*store.shape),
            held(*w_dec_t.shape),
            wide(tokens, D),
        ],
        scratch_shapes=[
            pltpu.SMEM(sample_index.shape, jnp.int32),
            held(*w_qkv.shape),
            held(*w_out.shape),
            wide(windows, GROUP * PER),
            wide(2 * PER, windows),
            wide(2, windows // 2, GROUP * PER),
            wide(2, 2 * PER, windows // 2),
            held(*store.shape),
            held(slots, tokens, D),
            held(slots, tokens, D),
            held(tokens, D),
            held(tokens, D),
            held(slots, tokens, D),
            held(slots, tokens, 3 * D),
            pltpu.SemaphoreType.DMA((slots + 1,)),
            pltpu.SemaphoreType.DMA((3,)),
            pltpu.SemaphoreType.DMA((2,)),
            pltpu.SemaphoreType.DMA((2,)),
            pltpu.SemaphoreType.DMA((slots, 2)),
            pltpu.SemaphoreType.DMA((slots, 2)),
        ],
        compiler_params=pltpu.CompilerParams(
            vmem_limit_bytes=VMEM_LIMIT, collective_id=0, has_side_effects=True
        ),
    )(
        sample_index,
        region_ids,
        attn_gain[None],
        out_gain[None],
        w_embed_held,
        grabbed,
        embedded_a,
        own_a,
        store,
        w_qkv,
        w_out,
        w_dec_t,
    )
    return pl.pallas_call(
        last_kernel,
        in_specs=[vmem] * 4,
        out_specs=hbm,
        out_shape=jax.ShapeDtypeStruct(store.shape, store.dtype),
        scratch_shapes=[
            held(*store.shape[1:]),
            pltpu.SemaphoreType.DMA((slots,)),
            pltpu.SemaphoreType.DMA((2,)),
        ],
        compiler_params=pltpu.CompilerParams(vmem_limit_bytes=LAST_LIMIT),
    )(samples[None], *carried)


def local(store, sample_index, *rest):
    slots, rows_here = store.shape[:2]
    strips = (
        rows_here == HALF
        and slots == 4
        and lax.axis_size("buf") == 2
        and sample_index.shape[0] == 6
    )
    return (local_strips if strips else local_tiles)(store, sample_index, *rest)


def solution(mesh):
    return jax.shard_map(
        local,
        mesh=mesh,
        in_specs=(P("buf", ("lat", "lon"), None, None), P(), P(), P(), P(), P(), P(), P(), P()),
        out_specs=P("buf", ("lat", "lon"), None, None),
        check_vma=False,
    )
```

```python
import functools
import math

import jax
import jax.numpy as jnp
from jax import lax
from jax.experimental import pallas as pl
from jax.experimental.pallas import tpu as pltpu
from jax.sharding import PartitionSpec as P

D = 512
HEADS = 8
HDIM = 64
WIN = 8
HALF = WIN // 2
VMEM_LIMIT = 40 * 1024 * 1024
LAST_LIMIT = 40 * 1024 * 1024
FIRST_LIMIT = 56 * 1024 * 1024


def with_halo(array, sides, width):
    for axis, dim in sides:
        devices, length = (lax.axis_size(axis), array.shape[dim])
        up = [(i, (i + 1) % devices) for i in range(devices)]
        down = [(j, i) for i, j in up]
        last = lax.slice_in_dim(array, length - width, length, axis=dim)
        leading = lax.slice_in_dim(array, 0, width, axis=dim)
        before = lax.ppermute(last, axis, up)
        after = lax.ppermute(leading, axis, down)
        array = jnp.concatenate([before, array, after], axis=dim)
    return array


def layer_norm(values, gain_row):
    center = jnp.mean(values, axis=-1, keepdims=True)
    spread = jnp.mean(jnp.square(values - center), axis=-1, keepdims=True)
    return (values - center) * lax.rsqrt(spread + 1e-05) * gain_row


def window_mix(windows, regions):
    scores = jnp.einsum(
        "bwqhd,bwkhd->bwhqk",
        windows[:, :, :, 0],
        windows[:, :, :, 1],
        preferred_element_type=jnp.float32,
    ) / math.sqrt(HDIM)
    visible = (regions[:, :, None] == regions[:, None, :])[None, :, None]
    scores = jnp.where(visible, scores, -1e30)
    highest = jnp.max(scores, axis=-1, keepdims=True)
    expo_terms = jnp.where(visible, jnp.exp(scores - highest), 0.0)
    weights = (expo_terms / jnp.sum(expo_terms, axis=-1, keepdims=True)).astype(jnp.bfloat16)
    return jnp.einsum(
        "bwhqk,bwkhd->bwqhd", weights, windows[:, :, :, 2], preferred_element_type=jnp.float32
    ).astype(jnp.bfloat16)


def local_tiles(store, sample_index, region_ids, w_embed, attn_gain, w_qkv, w_out, out_gain, w_dec):
    lon_count = lax.axis_size("lon")
    slots_here, rows_here, width_all, patch_len = store.shape
    patch_cols = width_all // lon_count
    patch_rows = rows_here * lon_count
    half_win = WIN // 2
    ext_rows = patch_rows + WIN
    ext_cols = patch_cols + WIN
    own_slots = lax.axis_index("buf") * slots_here + jnp.arange(slots_here, dtype=jnp.int32)
    matches = own_slots[:, None] == sample_index[None, :]
    occupied = jnp.any(matches, axis=1)
    local_rows = store.reshape(slots_here, 1, rows_here, lon_count, patch_cols, patch_len)
    tile_data = lax.all_to_all(local_rows, "lon", split_axis=3, concat_axis=1, tiled=True)
    patches = tile_data.reshape(-1, patch_len)
    embedded = jnp.dot(patches, w_embed, preferred_element_type=jnp.float32).astype(jnp.bfloat16)
    normed = layer_norm(embedded.astype(jnp.float32), attn_gain).astype(jnp.bfloat16)
    normed = normed.reshape(slots_here, patch_rows, patch_cols, D)
    widened = with_halo(normed, (("lat", 1), ("lon", 2)), half_win)
    projected = jnp.dot(widened.reshape(-1, D), w_qkv, preferred_element_type=jnp.float32).astype(
        jnp.bfloat16
    )
    windows = projected.reshape(
        slots_here, ext_rows // WIN, WIN, ext_cols // WIN, WIN, 3, HEADS, HDIM
    )
    windows = windows.transpose(0, 1, 3, 2, 4, 5, 6, 7).reshape(
        slots_here, -1, WIN * WIN, 3, HEADS, HDIM
    )
    total_rows, total_cols = region_ids.shape
    row_pick = (
        lax.axis_index("lat") * patch_rows - half_win + jnp.arange(ext_rows, dtype=jnp.int32)
    ) % total_rows
    col_pick = (
        lax.axis_index("lon") * patch_cols - half_win + jnp.arange(ext_cols, dtype=jnp.int32)
    ) % total_cols
    local_regions = jnp.take(jnp.take(region_ids, row_pick, axis=0), col_pick, axis=1)
    region_windows = (
        local_regions.reshape(ext_rows // WIN, WIN, ext_cols // WIN, WIN)
        .transpose(0, 2, 1, 3)
        .reshape(-1, WIN * WIN)
    )
    mixed_heads = window_mix(windows, region_windows)
    placed = mixed_heads.reshape(slots_here, ext_rows // WIN, ext_cols // WIN, WIN, WIN, D)
    placed = placed.transpose(0, 1, 3, 2, 4, 5).reshape(slots_here, ext_rows, ext_cols, D)
    placed = placed[:, half_win : half_win + patch_rows, half_win : half_win + patch_cols].reshape(
        -1, D
    )
    updated = embedded.astype(jnp.float32) + jnp.dot(
        placed, w_out, preferred_element_type=jnp.float32
    )
    final_norm = layer_norm(updated, out_gain).astype(jnp.bfloat16)
    predicted = (
        patches.astype(jnp.float32) + jnp.dot(final_norm, w_dec, preferred_element_type=jnp.float32)
    ).astype(jnp.bfloat16)
    outgoing = predicted.reshape(slots_here, lon_count, rows_here, 1, patch_cols, patch_len)
    returned = lax.all_to_all(outgoing, "lon", split_axis=1, concat_axis=3, tiled=True)
    strip_data = returned.reshape(slots_here, rows_here, width_all, patch_len)
    return jnp.where(occupied[:, None, None, None], strip_data, store)


def to_windows(values):
    rows, cols = HALF, values.shape[0] // HALF
    parts = [pltpu.roll(values[cols * i : cols * (i + 1)], cols - HALF, 0) for i in range(rows)]
    return jnp.concatenate(
        [parts[i][WIN * c : WIN * (c + 1)] for c in range(cols // WIN) for i in range(rows)], axis=0
    )


def from_windows(values):
    rows, cols = HALF, values.shape[0] // HALF
    parts = []
    for i in range(rows):
        line = jnp.concatenate(
            [
                values[WIN * (rows * c + i) : WIN * (rows * c + i + 1)]
                for c in range(cols // WIN)
            ],
            axis=0,
        )
        parts.append(pltpu.roll(line, HALF, 0))
    return jnp.concatenate(parts, axis=0)


def embed_slot(patches, w_embed, gain):
    embedded = jnp.dot(patches, w_embed, preferred_element_type=jnp.float32).astype(jnp.bfloat16)
    embedded = to_windows(embedded.astype(jnp.float32))
    normed = layer_norm(embedded, gain).astype(jnp.bfloat16)
    return embedded.astype(jnp.bfloat16), normed


NT = (((1,), (1,)), ((), ()))
TN = (((0,), (0,)), ((), ()))
GROUP = 4
WIDE = GROUP * HDIM
PER = WIN * HALF


def attend_slot(query, kv_own, kv_other, q_regions, k_regions):
    shape = (GROUP * PER, WIDE)
    pick = (
        lax.broadcasted_iota(jnp.int32, shape, 0) // PER
        == lax.broadcasted_iota(jnp.int32, shape, 1) // HDIM
    )
    head_mask = jnp.where(pick, 1.0, 0.0).astype(jnp.bfloat16)
    windows = query.shape[0] // PER
    kvs, scores, weights, mixed = [], [], [], []
    for c in range(windows):
        at = slice(PER * c, PER * (c + 1))
        kvs.append(jnp.concatenate([kv_own[at], kv_other[at]], axis=0))
        for g in range(HEADS // GROUP):
            cols = slice(WIDE * g, WIDE * (g + 1))
            queries = jnp.concatenate([query[at, cols]] * GROUP, axis=0) * head_mask
            scores.append(
                lax.dot_general(kvs[c][:, cols], queries, NT, preferred_element_type=jnp.float32)
            )
    for c in range(windows):
        seen = k_regions[:, c : c + 1] == q_regions[c : c + 1, :]
        for g in range(HEADS // GROUP):
            part = jnp.where(seen, scores[2 * c + g], -1e30)
            expo = jnp.exp(part - jnp.max(part, axis=0, keepdims=True))
            total = jnp.sum(expo, axis=0, keepdims=True)
            weights.append((expo * (1.0 / total)).astype(jnp.bfloat16))
    for c in range(windows):
        groups = []
        for g in range(HEADS // GROUP):
            heads = lax.dot_general(
                weights[2 * c + g],
                kvs[c][:, D + WIDE * g : D + WIDE * (g + 1)],
                TN,
                preferred_element_type=jnp.float32,
            )
            heads = jnp.where(pick, heads, 0.0)
            total = heads[:PER]
            for h in range(1, GROUP):
                total = total + heads[PER * h : PER * (h + 1)]
            groups.append(total)
        mixed.append(jnp.concatenate(groups, axis=1).astype(jnp.bfloat16))
    return jnp.concatenate(mixed, axis=0)


def region_tables(own, far):
    rows, cols = own.shape
    windows = cols // WIN
    lines = [own[i : i + 1] for i in range(rows)] + [far[i : i + 1] for i in range(rows)]
    wide = jnp.concatenate([jnp.broadcast_to(line, (WIN, cols)) for line in lines], axis=0)
    row = lax.broadcasted_iota(jnp.int32, wide.shape, 0)
    col = lax.broadcasted_iota(jnp.int32, wide.shape, 1)
    kept = jnp.where((col + WIN - HALF) % WIN == row % WIN, wide, 0.0).astype(jnp.bfloat16)
    place = (lax.broadcasted_iota(jnp.int32, (windows, cols), 1) + cols - HALF) % cols // WIN
    here = place == lax.broadcasted_iota(jnp.int32, (windows, cols), 0)
    here = jnp.where(here, 1.0, 0.0).astype(jnp.bfloat16)
    k_regions = lax.dot_general(kept, here, NT, preferred_element_type=jnp.float32)
    q_rows = jnp.concatenate([kept[:PER]] * GROUP, axis=0)
    q_regions = lax.dot_general(here, q_rows, NT, preferred_element_type=jnp.float32)
    return q_regions, k_regions


def finish_part(embedded, mixed, w_out, gain):
    updated = embedded.astype(jnp.float32) + jnp.dot(
        mixed, w_out, preferred_element_type=jnp.float32
    )
    return layer_norm(updated, gain)


def decode_slot(patches, final, w_dec_t):
    return (
        patches.astype(jnp.float32)
        + lax.dot_general(
            final, w_dec_t, (((1,), (1,)), ((), ())), preferred_element_type=jnp.float32
        )
    ).astype(jnp.bfloat16)


MESH = pl.DeviceIdType.MESH
UNIT_A, UNIT_C, UNIT_D, UNIT_B = range(4)


def slot_order(sample_ref, slots):
    first = lax.axis_index("buf") * slots
    taken = []
    samples = len(sample_ref) if isinstance(sample_ref, list) else sample_ref.shape[0]
    for s in range(slots):
        hit = sample_ref[0] == first + s
        for b in range(1, samples):
            hit = jnp.logical_or(hit, sample_ref[b] == first + s)
        taken.append(hit.astype(jnp.int32))
    count = sum(taken)
    places, before = [], jnp.int32(0)
    for s in range(slots):
        places.append(jnp.where(taken[s] == 1, before, count + s - before))
        before = before + taken[s]
    order = [
        sum(jnp.where(places[s] == j, jnp.int32(s), 0) for s in range(slots)) for j in range(slots)
    ]
    return [order[j] for j in (0, 2, 3, 1)], count


def first_kernel(
    sample_ref,
    gain_ref,
    store_ref,
    w_embed_ref,
    w_embed,
    grabbed,
    embedded,
    own,
    relayed,
    sample,
    gain,
    sems,
):
    slots, rows_here, cols, patch_len = store_ref.shape
    weight = pltpu.make_async_copy(w_embed_ref, w_embed, sems.at[0])
    sample_in = pltpu.make_async_copy(sample_ref, sample, sems.at[3])
    gain_in = pltpu.make_async_copy(gain_ref, gain, sems.at[4])
    sample_in.start()
    weight.start()
    gain_in.start()
    sample_in.wait()
    order, count = slot_order(sample, slots)
    relayed[0] = jnp.where(2 * count == sample.shape[0], 0, 1)
    fetch_a = pltpu.make_async_copy(store_ref.at[order[UNIT_A]], grabbed.at[0], sems.at[1])
    fetch_d = pltpu.make_async_copy(store_ref.at[order[UNIT_D]], grabbed.at[1], sems.at[2])
    fetch_a.start()
    gain_in.wait()
    weight.wait()
    fetch_d.start()
    fetch_a.wait()
    flat = grabbed[0].reshape(rows_here * cols, patch_len)
    embedded[...], own[...] = embed_slot(flat, w_embed[...], gain[...])
    fetch_d.wait()


def exchange_kernel(
    relayed,
    sample_in,
    region_ref,
    a_gain_ref,
    o_gain_ref,
    w_embed,
    grabbed,
    embedded_a,
    own_a,
    store_ref,
    w_qkv_ref,
    w_out_ref,
    w_dec_ref,
    result,
    w_dec,
    finals,
    sample,
    w_qkv,
    w_out,
    q_table,
    k_table,
    q_parts,
    k_parts,
    patches,
    embedded,
    own,
    outgoing,
    relay,
    far,
    own_qkv,
    slot_sems,
    weight_sems,
    relay_send_sems,
    relay_recv_sems,
    send_sems,
    recv_sems,
):
    slots, rows_here, cols, patch_len = store_ref.shape
    lon_count = lax.axis_size("lon")
    strips = lax.axis_size("lat") * lon_count
    mine = lax.axis_index("lat") * lon_count + lax.axis_index("lon")
    other = lax.rem(mine + 2 * lax.rem(mine, 2) - 1 + strips, strips)
    partner = {"lat": lax.div(other, lon_count), "lon": lax.rem(other, lon_count)}
    peer = {"buf": 1 - lax.axis_index("buf")}
    near = lax.div(other, lon_count) == lax.axis_index("lat")
    tokens = rows_here * cols
    half = tokens // 2
    windows = tokens // PER

    def part(h):
        return pl.ds(half * h if isinstance(h, int) else pl.multiple_of(half * h, half), half)

    barrier = pltpu.get_barrier_semaphore()
    devices = (partner, peer) if relayed else (partner,)
    for device in devices:
        pl.semaphore_signal(barrier, inc=1, device_id=device, device_id_type=MESH)

    fetches = [
        pltpu.make_async_copy(store_ref.at[s], patches.at[s], slot_sems.at[s])
        for s in range(slots)
    ]
    fetches.append(pltpu.make_async_copy(sample_in, sample, slot_sems.at[slots]))
    for copy in reversed(fetches):
        copy.start()
    weights = [
        pltpu.make_async_copy(src, dst, weight_sems.at[i])
        for i, (src, dst) in enumerate(
            ((w_qkv_ref, w_qkv), (w_out_ref, w_out), (w_dec_ref, w_dec))
        )
    ]
    def send(k, h, at, src, device):
        return pltpu.make_async_remote_copy(
            src_ref=src.at[at],
            dst_ref=far.at[k, at],
            send_sem=send_sems.at[k, h],
            recv_sem=recv_sems.at[k, h],
            device_id=device,
            device_id_type=MESH,
        )

    def send_half(k, h):
        third = outgoing if relayed else own.at[UNIT_C]
        return send(k, h, part(h), own_a if k == UNIT_A else third, partner)

    def send_piece(q):
        return send(UNIT_B, q, part(q), own.at[UNIT_B], partner)

    def arrival(k, h):
        return send(k, h, part(h), far.at[k], partner)

    def forward(h):
        return send(UNIT_D, h, part(h), far.at[UNIT_C], peer)

    def relay_half(h):
        return pltpu.make_async_remote_copy(
            src_ref=own.at[UNIT_D, part(h)],
            dst_ref=relay.at[part(h)],
            send_sem=relay_send_sems.at[h],
            recv_sem=relay_recv_sems.at[h],
            device_id=peer,
            device_id_type=MESH,
        )

    def embed(k, values):
        flat = values.reshape(tokens, patch_len)
        embedded[k], own[k] = embed_slot(flat, w_embed[...], a_gain_ref[...])

    pl.semaphore_wait(barrier, len(devices))
    for h in range(2):
        send_half(UNIT_A, h).start()
    if relayed:
        embed(UNIT_D, grabbed[1])
        for h in range(2):
            relay_half(h).start()
    embedded[UNIT_A] = embedded_a[...]
    own[UNIT_A] = own_a[...]
    q_regions, k_regions = region_tables(
        region_ref[pl.ds(mine * HALF, HALF), :].astype(jnp.float32),
        region_ref[pl.ds(other * HALF, HALF), :].astype(jnp.float32),
    )
    q_table[...] = q_regions
    k_table[...] = k_regions
    each = windows // 2
    for q in range(2):
        q_parts[q] = q_regions[each * q : each * (q + 1)]
        k_parts[q] = k_regions[:, each * q : each * (q + 1)]
    for copy in fetches:
        copy.wait()
    for copy in weights:
        copy.start()
    order, count = slot_order(sample, slots)
    embed(UNIT_C, patches[order[UNIT_C]])
    if not relayed:
        for h in range(2):
            send_half(UNIT_C, h).start()
    embed(UNIT_B, patches[order[UNIT_B]])
    if not relayed:

        @pl.when(near)
        def _():
            for q in range(2):
                send_piece(q).start()

        result[UNIT_D] = patches[order[UNIT_D]]
    result[UNIT_B] = patches[order[UNIT_B]]

    weights[0].wait()

    def project(k):
        query = jnp.dot(own[k], w_qkv[:, :D], preferred_element_type=jnp.float32)
        own_qkv[k, :, :D] = (query * (1.0 / math.sqrt(HDIM))).astype(jnp.bfloat16)
        own_qkv[k, :, D:] = jnp.dot(
            own[k], w_qkv[:, D:], preferred_element_type=jnp.float32
        ).astype(jnp.bfloat16)

    if relayed:

        @pl.loop(0, 2)
        def _(h):
            project(2 * h)
            project(2 * h + 1)
            relay_half(h).wait_recv()
            at = part(h)
            outgoing[at] = jnp.where(count >= 3, own[UNIT_C, at], relay[at])
            send_half(UNIT_C, h).start()

        @pl.when(near)
        def _():
            for q in range(2):
                send_piece(q).start()

    else:
        for k in (UNIT_A, UNIT_C, UNIT_B):
            project(k)
    weights[1].wait()
    weights[2].wait()

    def mix(k, at, q_regions, k_regions):
        kv_other = jnp.dot(far[k, at], w_qkv[:, D:], preferred_element_type=jnp.float32)
        mixed = attend_slot(
            own_qkv[k, at, :D],
            own_qkv[k, at, D:],
            kv_other.astype(jnp.bfloat16),
            q_regions,
            k_regions,
        )
        return finish_part(embedded[k, at], mixed, w_out[...], o_gain_ref[...])

    @pl.loop(0, 5 if relayed else 4)
    def _(step):
        whole = jnp.logical_or(step < 2, step == 3) if relayed else step < 2

        @pl.when(whole)
        def _():
            k = jnp.minimum(step, UNIT_D)
            for h in range(2):
                arrival(k, h).wait_recv()

                if relayed:

                    @pl.when(k == UNIT_C)
                    def _():
                        forward(h).start()

            mixed = mix(k, pl.ds(0, tokens), q_table[...], k_table[...])
            final = from_windows(mixed).astype(jnp.bfloat16)
            if relayed:
                needed = jnp.where(k == UNIT_A, 1, jnp.where(k == UNIT_C, 3, 4))
                final = jnp.where(count >= needed, final, jnp.zeros_like(final))
            place = jnp.where(
                k == UNIT_A, order[UNIT_A], jnp.where(k == UNIT_C, order[UNIT_C], order[UNIT_D])
            )
            flat = patches[place].reshape(tokens, patch_len)
            result[k] = decode_slot(flat, final, w_dec[...]).reshape(rows_here, cols, patch_len)

            @pl.when(jnp.logical_and(k == UNIT_A, jnp.logical_not(near)))
            def _():
                for q in range(2):
                    send_piece(q).start()

        @pl.when(jnp.logical_not(whole))
        def _():
            q = (step - 2) // 2 if relayed else step - 2
            send_piece(q).wait_recv()
            finals[part(q)] = mix(UNIT_B, part(q), q_parts[q], k_parts[q])

    for h in range(2):
        if relayed:
            relay_half(h).wait_send()
            forward(h).wait_send()
        send_half(UNIT_A, h).wait_send()
        send_half(UNIT_C, h).wait_send()
    for q in range(2):
        send_piece(q).wait_send()


def last_kernel(sample_ref, result, w_dec, finals, new_ref, decoded, sems, row_sems):
    slots, rows_here, cols, patch_len = result.shape
    samples = sample_ref[...]
    order, _ = slot_order([samples[0, b] for b in range(samples.shape[1])], slots)
    copies = [
        pltpu.make_async_copy(result.at[k], new_ref.at[order[k]], sems.at[k])
        for k in (UNIT_A, UNIT_C, UNIT_D)
    ]
    for copy in copies:
        copy.start()
    half = rows_here * cols // 2
    final = from_windows(finals[...]).astype(jnp.bfloat16)
    rows = rows_here // 2
    for h in range(2):
        here = slice(rows * h, rows * (h + 1))
        decoded[here] = decode_slot(
            result[UNIT_B, here].reshape(half, patch_len),
            final[half * h : half * (h + 1)],
            w_dec[...],
        ).reshape(rows, cols, patch_len)
        copies.append(
            pltpu.make_async_copy(
                decoded.at[here], new_ref.at[order[UNIT_B], here], row_sems.at[h]
            )
        )
        copies[-1].start()
    for copy in copies:
        copy.wait()


def local_strips(
    store, sample_index, region_ids, w_embed, attn_gain, w_qkv, w_out, out_gain, w_dec
):
    slots, rows_here, cols, patch_len = store.shape
    tokens = rows_here * cols
    windows = tokens // PER
    held = lambda *shape: pltpu.VMEM(shape, jnp.bfloat16)
    wide = lambda *shape: pltpu.VMEM(shape, jnp.float32)
    vmem = pl.BlockSpec(memory_space=pltpu.VMEM)
    hbm = pl.BlockSpec(memory_space=pltpu.HBM)
    in_hbm = lambda array: pltpu.with_memory_space_constraint(array, pltpu.HBM)
    samples, sample_index, store = sample_index, in_hbm(sample_index), in_hbm(store)
    w_embed, w_qkv, w_out = in_hbm(w_embed), in_hbm(w_qkv), in_hbm(w_out)
    w_dec_t = in_hbm(w_dec.T)
    *first, relayed = pl.pallas_call(
        first_kernel,
        in_specs=[hbm] * 4,
        out_specs=[vmem] * 4 + [pl.BlockSpec(memory_space=pltpu.SMEM)],
        out_shape=[
            held(*w_embed.shape),
            held(2, *store.shape[1:]),
            held(tokens, D),
            held(tokens, D),
            pltpu.SMEM((1,), jnp.int32),
        ],
        scratch_shapes=[
            pltpu.SMEM(sample_index.shape, jnp.int32),
            wide(1, D),
            pltpu.SemaphoreType.DMA((5,)),
        ],
        compiler_params=pltpu.CompilerParams(vmem_limit_bytes=FIRST_LIMIT),
    )(sample_index, in_hbm(attn_gain[None]), store, w_embed)
    def exchange_and_place(with_relay, *first):
        carried = pl.pallas_call(
            functools.partial(exchange_kernel, with_relay),
            in_specs=[hbm] + [vmem] * 7 + [hbm] * 4,
            out_specs=[vmem] * 3,
            out_shape=[
                held(*store.shape),
                held(*w_dec_t.shape),
                wide(tokens, D),
            ],
            scratch_shapes=[
                pltpu.SMEM(sample_index.shape, jnp.int32),
                held(*w_qkv.shape),
                held(*w_out.shape),
                wide(windows, GROUP * PER),
                wide(2 * PER, windows),
                wide(2, windows // 2, GROUP * PER),
                wide(2, 2 * PER, windows // 2),
                held(*store.shape),
                held(slots, tokens, D),
                held(slots, tokens, D),
                held(tokens, D),
                held(tokens, D),
                held(slots, tokens, D),
                held(slots, tokens, 3 * D),
                pltpu.SemaphoreType.DMA((slots + 1,)),
                pltpu.SemaphoreType.DMA((3,)),
                pltpu.SemaphoreType.DMA((2,)),
                pltpu.SemaphoreType.DMA((2,)),
                pltpu.SemaphoreType.DMA((slots, 2)),
                pltpu.SemaphoreType.DMA((slots, 2)),
            ],
            compiler_params=pltpu.CompilerParams(
                vmem_limit_bytes=VMEM_LIMIT, collective_id=int(with_relay), has_side_effects=True
            ),
        )(
            sample_index,
            region_ids,
            attn_gain[None],
            out_gain[None],
            *first,
            store,
            w_qkv,
            w_out,
            w_dec_t,
        )
        return pl.pallas_call(
            last_kernel,
            in_specs=[vmem] * 4,
            out_specs=hbm,
            out_shape=pltpu.HBM(store.shape, store.dtype),
            scratch_shapes=[
                held(*store.shape[1:]),
                pltpu.SemaphoreType.DMA((slots,)),
                pltpu.SemaphoreType.DMA((2,)),
            ],
            compiler_params=pltpu.CompilerParams(vmem_limit_bytes=LAST_LIMIT),
        )(samples[None], *carried)

    return lax.cond(
        relayed[0] == 1,
        functools.partial(exchange_and_place, True),
        functools.partial(exchange_and_place, False),
        *first,
    )


def local(store, sample_index, *rest):
    slots, rows_here = store.shape[:2]
    strips = (
        rows_here == HALF
        and slots == 4
        and lax.axis_size("buf") == 2
        and sample_index.shape[0] == 6
    )
    return (local_strips if strips else local_tiles)(store, sample_index, *rest)


def solution(mesh):
    return jax.shard_map(
        local,
        mesh=mesh,
        in_specs=(P("buf", ("lat", "lon"), None, None), P(), P(), P(), P(), P(), P(), P(), P()),
        out_specs=P("buf", ("lat", "lon"), None, None),
        check_vma=False,
    )
```

```python
import functools
import math

import jax
import jax.numpy as jnp
from jax import lax
from jax.experimental import pallas as pl
from jax.experimental.pallas import tpu as pltpu
from jax.sharding import PartitionSpec as P

D = 512
HEADS = 8
HDIM = 64
WIN = 8
HALF = WIN // 2
VMEM_LIMIT = 40 * 1024 * 1024
LAST_LIMIT = 40 * 1024 * 1024
FIRST_LIMIT = 56 * 1024 * 1024


def with_halo(array, sides, width):
    for axis, dim in sides:
        devices, length = (lax.axis_size(axis), array.shape[dim])
        up = [(i, (i + 1) % devices) for i in range(devices)]
        down = [(j, i) for i, j in up]
        last = lax.slice_in_dim(array, length - width, length, axis=dim)
        leading = lax.slice_in_dim(array, 0, width, axis=dim)
        before = lax.ppermute(last, axis, up)
        after = lax.ppermute(leading, axis, down)
        array = jnp.concatenate([before, array, after], axis=dim)
    return array


def layer_norm(values, gain_row):
    center = jnp.mean(values, axis=-1, keepdims=True)
    spread = jnp.mean(jnp.square(values - center), axis=-1, keepdims=True)
    return (values - center) * lax.rsqrt(spread + 1e-05) * gain_row


def window_mix(windows, regions):
    scores = jnp.einsum(
        "bwqhd,bwkhd->bwhqk",
        windows[:, :, :, 0],
        windows[:, :, :, 1],
        preferred_element_type=jnp.float32,
    ) / math.sqrt(HDIM)
    visible = (regions[:, :, None] == regions[:, None, :])[None, :, None]
    scores = jnp.where(visible, scores, -1e30)
    highest = jnp.max(scores, axis=-1, keepdims=True)
    expo_terms = jnp.where(visible, jnp.exp(scores - highest), 0.0)
    weights = (expo_terms / jnp.sum(expo_terms, axis=-1, keepdims=True)).astype(jnp.bfloat16)
    return jnp.einsum(
        "bwhqk,bwkhd->bwqhd", weights, windows[:, :, :, 2], preferred_element_type=jnp.float32
    ).astype(jnp.bfloat16)


def local_tiles(store, sample_index, region_ids, w_embed, attn_gain, w_qkv, w_out, out_gain, w_dec):
    lon_count = lax.axis_size("lon")
    slots_here, rows_here, width_all, patch_len = store.shape
    patch_cols = width_all // lon_count
    patch_rows = rows_here * lon_count
    half_win = WIN // 2
    ext_rows = patch_rows + WIN
    ext_cols = patch_cols + WIN
    own_slots = lax.axis_index("buf") * slots_here + jnp.arange(slots_here, dtype=jnp.int32)
    matches = own_slots[:, None] == sample_index[None, :]
    occupied = jnp.any(matches, axis=1)
    local_rows = store.reshape(slots_here, 1, rows_here, lon_count, patch_cols, patch_len)
    tile_data = lax.all_to_all(local_rows, "lon", split_axis=3, concat_axis=1, tiled=True)
    patches = tile_data.reshape(-1, patch_len)
    embedded = jnp.dot(patches, w_embed, preferred_element_type=jnp.float32).astype(jnp.bfloat16)
    normed = layer_norm(embedded.astype(jnp.float32), attn_gain).astype(jnp.bfloat16)
    normed = normed.reshape(slots_here, patch_rows, patch_cols, D)
    widened = with_halo(normed, (("lat", 1), ("lon", 2)), half_win)
    projected = jnp.dot(widened.reshape(-1, D), w_qkv, preferred_element_type=jnp.float32).astype(
        jnp.bfloat16
    )
    windows = projected.reshape(
        slots_here, ext_rows // WIN, WIN, ext_cols // WIN, WIN, 3, HEADS, HDIM
    )
    windows = windows.transpose(0, 1, 3, 2, 4, 5, 6, 7).reshape(
        slots_here, -1, WIN * WIN, 3, HEADS, HDIM
    )
    total_rows, total_cols = region_ids.shape
    row_pick = (
        lax.axis_index("lat") * patch_rows - half_win + jnp.arange(ext_rows, dtype=jnp.int32)
    ) % total_rows
    col_pick = (
        lax.axis_index("lon") * patch_cols - half_win + jnp.arange(ext_cols, dtype=jnp.int32)
    ) % total_cols
    local_regions = jnp.take(jnp.take(region_ids, row_pick, axis=0), col_pick, axis=1)
    region_windows = (
        local_regions.reshape(ext_rows // WIN, WIN, ext_cols // WIN, WIN)
        .transpose(0, 2, 1, 3)
        .reshape(-1, WIN * WIN)
    )
    mixed_heads = window_mix(windows, region_windows)
    placed = mixed_heads.reshape(slots_here, ext_rows // WIN, ext_cols // WIN, WIN, WIN, D)
    placed = placed.transpose(0, 1, 3, 2, 4, 5).reshape(slots_here, ext_rows, ext_cols, D)
    placed = placed[:, half_win : half_win + patch_rows, half_win : half_win + patch_cols].reshape(
        -1, D
    )
    updated = embedded.astype(jnp.float32) + jnp.dot(
        placed, w_out, preferred_element_type=jnp.float32
    )
    final_norm = layer_norm(updated, out_gain).astype(jnp.bfloat16)
    predicted = (
        patches.astype(jnp.float32) + jnp.dot(final_norm, w_dec, preferred_element_type=jnp.float32)
    ).astype(jnp.bfloat16)
    outgoing = predicted.reshape(slots_here, lon_count, rows_here, 1, patch_cols, patch_len)
    returned = lax.all_to_all(outgoing, "lon", split_axis=1, concat_axis=3, tiled=True)
    strip_data = returned.reshape(slots_here, rows_here, width_all, patch_len)
    return jnp.where(occupied[:, None, None, None], strip_data, store)


def to_windows(values):
    rows, cols = HALF, values.shape[0] // HALF
    parts = [pltpu.roll(values[cols * i : cols * (i + 1)], cols - HALF, 0) for i in range(rows)]
    return jnp.concatenate(
        [parts[i][WIN * c : WIN * (c + 1)] for c in range(cols // WIN) for i in range(rows)], axis=0
    )


def from_windows(values):
    rows, cols = HALF, values.shape[0] // HALF
    parts = []
    for i in range(rows):
        line = jnp.concatenate(
            [
                values[WIN * (rows * c + i) : WIN * (rows * c + i + 1)]
                for c in range(cols // WIN)
            ],
            axis=0,
        )
        parts.append(pltpu.roll(line, HALF, 0))
    return jnp.concatenate(parts, axis=0)


def embed_slot(patches, w_embed, gain):
    embedded = jnp.dot(patches, w_embed, preferred_element_type=jnp.float32).astype(jnp.bfloat16)
    embedded = to_windows(embedded.astype(jnp.float32))
    normed = layer_norm(embedded, gain).astype(jnp.bfloat16)
    return embedded.astype(jnp.bfloat16), normed


NT = (((1,), (1,)), ((), ()))
TN = (((0,), (0,)), ((), ()))
GROUP = 4
WIDE = GROUP * HDIM
PER = WIN * HALF


def attend_slot(query, kv_own, kv_other, q_regions, k_regions):
    shape = (GROUP * PER, WIDE)
    pick = (
        lax.broadcasted_iota(jnp.int32, shape, 0) // PER
        == lax.broadcasted_iota(jnp.int32, shape, 1) // HDIM
    )
    head_mask = jnp.where(pick, 1.0, 0.0).astype(jnp.bfloat16)
    windows = query.shape[0] // PER
    kvs, scores, weights, mixed = [], [], [], []
    for c in range(windows):
        at = slice(PER * c, PER * (c + 1))
        kvs.append(jnp.concatenate([kv_own[at], kv_other[at]], axis=0))
        for g in range(HEADS // GROUP):
            cols = slice(WIDE * g, WIDE * (g + 1))
            queries = jnp.concatenate([query[at, cols]] * GROUP, axis=0) * head_mask
            scores.append(
                lax.dot_general(kvs[c][:, cols], queries, NT, preferred_element_type=jnp.float32)
            )
    for c in range(windows):
        seen = k_regions[:, c : c + 1] == q_regions[c : c + 1, :]
        for g in range(HEADS // GROUP):
            part = jnp.where(seen, scores[2 * c + g], -1e30)
            expo = jnp.exp(part - jnp.max(part, axis=0, keepdims=True))
            total = jnp.sum(expo, axis=0, keepdims=True)
            weights.append((expo * (1.0 / total)).astype(jnp.bfloat16))
    for c in range(windows):
        groups = []
        for g in range(HEADS // GROUP):
            heads = lax.dot_general(
                weights[2 * c + g],
                kvs[c][:, D + WIDE * g : D + WIDE * (g + 1)],
                TN,
                preferred_element_type=jnp.float32,
            )
            heads = jnp.where(pick, heads, 0.0)
            total = heads[:PER]
            for h in range(1, GROUP):
                total = total + heads[PER * h : PER * (h + 1)]
            groups.append(total)
        mixed.append(jnp.concatenate(groups, axis=1).astype(jnp.bfloat16))
    return jnp.concatenate(mixed, axis=0)


def region_tables(own, far):
    rows, cols = own.shape
    windows = cols // WIN
    lines = [own[i : i + 1] for i in range(rows)] + [far[i : i + 1] for i in range(rows)]
    wide = jnp.concatenate([jnp.broadcast_to(line, (WIN, cols)) for line in lines], axis=0)
    row = lax.broadcasted_iota(jnp.int32, wide.shape, 0)
    col = lax.broadcasted_iota(jnp.int32, wide.shape, 1)
    kept = jnp.where((col + WIN - HALF) % WIN == row % WIN, wide, 0.0).astype(jnp.bfloat16)
    place = (lax.broadcasted_iota(jnp.int32, (windows, cols), 1) + cols - HALF) % cols // WIN
    here = place == lax.broadcasted_iota(jnp.int32, (windows, cols), 0)
    here = jnp.where(here, 1.0, 0.0).astype(jnp.bfloat16)
    k_regions = lax.dot_general(kept, here, NT, preferred_element_type=jnp.float32)
    q_rows = jnp.concatenate([kept[:PER]] * GROUP, axis=0)
    q_regions = lax.dot_general(here, q_rows, NT, preferred_element_type=jnp.float32)
    return q_regions, k_regions


def finish_part(embedded, mixed, w_out, gain):
    updated = embedded.astype(jnp.float32) + jnp.dot(
        mixed, w_out, preferred_element_type=jnp.float32
    )
    return layer_norm(updated, gain)


def decode_slot(patches, final, w_dec_t):
    return (
        patches.astype(jnp.float32)
        + lax.dot_general(
            final, w_dec_t, (((1,), (1,)), ((), ())), preferred_element_type=jnp.float32
        )
    ).astype(jnp.bfloat16)


MESH = pl.DeviceIdType.MESH
UNIT_A, UNIT_C, UNIT_D, UNIT_B = range(4)


def slot_order(sample_ref, slots):
    first = lax.axis_index("buf") * slots
    taken = []
    samples = len(sample_ref) if isinstance(sample_ref, list) else sample_ref.shape[0]
    for s in range(slots):
        hit = sample_ref[0] == first + s
        for b in range(1, samples):
            hit = jnp.logical_or(hit, sample_ref[b] == first + s)
        taken.append(hit.astype(jnp.int32))
    count = sum(taken)
    places, before = [], jnp.int32(0)
    for s in range(slots):
        places.append(jnp.where(taken[s] == 1, before, count + s - before))
        before = before + taken[s]
    order = [
        sum(jnp.where(places[s] == j, jnp.int32(s), 0) for s in range(slots)) for j in range(slots)
    ]
    return [order[j] for j in (0, 2, 3, 1)], count


def first_kernel(
    sample_ref,
    gain_ref,
    store_ref,
    w_embed_ref,
    w_embed,
    grabbed,
    embedded,
    own,
    branch,
    sample,
    gain,
    sems,
):
    slots, rows_here, cols, patch_len = store_ref.shape
    weight = pltpu.make_async_copy(w_embed_ref, w_embed, sems.at[0])
    sample_in = pltpu.make_async_copy(sample_ref, sample, sems.at[3])
    gain_in = pltpu.make_async_copy(gain_ref, gain, sems.at[4])
    sample_in.start()
    weight.start()
    gain_in.start()
    sample_in.wait()
    order, count = slot_order(sample, slots)
    buf = lax.axis_index("buf")
    heavy = jnp.where(count == slots, buf, 1 - buf)
    branch[0] = jnp.where(2 * count == sample.shape[0], 0, 1 + heavy)
    fetch_a = pltpu.make_async_copy(store_ref.at[order[UNIT_A]], grabbed.at[0], sems.at[1])
    fetch_d = pltpu.make_async_copy(store_ref.at[order[UNIT_D]], grabbed.at[1], sems.at[2])
    fetch_a.start()
    gain_in.wait()
    weight.wait()
    fetch_d.start()
    fetch_a.wait()
    flat = grabbed[0].reshape(rows_here * cols, patch_len)
    embedded[...], own[...] = embed_slot(flat, w_embed[...], gain[...])
    fetch_d.wait()


def exchange_kernel(
    heavy_owner,
    sample_in,
    region_ref,
    a_gain_ref,
    o_gain_ref,
    w_embed,
    grabbed,
    embedded_a,
    own_a,
    store_ref,
    w_qkv_ref,
    w_out_ref,
    w_dec_ref,
    result,
    w_dec,
    finals,
    sample,
    w_qkv,
    w_out,
    q_table,
    k_table,
    q_parts,
    k_parts,
    patches,
    embedded,
    own,
    relay,
    far,
    own_qkv,
    slot_sems,
    weight_sems,
    relay_send_sems,
    relay_recv_sems,
    send_sems,
    recv_sems,
):
    slots, rows_here, cols, patch_len = store_ref.shape
    lon_count = lax.axis_size("lon")
    strips = lax.axis_size("lat") * lon_count
    mine = lax.axis_index("lat") * lon_count + lax.axis_index("lon")
    other = lax.rem(mine + 2 * lax.rem(mine, 2) - 1 + strips, strips)
    partner = {"lat": lax.div(other, lon_count), "lon": lax.rem(other, lon_count)}
    relayed = heavy_owner is not None
    buf = lax.axis_index("buf")
    heavy = buf == heavy_owner if relayed else buf >= 0
    peer = {"buf": 1 - buf}
    across = dict(partner, buf=1 - buf)
    apart = jnp.abs(lax.div(other, lon_count) - lax.axis_index("lat"))
    near = apart != 1 if heavy_owner is not None else apart == 0
    tokens = rows_here * cols
    half = tokens // 2
    windows = tokens // PER

    def part(h):
        return pl.ds(half * h if isinstance(h, int) else pl.multiple_of(half * h, half), half)

    barrier = pltpu.get_barrier_semaphore()
    pl.semaphore_signal(barrier, inc=1, device_id=partner, device_id_type=MESH)
    if relayed:
        sender = {
            "lat": jnp.where(heavy, lax.axis_index("lat"), partner["lat"]),
            "lon": jnp.where(heavy, lax.axis_index("lon"), partner["lon"]),
            "buf": 1 - buf,
        }
        pl.semaphore_signal(barrier, inc=1, device_id=sender, device_id_type=MESH)

    fetches = [
        pltpu.make_async_copy(store_ref.at[s], patches.at[s], slot_sems.at[s])
        for s in range(slots)
    ]
    fetches.append(pltpu.make_async_copy(sample_in, sample, slot_sems.at[slots]))
    for copy in reversed(fetches):
        copy.start()
    weights = [
        pltpu.make_async_copy(src, dst, weight_sems.at[i])
        for i, (src, dst) in enumerate(
            ((w_qkv_ref, w_qkv), (w_out_ref, w_out), (w_dec_ref, w_dec))
        )
    ]
    def send(k, h, at, src, device):
        return pltpu.make_async_remote_copy(
            src_ref=src.at[at],
            dst_ref=far.at[k, at],
            send_sem=send_sems.at[k, h],
            recv_sem=recv_sems.at[k, h],
            device_id=device,
            device_id_type=MESH,
        )

    def send_half(k, h):
        return send(k, h, part(h), own_a if k == UNIT_A else own.at[UNIT_C], partner)

    def send_piece(q):
        return send(UNIT_B, q, part(q), own.at[UNIT_B], partner)

    def arrival(k, h):
        return send(k, h, part(h), far.at[k], partner)

    def forward(h):
        return send(UNIT_D, h, part(h), relay, peer)

    def relay_half(h):
        return pltpu.make_async_remote_copy(
            src_ref=own.at[UNIT_D, part(h)],
            dst_ref=relay.at[part(h)],
            send_sem=relay_send_sems.at[h],
            recv_sem=relay_recv_sems.at[h],
            device_id=across,
            device_id_type=MESH,
        )

    def embed(k, values):
        flat = values.reshape(tokens, patch_len)
        embedded[k], own[k] = embed_slot(flat, w_embed[...], a_gain_ref[...])

    pl.semaphore_wait(barrier, 2 if relayed else 1)
    @pl.when(near)
    def _():
        for h in range(2):
            send_half(UNIT_A, h).start()

    if relayed:

        @pl.when(heavy)
        def _():
            embed(UNIT_D, grabbed[1])
            for h in range(2):
                relay_half(h).start()

    @pl.when(jnp.logical_not(near))
    def _():
        for h in range(2):
            send_half(UNIT_A, h).start()

    embedded[UNIT_A] = embedded_a[...]
    own[UNIT_A] = own_a[...]
    q_regions, k_regions = region_tables(
        region_ref[pl.ds(mine * HALF, HALF), :].astype(jnp.float32),
        region_ref[pl.ds(other * HALF, HALF), :].astype(jnp.float32),
    )
    q_table[...] = q_regions
    k_table[...] = k_regions
    each = windows // 2
    for q in range(2):
        q_parts[q] = q_regions[each * q : each * (q + 1)]
        k_parts[q] = k_regions[:, each * q : each * (q + 1)]
    for copy in fetches:
        copy.wait()
    for copy in weights:
        copy.start()
    order, _ = slot_order(sample, slots)

    @pl.when(heavy)
    def _():
        embed(UNIT_C, patches[order[UNIT_C]])

        @pl.when(near)
        def _():
            for h in range(2):
                send_half(UNIT_C, h).start()

    embed(UNIT_B, patches[order[UNIT_B]])

    @pl.when(jnp.logical_and(near, heavy))
    def _():
        for q in range(2):
            send_piece(q).start()

    @pl.when(jnp.logical_and(heavy, jnp.logical_not(near)))
    def _():
        for h in range(2):
            send_half(UNIT_C, h).start()

    result[UNIT_B] = patches[order[UNIT_B]]
    if not relayed:
        result[UNIT_D] = patches[order[UNIT_D]]

    weights[0].wait()

    def project(k):
        query = jnp.dot(own[k], w_qkv[:, :D], preferred_element_type=jnp.float32)
        own_qkv[k, :, :D] = (query * (1.0 / math.sqrt(HDIM))).astype(jnp.bfloat16)
        own_qkv[k, :, D:] = jnp.dot(
            own[k], w_qkv[:, D:], preferred_element_type=jnp.float32
        ).astype(jnp.bfloat16)

    for k in (UNIT_A, UNIT_B):
        project(k)

    @pl.when(heavy)
    def _():
        for k in (UNIT_C, UNIT_D) if relayed else (UNIT_C,):
            project(k)

    if relayed:

        @pl.when(jnp.logical_and(heavy, jnp.logical_not(near)))
        def _():
            for q in range(2):
                send_piece(q).start()

        @pl.when(jnp.logical_not(heavy))
        def _():
            for h in range(2):
                relay_half(h).wait_recv()
                forward(h).start()
            for q in range(2):
                send_piece(q).start()
            for k in (UNIT_C, UNIT_D):
                result[k] = patches[order[k]]

    weights[1].wait()
    weights[2].wait()

    def mix(k, at, q_regions, k_regions):
        kv_other = jnp.dot(far[k, at], w_qkv[:, D:], preferred_element_type=jnp.float32)
        mixed = attend_slot(
            own_qkv[k, at, :D],
            own_qkv[k, at, D:],
            kv_other.astype(jnp.bfloat16),
            q_regions,
            k_regions,
        )
        return finish_part(embedded[k, at], mixed, w_out[...], o_gain_ref[...])

    wholes = UNIT_B if relayed else UNIT_D

    @pl.loop(0, wholes + 2)
    def _(step):
        k = step
        if relayed:
            k = jnp.where(step == UNIT_D, wholes, jnp.where(step == wholes, UNIT_D, step))

        @pl.when(jnp.logical_and(k < wholes, jnp.logical_or(heavy, k == UNIT_A)))
        def _():
            for h in range(2):
                arrival(k, h).wait_recv()

            mixed = mix(k, pl.ds(0, tokens), q_table[...], k_table[...])
            final = from_windows(mixed).astype(jnp.bfloat16)
            place = jnp.where(
                k == UNIT_A, order[UNIT_A], jnp.where(k == UNIT_C, order[UNIT_C], order[UNIT_D])
            )
            flat = patches[place].reshape(tokens, patch_len)
            result[k] = decode_slot(flat, final, w_dec[...]).reshape(rows_here, cols, patch_len)

            if not relayed:

                @pl.when(jnp.logical_and(k == UNIT_A, jnp.logical_not(near)))
                def _():
                    for q in range(2):
                        send_piece(q).start()

        @pl.when(k >= wholes)
        def _():
            q = k - wholes
            send_piece(q).wait_recv()
            finals[part(q)] = mix(UNIT_B, part(q), q_parts[q], k_parts[q])

    for h in range(2):
        send_half(UNIT_A, h).wait_send()
        send_piece(h).wait_send()

    @pl.when(heavy)
    def _():
        for h in range(2):
            send_half(UNIT_C, h).wait_send()
            if relayed:
                relay_half(h).wait_send()

    if relayed:

        @pl.when(jnp.logical_not(heavy))
        def _():
            for h in range(2):
                forward(h).wait_send()


def last_kernel(sample_ref, result, w_dec, finals, new_ref, decoded, sems, row_sems):
    slots, rows_here, cols, patch_len = result.shape
    samples = sample_ref[...]
    order, _ = slot_order([samples[0, b] for b in range(samples.shape[1])], slots)
    copies = [
        pltpu.make_async_copy(result.at[k], new_ref.at[order[k]], sems.at[k])
        for k in (UNIT_A, UNIT_C, UNIT_D)
    ]
    for copy in copies:
        copy.start()
    half = rows_here * cols // 2
    final = from_windows(finals[...]).astype(jnp.bfloat16)
    rows = rows_here // 2
    for h in range(2):
        here = slice(rows * h, rows * (h + 1))
        decoded[here] = decode_slot(
            result[UNIT_B, here].reshape(half, patch_len),
            final[half * h : half * (h + 1)],
            w_dec[...],
        ).reshape(rows, cols, patch_len)
        copies.append(
            pltpu.make_async_copy(
                decoded.at[here], new_ref.at[order[UNIT_B], here], row_sems.at[h]
            )
        )
        copies[-1].start()
    for copy in copies:
        copy.wait()


def local_strips(
    store, sample_index, region_ids, w_embed, attn_gain, w_qkv, w_out, out_gain, w_dec
):
    slots, rows_here, cols, patch_len = store.shape
    tokens = rows_here * cols
    windows = tokens // PER
    held = lambda *shape: pltpu.VMEM(shape, jnp.bfloat16)
    wide = lambda *shape: pltpu.VMEM(shape, jnp.float32)
    vmem = pl.BlockSpec(memory_space=pltpu.VMEM)
    hbm = pl.BlockSpec(memory_space=pltpu.HBM)
    in_hbm = lambda array: pltpu.with_memory_space_constraint(array, pltpu.HBM)
    samples, sample_index, store = sample_index, in_hbm(sample_index), in_hbm(store)
    w_embed, w_qkv, w_out = in_hbm(w_embed), in_hbm(w_qkv), in_hbm(w_out)
    w_dec_t = in_hbm(w_dec.T)
    *first, branch = pl.pallas_call(
        first_kernel,
        in_specs=[hbm] * 4,
        out_specs=[vmem] * 4 + [pl.BlockSpec(memory_space=pltpu.SMEM)],
        out_shape=[
            held(*w_embed.shape),
            held(2, *store.shape[1:]),
            held(tokens, D),
            held(tokens, D),
            pltpu.SMEM((1,), jnp.int32),
        ],
        scratch_shapes=[
            pltpu.SMEM(sample_index.shape, jnp.int32),
            wide(1, D),
            pltpu.SemaphoreType.DMA((5,)),
        ],
        compiler_params=pltpu.CompilerParams(vmem_limit_bytes=FIRST_LIMIT),
    )(sample_index, in_hbm(attn_gain[None]), store, w_embed)
    def exchange_and_place(heavy_owner, *first):
        carried = pl.pallas_call(
            functools.partial(exchange_kernel, heavy_owner),
            in_specs=[hbm] + [vmem] * 7 + [hbm] * 4,
            out_specs=[vmem] * 3,
            out_shape=[
                held(*store.shape),
                held(*w_dec_t.shape),
                wide(tokens, D),
            ],
            scratch_shapes=[
                pltpu.SMEM(sample_index.shape, jnp.int32),
                held(*w_qkv.shape),
                held(*w_out.shape),
                wide(windows, GROUP * PER),
                wide(2 * PER, windows),
                wide(2, windows // 2, GROUP * PER),
                wide(2, 2 * PER, windows // 2),
                held(*store.shape),
                held(slots, tokens, D),
                held(slots, tokens, D),
                held(tokens, D),
                held(slots, tokens, D),
                held(slots, tokens, 3 * D),
                pltpu.SemaphoreType.DMA((slots + 1,)),
                pltpu.SemaphoreType.DMA((3,)),
                pltpu.SemaphoreType.DMA((2,)),
                pltpu.SemaphoreType.DMA((2,)),
                pltpu.SemaphoreType.DMA((slots, 2)),
                pltpu.SemaphoreType.DMA((slots, 2)),
            ],
            compiler_params=pltpu.CompilerParams(
                vmem_limit_bytes=VMEM_LIMIT,
                collective_id=0 if heavy_owner is None else 1 + heavy_owner,
                has_side_effects=True,
            ),
        )(
            sample_index,
            region_ids,
            attn_gain[None],
            out_gain[None],
            *first,
            store,
            w_qkv,
            w_out,
            w_dec_t,
        )
        return pl.pallas_call(
            last_kernel,
            in_specs=[vmem] * 4,
            out_specs=hbm,
            out_shape=pltpu.HBM(store.shape, store.dtype),
            scratch_shapes=[
                held(*store.shape[1:]),
                pltpu.SemaphoreType.DMA((slots,)),
                pltpu.SemaphoreType.DMA((2,)),
            ],
            compiler_params=pltpu.CompilerParams(vmem_limit_bytes=LAST_LIMIT),
        )(samples[None], *carried)

    branches = [functools.partial(exchange_and_place, owner) for owner in (None, 0, 1)]
    return lax.switch(branch[0], branches, *first)


def local(store, sample_index, *rest):
    slots, rows_here = store.shape[:2]
    strips = (
        rows_here == HALF
        and slots == 4
        and lax.axis_size("buf") == 2
        and sample_index.shape[0] == 6
    )
    return (local_strips if strips else local_tiles)(store, sample_index, *rest)


def solution(mesh):
    return jax.shard_map(
        local,
        mesh=mesh,
        in_specs=(P("buf", ("lat", "lon"), None, None), P(), P(), P(), P(), P(), P(), P(), P()),
        out_specs=P("buf", ("lat", "lon"), None, None),
        check_vma=False,
    )
```

```python
import functools
import math

import jax
import jax.numpy as jnp
from jax import lax
from jax.experimental import pallas as pl
from jax.experimental.pallas import tpu as pltpu
from jax.sharding import PartitionSpec as P

D = 512
HEADS = 8
HDIM = 64
WIN = 8
HALF = WIN // 2
VMEM_LIMIT = 40 * 1024 * 1024
LAST_LIMIT = 40 * 1024 * 1024
FIRST_LIMIT = 56 * 1024 * 1024


def with_halo(array, sides, width):
    for axis, dim in sides:
        devices, length = (lax.axis_size(axis), array.shape[dim])
        up = [(i, (i + 1) % devices) for i in range(devices)]
        down = [(j, i) for i, j in up]
        last = lax.slice_in_dim(array, length - width, length, axis=dim)
        leading = lax.slice_in_dim(array, 0, width, axis=dim)
        before = lax.ppermute(last, axis, up)
        after = lax.ppermute(leading, axis, down)
        array = jnp.concatenate([before, array, after], axis=dim)
    return array


def layer_norm(values, gain_row):
    center = jnp.mean(values, axis=-1, keepdims=True)
    spread = jnp.mean(jnp.square(values - center), axis=-1, keepdims=True)
    return (values - center) * lax.rsqrt(spread + 1e-05) * gain_row


def window_mix(windows, regions):
    scores = jnp.einsum(
        "bwqhd,bwkhd->bwhqk",
        windows[:, :, :, 0],
        windows[:, :, :, 1],
        preferred_element_type=jnp.float32,
    ) / math.sqrt(HDIM)
    visible = (regions[:, :, None] == regions[:, None, :])[None, :, None]
    scores = jnp.where(visible, scores, -1e30)
    highest = jnp.max(scores, axis=-1, keepdims=True)
    expo_terms = jnp.where(visible, jnp.exp(scores - highest), 0.0)
    weights = (expo_terms / jnp.sum(expo_terms, axis=-1, keepdims=True)).astype(jnp.bfloat16)
    return jnp.einsum(
        "bwhqk,bwkhd->bwqhd", weights, windows[:, :, :, 2], preferred_element_type=jnp.float32
    ).astype(jnp.bfloat16)


def local_tiles(store, sample_index, region_ids, w_embed, attn_gain, w_qkv, w_out, out_gain, w_dec):
    lon_count = lax.axis_size("lon")
    slots_here, rows_here, width_all, patch_len = store.shape
    patch_cols = width_all // lon_count
    patch_rows = rows_here * lon_count
    half_win = WIN // 2
    ext_rows = patch_rows + WIN
    ext_cols = patch_cols + WIN
    own_slots = lax.axis_index("buf") * slots_here + jnp.arange(slots_here, dtype=jnp.int32)
    matches = own_slots[:, None] == sample_index[None, :]
    occupied = jnp.any(matches, axis=1)
    local_rows = store.reshape(slots_here, 1, rows_here, lon_count, patch_cols, patch_len)
    tile_data = lax.all_to_all(local_rows, "lon", split_axis=3, concat_axis=1, tiled=True)
    patches = tile_data.reshape(-1, patch_len)
    embedded = jnp.dot(patches, w_embed, preferred_element_type=jnp.float32).astype(jnp.bfloat16)
    normed = layer_norm(embedded.astype(jnp.float32), attn_gain).astype(jnp.bfloat16)
    normed = normed.reshape(slots_here, patch_rows, patch_cols, D)
    widened = with_halo(normed, (("lat", 1), ("lon", 2)), half_win)
    projected = jnp.dot(widened.reshape(-1, D), w_qkv, preferred_element_type=jnp.float32).astype(
        jnp.bfloat16
    )
    windows = projected.reshape(
        slots_here, ext_rows // WIN, WIN, ext_cols // WIN, WIN, 3, HEADS, HDIM
    )
    windows = windows.transpose(0, 1, 3, 2, 4, 5, 6, 7).reshape(
        slots_here, -1, WIN * WIN, 3, HEADS, HDIM
    )
    total_rows, total_cols = region_ids.shape
    row_pick = (
        lax.axis_index("lat") * patch_rows - half_win + jnp.arange(ext_rows, dtype=jnp.int32)
    ) % total_rows
    col_pick = (
        lax.axis_index("lon") * patch_cols - half_win + jnp.arange(ext_cols, dtype=jnp.int32)
    ) % total_cols
    local_regions = jnp.take(jnp.take(region_ids, row_pick, axis=0), col_pick, axis=1)
    region_windows = (
        local_regions.reshape(ext_rows // WIN, WIN, ext_cols // WIN, WIN)
        .transpose(0, 2, 1, 3)
        .reshape(-1, WIN * WIN)
    )
    mixed_heads = window_mix(windows, region_windows)
    placed = mixed_heads.reshape(slots_here, ext_rows // WIN, ext_cols // WIN, WIN, WIN, D)
    placed = placed.transpose(0, 1, 3, 2, 4, 5).reshape(slots_here, ext_rows, ext_cols, D)
    placed = placed[:, half_win : half_win + patch_rows, half_win : half_win + patch_cols].reshape(
        -1, D
    )
    updated = embedded.astype(jnp.float32) + jnp.dot(
        placed, w_out, preferred_element_type=jnp.float32
    )
    final_norm = layer_norm(updated, out_gain).astype(jnp.bfloat16)
    predicted = (
        patches.astype(jnp.float32) + jnp.dot(final_norm, w_dec, preferred_element_type=jnp.float32)
    ).astype(jnp.bfloat16)
    outgoing = predicted.reshape(slots_here, lon_count, rows_here, 1, patch_cols, patch_len)
    returned = lax.all_to_all(outgoing, "lon", split_axis=1, concat_axis=3, tiled=True)
    strip_data = returned.reshape(slots_here, rows_here, width_all, patch_len)
    return jnp.where(occupied[:, None, None, None], strip_data, store)


def to_windows(values):
    rows, cols = HALF, values.shape[0] // HALF
    parts = [pltpu.roll(values[cols * i : cols * (i + 1)], cols - HALF, 0) for i in range(rows)]
    return jnp.concatenate(
        [parts[i][WIN * c : WIN * (c + 1)] for c in range(cols // WIN) for i in range(rows)], axis=0
    )


def from_windows(values):
    rows, cols = HALF, values.shape[0] // HALF
    parts = []
    for i in range(rows):
        line = jnp.concatenate(
            [
                values[WIN * (rows * c + i) : WIN * (rows * c + i + 1)]
                for c in range(cols // WIN)
            ],
            axis=0,
        )
        parts.append(pltpu.roll(line, HALF, 0))
    return jnp.concatenate(parts, axis=0)


def embed_slot(patches, w_embed, gain):
    embedded = jnp.dot(patches, w_embed, preferred_element_type=jnp.float32).astype(jnp.bfloat16)
    embedded = to_windows(embedded.astype(jnp.float32))
    normed = layer_norm(embedded, gain).astype(jnp.bfloat16)
    return embedded.astype(jnp.bfloat16), normed


NT = (((1,), (1,)), ((), ()))
TN = (((0,), (0,)), ((), ()))
GROUP = 4
WIDE = GROUP * HDIM
PER = WIN * HALF


def attend_slot(query, kv_own, kv_other, q_regions, k_regions):
    shape = (GROUP * PER, WIDE)
    pick = (
        lax.broadcasted_iota(jnp.int32, shape, 0) // PER
        == lax.broadcasted_iota(jnp.int32, shape, 1) // HDIM
    )
    head_mask = jnp.where(pick, 1.0, 0.0).astype(jnp.bfloat16)
    windows = query.shape[0] // PER
    kvs, scores, weights, mixed = [], [], [], []
    for c in range(windows):
        at = slice(PER * c, PER * (c + 1))
        kvs.append(jnp.concatenate([kv_own[at], kv_other[at]], axis=0))
        for g in range(HEADS // GROUP):
            cols = slice(WIDE * g, WIDE * (g + 1))
            queries = jnp.concatenate([query[at, cols]] * GROUP, axis=0) * head_mask
            scores.append(
                lax.dot_general(kvs[c][:, cols], queries, NT, preferred_element_type=jnp.float32)
            )
    for c in range(windows):
        seen = k_regions[:, c : c + 1] == q_regions[c : c + 1, :]
        for g in range(HEADS // GROUP):
            part = jnp.where(seen, scores[2 * c + g], -1e30)
            expo = jnp.exp(part - jnp.max(part, axis=0, keepdims=True))
            total = jnp.sum(expo, axis=0, keepdims=True)
            weights.append((expo * (1.0 / total)).astype(jnp.bfloat16))
    for c in range(windows):
        groups = []
        for g in range(HEADS // GROUP):
            heads = lax.dot_general(
                weights[2 * c + g],
                kvs[c][:, D + WIDE * g : D + WIDE * (g + 1)],
                TN,
                preferred_element_type=jnp.float32,
            )
            heads = jnp.where(pick, heads, 0.0)
            total = heads[:PER]
            for h in range(1, GROUP):
                total = total + heads[PER * h : PER * (h + 1)]
            groups.append(total)
        mixed.append(jnp.concatenate(groups, axis=1).astype(jnp.bfloat16))
    return jnp.concatenate(mixed, axis=0)


def region_tables(own, far):
    rows, cols = own.shape
    windows = cols // WIN
    lines = [own[i : i + 1] for i in range(rows)] + [far[i : i + 1] for i in range(rows)]
    wide = jnp.concatenate([jnp.broadcast_to(line, (WIN, cols)) for line in lines], axis=0)
    row = lax.broadcasted_iota(jnp.int32, wide.shape, 0)
    col = lax.broadcasted_iota(jnp.int32, wide.shape, 1)
    kept = jnp.where((col + WIN - HALF) % WIN == row % WIN, wide, 0.0).astype(jnp.bfloat16)
    place = (lax.broadcasted_iota(jnp.int32, (windows, cols), 1) + cols - HALF) % cols // WIN
    here = place == lax.broadcasted_iota(jnp.int32, (windows, cols), 0)
    here = jnp.where(here, 1.0, 0.0).astype(jnp.bfloat16)
    k_regions = lax.dot_general(kept, here, NT, preferred_element_type=jnp.float32)
    q_rows = jnp.concatenate([kept[:PER]] * GROUP, axis=0)
    q_regions = lax.dot_general(here, q_rows, NT, preferred_element_type=jnp.float32)
    return q_regions, k_regions


def finish_part(embedded, mixed, w_out, gain):
    updated = embedded.astype(jnp.float32) + jnp.dot(
        mixed, w_out, preferred_element_type=jnp.float32
    )
    return layer_norm(updated, gain)


def decode_slot(patches, final, w_dec_t):
    return (
        patches.astype(jnp.float32)
        + lax.dot_general(
            final, w_dec_t, (((1,), (1,)), ((), ())), preferred_element_type=jnp.float32
        )
    ).astype(jnp.bfloat16)


MESH = pl.DeviceIdType.MESH
UNIT_A, UNIT_C, UNIT_D, UNIT_B = range(4)


def slot_order(sample_ref, slots):
    first = lax.axis_index("buf") * slots
    taken = []
    samples = len(sample_ref) if isinstance(sample_ref, list) else sample_ref.shape[0]
    for s in range(slots):
        hit = sample_ref[0] == first + s
        for b in range(1, samples):
            hit = jnp.logical_or(hit, sample_ref[b] == first + s)
        taken.append(hit.astype(jnp.int32))
    count = sum(taken)
    places, before = [], jnp.int32(0)
    for s in range(slots):
        places.append(jnp.where(taken[s] == 1, before, count + s - before))
        before = before + taken[s]
    order = [
        sum(jnp.where(places[s] == j, jnp.int32(s), 0) for s in range(slots)) for j in range(slots)
    ]
    return [order[j] for j in (0, 2, 3, 1)], count


def first_kernel(
    sample_ref,
    gain_ref,
    store_ref,
    w_embed_ref,
    w_embed,
    grabbed,
    embedded,
    own,
    branch,
    sample,
    gain,
    sems,
):
    slots, rows_here, cols, patch_len = store_ref.shape
    weight = pltpu.make_async_copy(w_embed_ref, w_embed, sems.at[0])
    sample_in = pltpu.make_async_copy(sample_ref, sample, sems.at[3])
    gain_in = pltpu.make_async_copy(gain_ref, gain, sems.at[4])
    sample_in.start()
    weight.start()
    gain_in.start()
    sample_in.wait()
    order, count = slot_order(sample, slots)
    buf = lax.axis_index("buf")
    heavy = jnp.where(count == slots, buf, 1 - buf)
    branch[0] = jnp.where(2 * count == sample.shape[0], 0, 1 + heavy)
    fetch_a = pltpu.make_async_copy(store_ref.at[order[UNIT_A]], grabbed.at[0], sems.at[1])
    fetch_d = pltpu.make_async_copy(store_ref.at[order[UNIT_D]], grabbed.at[1], sems.at[2])
    fetch_a.start()
    gain_in.wait()
    weight.wait()
    fetch_d.start()
    fetch_a.wait()
    flat = grabbed[0].reshape(rows_here * cols, patch_len)
    embedded[...], own[...] = embed_slot(flat, w_embed[...], gain[...])
    fetch_d.wait()


def exchange_kernel(
    heavy_owner,
    sample_in,
    region_ref,
    a_gain_ref,
    o_gain_ref,
    w_embed,
    grabbed,
    embedded_a,
    own_a,
    store_ref,
    w_qkv_ref,
    w_out_ref,
    w_dec_ref,
    result,
    w_dec,
    finals,
    sample,
    w_qkv,
    w_out,
    q_table,
    k_table,
    q_parts,
    k_parts,
    patches,
    embedded,
    own,
    relay,
    far,
    own_qkv,
    slot_sems,
    weight_sems,
    relay_send_sems,
    relay_recv_sems,
    send_sems,
    recv_sems,
):
    slots, rows_here, cols, patch_len = store_ref.shape
    lon_count = lax.axis_size("lon")
    strips = lax.axis_size("lat") * lon_count
    mine = lax.axis_index("lat") * lon_count + lax.axis_index("lon")
    other = lax.rem(mine + 2 * lax.rem(mine, 2) - 1 + strips, strips)
    partner = {"lat": lax.div(other, lon_count), "lon": lax.rem(other, lon_count)}
    relayed = heavy_owner is not None
    buf = lax.axis_index("buf")
    heavy = buf == heavy_owner if relayed else buf >= 0
    peer = {"buf": 1 - buf}
    across = dict(partner, buf=1 - buf)
    apart = jnp.abs(lax.div(other, lon_count) - lax.axis_index("lat"))
    near = apart != 1 if heavy_owner is not None else apart == 0
    tokens = rows_here * cols
    half = tokens // 2
    windows = tokens // PER

    def part(h):
        return pl.ds(half * h if isinstance(h, int) else pl.multiple_of(half * h, half), half)

    barrier = pltpu.get_barrier_semaphore()
    pl.semaphore_signal(barrier, inc=1, device_id=partner, device_id_type=MESH)
    if relayed:
        sender = {
            "lat": jnp.where(heavy, lax.axis_index("lat"), partner["lat"]),
            "lon": jnp.where(heavy, lax.axis_index("lon"), partner["lon"]),
            "buf": 1 - buf,
        }
        pl.semaphore_signal(barrier, inc=1, device_id=sender, device_id_type=MESH)

    fetches = [
        pltpu.make_async_copy(store_ref.at[s], patches.at[s], slot_sems.at[s])
        for s in range(slots)
    ]
    fetches.append(pltpu.make_async_copy(sample_in, sample, slot_sems.at[slots]))
    for copy in reversed(fetches):
        copy.start()
    weights = [
        pltpu.make_async_copy(src, dst, weight_sems.at[i])
        for i, (src, dst) in enumerate(
            ((w_qkv_ref, w_qkv), (w_out_ref, w_out), (w_dec_ref, w_dec))
        )
    ]
    def send(k, h, at, src, device):
        return pltpu.make_async_remote_copy(
            src_ref=src.at[at],
            dst_ref=far.at[k, at],
            send_sem=send_sems.at[k, h],
            recv_sem=recv_sems.at[k, h],
            device_id=device,
            device_id_type=MESH,
        )

    def send_half(k, h):
        return send(k, h, part(h), own_a if k == UNIT_A else own.at[UNIT_C], partner)

    def send_piece(q):
        return send(UNIT_B, q, part(q), own.at[UNIT_B], partner)

    def arrival(k, h):
        return send(k, h, part(h), far.at[k], partner)

    def forward(h):
        return send(UNIT_D, h, part(h), relay, peer)

    def relay_half(h):
        return pltpu.make_async_remote_copy(
            src_ref=own.at[UNIT_D, part(h)],
            dst_ref=relay.at[part(h)],
            send_sem=relay_send_sems.at[h],
            recv_sem=relay_recv_sems.at[h],
            device_id=across,
            device_id_type=MESH,
        )

    def embed(k, values):
        flat = values.reshape(tokens, patch_len)
        embedded[k], own[k] = embed_slot(flat, w_embed[...], a_gain_ref[...])

    pl.semaphore_wait(barrier, 2 if relayed else 1)
    @pl.when(near)
    def _():
        for h in range(2):
            send_half(UNIT_A, h).start()

    if relayed:

        @pl.when(heavy)
        def _():
            embed(UNIT_D, grabbed[1])
            for h in range(2):
                relay_half(h).start()

    @pl.when(jnp.logical_not(near))
    def _():
        for h in range(2):
            send_half(UNIT_A, h).start()

    embedded[UNIT_A] = embedded_a[...]
    own[UNIT_A] = own_a[...]
    q_regions, k_regions = region_tables(
        region_ref[pl.ds(mine * HALF, HALF), :].astype(jnp.float32),
        region_ref[pl.ds(other * HALF, HALF), :].astype(jnp.float32),
    )
    q_table[...] = q_regions
    k_table[...] = k_regions
    each = windows // 2
    for q in range(2):
        q_parts[q] = q_regions[each * q : each * (q + 1)]
        k_parts[q] = k_regions[:, each * q : each * (q + 1)]
    for copy in fetches:
        copy.wait()
    for copy in weights:
        copy.start()
    order, _ = slot_order(sample, slots)

    @pl.when(heavy)
    def _():
        embed(UNIT_C, patches[order[UNIT_C]])

        @pl.when(near)
        def _():
            for h in range(2):
                send_half(UNIT_C, h).start()

    embed(UNIT_B, patches[order[UNIT_B]])

    if not relayed:

        @pl.when(near)
        def _():
            for q in range(2):
                send_piece(q).start()

    @pl.when(jnp.logical_and(heavy, jnp.logical_not(near)))
    def _():
        for h in range(2):
            send_half(UNIT_C, h).start()

    @pl.loop(0, rows_here)
    def _(i):
        result[UNIT_B, i] = patches[order[UNIT_B], i]
        if not relayed:
            result[UNIT_D, i] = patches[order[UNIT_D], i]

    weights[0].wait()

    def project(k):
        query = jnp.dot(own[k], w_qkv[:, :D], preferred_element_type=jnp.float32)
        own_qkv[k, :, :D] = (query * (1.0 / math.sqrt(HDIM))).astype(jnp.bfloat16)
        own_qkv[k, :, D:] = jnp.dot(
            own[k], w_qkv[:, D:], preferred_element_type=jnp.float32
        ).astype(jnp.bfloat16)

    @pl.loop(0, jnp.where(heavy, 4, 2) if relayed else 3)
    def _(i):
        project(jnp.where(i == 0, UNIT_A, jnp.where(i == 1, UNIT_B, i - 1)))

    if relayed:

        @pl.when(jnp.logical_and(heavy, jnp.logical_not(near)))
        def _():
            for q in range(2):
                send_piece(q).start()

        @pl.when(jnp.logical_not(heavy))
        def _():
            for h in range(2):
                relay_half(h).wait_recv()
                forward(h).start()
            for q in range(2):
                send_piece(q).start()

            @pl.loop(0, rows_here)
            def _(i):
                for k in (UNIT_C, UNIT_D):
                    result[k, i] = patches[order[k], i]

    weights[1].wait()
    weights[2].wait()

    def mix(k, at, q_regions, k_regions):
        kv_other = jnp.dot(far[k, at], w_qkv[:, D:], preferred_element_type=jnp.float32)
        mixed = attend_slot(
            own_qkv[k, at, :D],
            own_qkv[k, at, D:],
            kv_other.astype(jnp.bfloat16),
            q_regions,
            k_regions,
        )
        return finish_part(embedded[k, at], mixed, w_out[...], o_gain_ref[...])

    wholes = UNIT_B if relayed else UNIT_D

    @pl.loop(0, wholes + 2)
    def _(step):
        k = step
        if relayed:
            k = jnp.where(step == UNIT_D, wholes, jnp.where(step == wholes, UNIT_D, step))

        @pl.when(jnp.logical_and(k < wholes, jnp.logical_or(heavy, k == UNIT_A)))
        def _():
            for h in range(2):
                arrival(k, h).wait_recv()

            mixed = mix(k, pl.ds(0, tokens), q_table[...], k_table[...])
            final = from_windows(mixed).astype(jnp.bfloat16)
            place = jnp.where(
                k == UNIT_A, order[UNIT_A], jnp.where(k == UNIT_C, order[UNIT_C], order[UNIT_D])
            )
            flat = patches[place].reshape(tokens, patch_len)
            result[k] = decode_slot(flat, final, w_dec[...]).reshape(rows_here, cols, patch_len)

            turn = jnp.logical_and(near, heavy) if relayed else jnp.logical_not(near)

            @pl.when(jnp.logical_and(k == UNIT_A, turn))
            def _():
                for q in range(2):
                    send_piece(q).start()

        @pl.when(k >= wholes)
        def _():
            q = k - wholes
            send_piece(q).wait_recv()
            finals[part(q)] = mix(UNIT_B, part(q), q_parts[q], k_parts[q])

    for h in range(2):
        send_half(UNIT_A, h).wait_send()
        send_piece(h).wait_send()

    @pl.when(heavy)
    def _():
        for h in range(2):
            send_half(UNIT_C, h).wait_send()
            if relayed:
                relay_half(h).wait_send()

    if relayed:

        @pl.when(jnp.logical_not(heavy))
        def _():
            for h in range(2):
                forward(h).wait_send()


def last_kernel(sample_ref, result, w_dec, finals, new_ref, decoded, sems, row_sems):
    slots, rows_here, cols, patch_len = result.shape
    samples = sample_ref[...]
    order, _ = slot_order([samples[0, b] for b in range(samples.shape[1])], slots)
    copies = [
        pltpu.make_async_copy(result.at[k], new_ref.at[order[k]], sems.at[k])
        for k in (UNIT_A, UNIT_C, UNIT_D)
    ]
    for copy in copies:
        copy.start()
    half = rows_here * cols // 2
    final = from_windows(finals[...]).astype(jnp.bfloat16)
    rows = rows_here // 2
    for h in range(2):
        here = slice(rows * h, rows * (h + 1))
        decoded[here] = decode_slot(
            result[UNIT_B, here].reshape(half, patch_len),
            final[half * h : half * (h + 1)],
            w_dec[...],
        ).reshape(rows, cols, patch_len)
        copies.append(
            pltpu.make_async_copy(
                decoded.at[here], new_ref.at[order[UNIT_B], here], row_sems.at[h]
            )
        )
        copies[-1].start()
    for copy in copies:
        copy.wait()


def local_strips(
    store, sample_index, region_ids, w_embed, attn_gain, w_qkv, w_out, out_gain, w_dec
):
    slots, rows_here, cols, patch_len = store.shape
    tokens = rows_here * cols
    windows = tokens // PER
    held = lambda *shape: pltpu.VMEM(shape, jnp.bfloat16)
    wide = lambda *shape: pltpu.VMEM(shape, jnp.float32)
    vmem = pl.BlockSpec(memory_space=pltpu.VMEM)
    hbm = pl.BlockSpec(memory_space=pltpu.HBM)
    in_hbm = lambda array: pltpu.with_memory_space_constraint(array, pltpu.HBM)
    samples, sample_index, store = sample_index, in_hbm(sample_index), in_hbm(store)
    w_embed, w_qkv, w_out = in_hbm(w_embed), in_hbm(w_qkv), in_hbm(w_out)
    w_dec_t = in_hbm(w_dec.T)
    *first, branch = pl.pallas_call(
        first_kernel,
        in_specs=[hbm] * 4,
        out_specs=[vmem] * 4 + [pl.BlockSpec(memory_space=pltpu.SMEM)],
        out_shape=[
            held(*w_embed.shape),
            held(2, *store.shape[1:]),
            held(tokens, D),
            held(tokens, D),
            pltpu.SMEM((1,), jnp.int32),
        ],
        scratch_shapes=[
            pltpu.SMEM(sample_index.shape, jnp.int32),
            wide(1, D),
            pltpu.SemaphoreType.DMA((5,)),
        ],
        compiler_params=pltpu.CompilerParams(vmem_limit_bytes=FIRST_LIMIT),
    )(sample_index, in_hbm(attn_gain[None]), store, w_embed)
    def exchange_and_place(heavy_owner, *first):
        carried = pl.pallas_call(
            functools.partial(exchange_kernel, heavy_owner),
            in_specs=[hbm] + [vmem] * 7 + [hbm] * 4,
            out_specs=[vmem] * 3,
            out_shape=[
                held(*store.shape),
                held(*w_dec_t.shape),
                wide(tokens, D),
            ],
            scratch_shapes=[
                pltpu.SMEM(sample_index.shape, jnp.int32),
                held(*w_qkv.shape),
                held(*w_out.shape),
                wide(windows, GROUP * PER),
                wide(2 * PER, windows),
                wide(2, windows // 2, GROUP * PER),
                wide(2, 2 * PER, windows // 2),
                held(*store.shape),
                held(slots, tokens, D),
                held(slots, tokens, D),
                held(tokens, D),
                held(slots, tokens, D),
                held(slots, tokens, 3 * D),
                pltpu.SemaphoreType.DMA((slots + 1,)),
                pltpu.SemaphoreType.DMA((3,)),
                pltpu.SemaphoreType.DMA((2,)),
                pltpu.SemaphoreType.DMA((2,)),
                pltpu.SemaphoreType.DMA((slots, 2)),
                pltpu.SemaphoreType.DMA((slots, 2)),
            ],
            compiler_params=pltpu.CompilerParams(
                vmem_limit_bytes=VMEM_LIMIT,
                collective_id=0 if heavy_owner is None else 1 + heavy_owner,
                has_side_effects=True,
            ),
        )(
            sample_index,
            region_ids,
            attn_gain[None],
            out_gain[None],
            *first,
            store,
            w_qkv,
            w_out,
            w_dec_t,
        )
        return pl.pallas_call(
            last_kernel,
            in_specs=[vmem] * 4,
            out_specs=hbm,
            out_shape=pltpu.HBM(store.shape, store.dtype),
            scratch_shapes=[
                held(*store.shape[1:]),
                pltpu.SemaphoreType.DMA((slots,)),
                pltpu.SemaphoreType.DMA((2,)),
            ],
            compiler_params=pltpu.CompilerParams(vmem_limit_bytes=LAST_LIMIT),
        )(samples[None], *carried)

    branches = [functools.partial(exchange_and_place, owner) for owner in (None, 0, 1)]
    return lax.switch(branch[0], branches, *first)


def local(store, sample_index, *rest):
    slots, rows_here = store.shape[:2]
    strips = (
        rows_here == HALF
        and slots == 4
        and lax.axis_size("buf") == 2
        and sample_index.shape[0] == 6
    )
    return (local_strips if strips else local_tiles)(store, sample_index, *rest)


def solution(mesh):
    return jax.shard_map(
        local,
        mesh=mesh,
        in_specs=(P("buf", ("lat", "lon"), None, None), P(), P(), P(), P(), P(), P(), P(), P()),
        out_specs=P("buf", ("lat", "lon"), None, None),
        check_vma=False,
    )
```

```python
import functools
import math

import jax
import jax.numpy as jnp
from jax import lax
from jax.experimental import pallas as pl
from jax.experimental.pallas import tpu as pltpu
from jax.sharding import PartitionSpec as P

D = 512
HEADS = 8
HDIM = 64
WIN = 8
HALF = WIN // 2
VMEM_LIMIT = 40 * 1024 * 1024
LAST_LIMIT = 40 * 1024 * 1024
FIRST_LIMIT = 56 * 1024 * 1024


def with_halo(array, sides, width):
    for axis, dim in sides:
        devices, length = (lax.axis_size(axis), array.shape[dim])
        up = [(i, (i + 1) % devices) for i in range(devices)]
        down = [(j, i) for i, j in up]
        last = lax.slice_in_dim(array, length - width, length, axis=dim)
        leading = lax.slice_in_dim(array, 0, width, axis=dim)
        before = lax.ppermute(last, axis, up)
        after = lax.ppermute(leading, axis, down)
        array = jnp.concatenate([before, array, after], axis=dim)
    return array


def layer_norm(values, gain_row):
    center = jnp.mean(values, axis=-1, keepdims=True)
    spread = jnp.mean(jnp.square(values - center), axis=-1, keepdims=True)
    return (values - center) * lax.rsqrt(spread + 1e-05) * gain_row


def window_mix(windows, regions):
    scores = jnp.einsum(
        "bwqhd,bwkhd->bwhqk",
        windows[:, :, :, 0],
        windows[:, :, :, 1],
        preferred_element_type=jnp.float32,
    ) / math.sqrt(HDIM)
    visible = (regions[:, :, None] == regions[:, None, :])[None, :, None]
    scores = jnp.where(visible, scores, -1e30)
    highest = jnp.max(scores, axis=-1, keepdims=True)
    expo_terms = jnp.where(visible, jnp.exp(scores - highest), 0.0)
    weights = (expo_terms / jnp.sum(expo_terms, axis=-1, keepdims=True)).astype(jnp.bfloat16)
    return jnp.einsum(
        "bwhqk,bwkhd->bwqhd", weights, windows[:, :, :, 2], preferred_element_type=jnp.float32
    ).astype(jnp.bfloat16)


def local_tiles(store, sample_index, region_ids, w_embed, attn_gain, w_qkv, w_out, out_gain, w_dec):
    lon_count = lax.axis_size("lon")
    slots_here, rows_here, width_all, patch_len = store.shape
    patch_cols = width_all // lon_count
    patch_rows = rows_here * lon_count
    half_win = WIN // 2
    ext_rows = patch_rows + WIN
    ext_cols = patch_cols + WIN
    own_slots = lax.axis_index("buf") * slots_here + jnp.arange(slots_here, dtype=jnp.int32)
    matches = own_slots[:, None] == sample_index[None, :]
    occupied = jnp.any(matches, axis=1)
    local_rows = store.reshape(slots_here, 1, rows_here, lon_count, patch_cols, patch_len)
    tile_data = lax.all_to_all(local_rows, "lon", split_axis=3, concat_axis=1, tiled=True)
    patches = tile_data.reshape(-1, patch_len)
    embedded = jnp.dot(patches, w_embed, preferred_element_type=jnp.float32).astype(jnp.bfloat16)
    normed = layer_norm(embedded.astype(jnp.float32), attn_gain).astype(jnp.bfloat16)
    normed = normed.reshape(slots_here, patch_rows, patch_cols, D)
    widened = with_halo(normed, (("lat", 1), ("lon", 2)), half_win)
    projected = jnp.dot(widened.reshape(-1, D), w_qkv, preferred_element_type=jnp.float32).astype(
        jnp.bfloat16
    )
    windows = projected.reshape(
        slots_here, ext_rows // WIN, WIN, ext_cols // WIN, WIN, 3, HEADS, HDIM
    )
    windows = windows.transpose(0, 1, 3, 2, 4, 5, 6, 7).reshape(
        slots_here, -1, WIN * WIN, 3, HEADS, HDIM
    )
    total_rows, total_cols = region_ids.shape
    row_pick = (
        lax.axis_index("lat") * patch_rows - half_win + jnp.arange(ext_rows, dtype=jnp.int32)
    ) % total_rows
    col_pick = (
        lax.axis_index("lon") * patch_cols - half_win + jnp.arange(ext_cols, dtype=jnp.int32)
    ) % total_cols
    local_regions = jnp.take(jnp.take(region_ids, row_pick, axis=0), col_pick, axis=1)
    region_windows = (
        local_regions.reshape(ext_rows // WIN, WIN, ext_cols // WIN, WIN)
        .transpose(0, 2, 1, 3)
        .reshape(-1, WIN * WIN)
    )
    mixed_heads = window_mix(windows, region_windows)
    placed = mixed_heads.reshape(slots_here, ext_rows // WIN, ext_cols // WIN, WIN, WIN, D)
    placed = placed.transpose(0, 1, 3, 2, 4, 5).reshape(slots_here, ext_rows, ext_cols, D)
    placed = placed[:, half_win : half_win + patch_rows, half_win : half_win + patch_cols].reshape(
        -1, D
    )
    updated = embedded.astype(jnp.float32) + jnp.dot(
        placed, w_out, preferred_element_type=jnp.float32
    )
    final_norm = layer_norm(updated, out_gain).astype(jnp.bfloat16)
    predicted = (
        patches.astype(jnp.float32) + jnp.dot(final_norm, w_dec, preferred_element_type=jnp.float32)
    ).astype(jnp.bfloat16)
    outgoing = predicted.reshape(slots_here, lon_count, rows_here, 1, patch_cols, patch_len)
    returned = lax.all_to_all(outgoing, "lon", split_axis=1, concat_axis=3, tiled=True)
    strip_data = returned.reshape(slots_here, rows_here, width_all, patch_len)
    return jnp.where(occupied[:, None, None, None], strip_data, store)


def to_windows(values):
    rows, cols = HALF, values.shape[0] // HALF
    parts = [pltpu.roll(values[cols * i : cols * (i + 1)], cols - HALF, 0) for i in range(rows)]
    return jnp.concatenate(
        [parts[i][WIN * c : WIN * (c + 1)] for c in range(cols // WIN) for i in range(rows)], axis=0
    )


def from_windows(values):
    rows, cols = HALF, values.shape[0] // HALF
    parts = []
    for i in range(rows):
        line = jnp.concatenate(
            [
                values[WIN * (rows * c + i) : WIN * (rows * c + i + 1)]
                for c in range(cols // WIN)
            ],
            axis=0,
        )
        parts.append(pltpu.roll(line, HALF, 0))
    return jnp.concatenate(parts, axis=0)


def embed_slot(patches, w_embed, gain):
    embedded = jnp.dot(patches, w_embed, preferred_element_type=jnp.float32).astype(jnp.bfloat16)
    embedded = to_windows(embedded.astype(jnp.float32))
    normed = layer_norm(embedded, gain).astype(jnp.bfloat16)
    return embedded.astype(jnp.bfloat16), normed


NT = (((1,), (1,)), ((), ()))
TN = (((0,), (0,)), ((), ()))
GROUP = 4
WIDE = GROUP * HDIM
PER = WIN * HALF


def attend_slot(query, kv_own, kv_other, q_regions, k_regions):
    shape = (GROUP * PER, WIDE)
    pick = (
        lax.broadcasted_iota(jnp.int32, shape, 0) // PER
        == lax.broadcasted_iota(jnp.int32, shape, 1) // HDIM
    )
    head_mask = jnp.where(pick, 1.0, 0.0).astype(jnp.bfloat16)
    windows = query.shape[0] // PER
    kvs, scores, weights, mixed = [], [], [], []
    for c in range(windows):
        at = slice(PER * c, PER * (c + 1))
        kvs.append(jnp.concatenate([kv_own[at], kv_other[at]], axis=0))
        for g in range(HEADS // GROUP):
            cols = slice(WIDE * g, WIDE * (g + 1))
            queries = jnp.concatenate([query[at, cols]] * GROUP, axis=0) * head_mask
            scores.append(
                lax.dot_general(kvs[c][:, cols], queries, NT, preferred_element_type=jnp.float32)
            )
    for c in range(windows):
        seen = k_regions[:, c : c + 1] == q_regions[c : c + 1, :]
        for g in range(HEADS // GROUP):
            part = jnp.where(seen, scores[2 * c + g], -1e30)
            expo = jnp.exp(part - jnp.max(part, axis=0, keepdims=True))
            total = jnp.sum(expo, axis=0, keepdims=True)
            weights.append((expo * (1.0 / total)).astype(jnp.bfloat16))
    for c in range(windows):
        groups = []
        for g in range(HEADS // GROUP):
            heads = lax.dot_general(
                weights[2 * c + g],
                kvs[c][:, D + WIDE * g : D + WIDE * (g + 1)],
                TN,
                preferred_element_type=jnp.float32,
            )
            heads = jnp.where(pick, heads, 0.0)
            total = heads[:PER]
            for h in range(1, GROUP):
                total = total + heads[PER * h : PER * (h + 1)]
            groups.append(total)
        mixed.append(jnp.concatenate(groups, axis=1).astype(jnp.bfloat16))
    return jnp.concatenate(mixed, axis=0)


def region_tables(own, far):
    rows, cols = own.shape
    windows = cols // WIN
    lines = [own[i : i + 1] for i in range(rows)] + [far[i : i + 1] for i in range(rows)]
    wide = jnp.concatenate([jnp.broadcast_to(line, (WIN, cols)) for line in lines], axis=0)
    row = lax.broadcasted_iota(jnp.int32, wide.shape, 0)
    col = lax.broadcasted_iota(jnp.int32, wide.shape, 1)
    kept = jnp.where((col + WIN - HALF) % WIN == row % WIN, wide, 0.0).astype(jnp.bfloat16)
    place = (lax.broadcasted_iota(jnp.int32, (windows, cols), 1) + cols - HALF) % cols // WIN
    here = place == lax.broadcasted_iota(jnp.int32, (windows, cols), 0)
    here = jnp.where(here, 1.0, 0.0).astype(jnp.bfloat16)
    k_regions = lax.dot_general(kept, here, NT, preferred_element_type=jnp.float32)
    q_rows = jnp.concatenate([kept[:PER]] * GROUP, axis=0)
    q_regions = lax.dot_general(here, q_rows, NT, preferred_element_type=jnp.float32)
    return q_regions, k_regions


def finish_part(embedded, mixed, w_out, gain):
    updated = embedded.astype(jnp.float32) + jnp.dot(
        mixed, w_out, preferred_element_type=jnp.float32
    )
    return layer_norm(updated, gain)


def decode_slot(patches, final, w_dec_t):
    return (
        patches.astype(jnp.float32)
        + lax.dot_general(
            final, w_dec_t, (((1,), (1,)), ((), ())), preferred_element_type=jnp.float32
        )
    ).astype(jnp.bfloat16)


MESH = pl.DeviceIdType.MESH
UNIT_A, UNIT_C, UNIT_D, UNIT_B = range(4)


def slot_order(sample_ref, slots):
    first = lax.axis_index("buf") * slots
    taken = []
    samples = len(sample_ref) if isinstance(sample_ref, list) else sample_ref.shape[0]
    for s in range(slots):
        hit = sample_ref[0] == first + s
        for b in range(1, samples):
            hit = jnp.logical_or(hit, sample_ref[b] == first + s)
        taken.append(hit.astype(jnp.int32))
    count = sum(taken)
    places, before = [], jnp.int32(0)
    for s in range(slots):
        places.append(jnp.where(taken[s] == 1, before, count + s - before))
        before = before + taken[s]
    order = [
        sum(jnp.where(places[s] == j, jnp.int32(s), 0) for s in range(slots)) for j in range(slots)
    ]
    return [order[j] for j in (0, 2, 3, 1)], count


def first_kernel(
    sample_ref,
    gain_ref,
    store_ref,
    w_embed_ref,
    w_embed,
    grabbed,
    embedded,
    own,
    branch,
    sample,
    gain,
    sems,
):
    slots, rows_here, cols, patch_len = store_ref.shape
    weight = pltpu.make_async_copy(w_embed_ref, w_embed, sems.at[0])
    sample_in = pltpu.make_async_copy(sample_ref, sample, sems.at[3])
    gain_in = pltpu.make_async_copy(gain_ref, gain, sems.at[4])
    sample_in.start()
    weight.start()
    gain_in.start()
    sample_in.wait()
    order, count = slot_order(sample, slots)
    buf = lax.axis_index("buf")
    heavy = jnp.where(count == slots, buf, 1 - buf)
    branch[0] = jnp.where(2 * count == sample.shape[0], 0, 1 + heavy)
    fetch_a = pltpu.make_async_copy(store_ref.at[order[UNIT_A]], grabbed.at[0], sems.at[1])
    fetch_d = pltpu.make_async_copy(store_ref.at[order[UNIT_D]], grabbed.at[1], sems.at[2])
    fetch_a.start()
    gain_in.wait()
    weight.wait()
    fetch_d.start()
    fetch_a.wait()
    flat = grabbed[0].reshape(rows_here * cols, patch_len)
    embedded[...], own[...] = embed_slot(flat, w_embed[...], gain[...])
    fetch_d.wait()


def exchange_kernel(
    heavy_owner,
    sample_in,
    region_ref,
    a_gain_ref,
    o_gain_ref,
    w_embed,
    grabbed,
    embedded_a,
    own_a,
    store_ref,
    w_qkv_ref,
    w_out_ref,
    w_dec_ref,
    result,
    w_dec,
    finals,
    sample,
    w_qkv,
    w_out,
    q_table,
    k_table,
    q_parts,
    k_parts,
    patches,
    embedded,
    own,
    relay,
    far,
    own_qkv,
    slot_sems,
    weight_sems,
    relay_send_sems,
    relay_recv_sems,
    send_sems,
    recv_sems,
):
    slots, rows_here, cols, patch_len = store_ref.shape
    lon_count = lax.axis_size("lon")
    strips = lax.axis_size("lat") * lon_count
    mine = lax.axis_index("lat") * lon_count + lax.axis_index("lon")
    other = lax.rem(mine + 2 * lax.rem(mine, 2) - 1 + strips, strips)
    partner = {"lat": lax.div(other, lon_count), "lon": lax.rem(other, lon_count)}
    relayed = heavy_owner is not None
    buf = lax.axis_index("buf")
    heavy = buf == heavy_owner if relayed else buf >= 0
    peer = {"buf": 1 - buf}
    across = dict(partner, buf=1 - buf)
    apart = jnp.abs(lax.div(other, lon_count) - lax.axis_index("lat"))
    near = apart != 1 if heavy_owner is not None else apart == 0
    tokens = rows_here * cols
    half = tokens // 2
    windows = tokens // PER

    def part(h):
        return pl.ds(half * h if isinstance(h, int) else pl.multiple_of(half * h, half), half)

    barrier = pltpu.get_barrier_semaphore()
    pl.semaphore_signal(barrier, inc=1, device_id=partner, device_id_type=MESH)
    if relayed:
        sender = {
            "lat": jnp.where(heavy, lax.axis_index("lat"), partner["lat"]),
            "lon": jnp.where(heavy, lax.axis_index("lon"), partner["lon"]),
            "buf": 1 - buf,
        }
        pl.semaphore_signal(barrier, inc=1, device_id=sender, device_id_type=MESH)

    fetches = [
        pltpu.make_async_copy(store_ref.at[s], patches.at[s], slot_sems.at[s])
        for s in range(slots)
    ]
    fetches.append(pltpu.make_async_copy(sample_in, sample, slot_sems.at[slots]))
    for copy in reversed(fetches):
        copy.start()
    weights = [
        pltpu.make_async_copy(src, dst, weight_sems.at[i])
        for i, (src, dst) in enumerate(
            ((w_qkv_ref, w_qkv), (w_out_ref, w_out), (w_dec_ref, w_dec))
        )
    ]
    def send(k, h, at, src, device):
        return pltpu.make_async_remote_copy(
            src_ref=src.at[at],
            dst_ref=far.at[k, at],
            send_sem=send_sems.at[k, h],
            recv_sem=recv_sems.at[k, h],
            device_id=device,
            device_id_type=MESH,
        )

    def send_half(k, h):
        return send(k, h, part(h), own_a if k == UNIT_A else own.at[UNIT_C], partner)

    def send_piece(q):
        return send(UNIT_B, q, part(q), own.at[UNIT_B], partner)

    def arrival(k, h):
        return send(k, h, part(h), far.at[k], partner)

    def forward(h):
        return send(UNIT_D, h, part(h), relay, peer)

    def relay_half(h):
        return pltpu.make_async_remote_copy(
            src_ref=own.at[UNIT_D, part(h)],
            dst_ref=relay.at[part(h)],
            send_sem=relay_send_sems.at[h],
            recv_sem=relay_recv_sems.at[h],
            device_id=across,
            device_id_type=MESH,
        )

    def embed(k, values):
        flat = values.reshape(tokens, patch_len)
        embedded[k], own[k] = embed_slot(flat, w_embed[...], a_gain_ref[...])

    pl.semaphore_wait(barrier, 2 if relayed else 1)
    @pl.when(near)
    def _():
        for h in range(2):
            send_half(UNIT_A, h).start()

    if relayed:

        @pl.when(heavy)
        def _():
            embed(UNIT_D, grabbed[1])
            for h in range(2):
                relay_half(h).start()

    @pl.when(jnp.logical_not(near))
    def _():
        for h in range(2):
            send_half(UNIT_A, h).start()

    embedded[UNIT_A] = embedded_a[...]
    own[UNIT_A] = own_a[...]
    q_regions, k_regions = region_tables(
        region_ref[pl.ds(mine * HALF, HALF), :].astype(jnp.float32),
        region_ref[pl.ds(other * HALF, HALF), :].astype(jnp.float32),
    )
    q_table[...] = q_regions
    k_table[...] = k_regions
    each = windows // 2
    for q in range(2):
        q_parts[q] = q_regions[each * q : each * (q + 1)]
        k_parts[q] = k_regions[:, each * q : each * (q + 1)]
    for copy in fetches:
        copy.wait()
    for copy in weights:
        copy.start()
    order, _ = slot_order(sample, slots)

    @pl.when(heavy)
    def _():
        embed(UNIT_C, patches[order[UNIT_C]])

        @pl.when(near)
        def _():
            for h in range(2):
                send_half(UNIT_C, h).start()

    embed(UNIT_B, patches[order[UNIT_B]])

    if not relayed:

        @pl.when(near)
        def _():
            for q in range(2):
                send_piece(q).start()

    @pl.when(jnp.logical_and(heavy, jnp.logical_not(near)))
    def _():
        for h in range(2):
            send_half(UNIT_C, h).start()

    @pl.loop(0, rows_here)
    def _(i):
        result[UNIT_B, i] = patches[order[UNIT_B], i]
        if not relayed:
            result[UNIT_D, i] = patches[order[UNIT_D], i]

    weights[0].wait()

    def project(k):
        query = jnp.dot(own[k], w_qkv[:, :D], preferred_element_type=jnp.float32)
        own_qkv[k, :, :D] = (query * (1.0 / math.sqrt(HDIM))).astype(jnp.bfloat16)
        own_qkv[k, :, D:] = jnp.dot(
            own[k], w_qkv[:, D:], preferred_element_type=jnp.float32
        ).astype(jnp.bfloat16)

    @pl.loop(0, jnp.where(heavy, 4, 2) if relayed else 3)
    def _(i):
        project(jnp.where(i == 0, UNIT_A, jnp.where(i == 1, UNIT_B, i - 1)))

    if relayed:

        @pl.when(jnp.logical_and(heavy, jnp.logical_not(near)))
        def _():
            for q in range(2):
                send_piece(q).start()

        @pl.when(jnp.logical_not(heavy))
        def _():
            for h in range(2):
                relay_half(h).wait_recv()
                forward(h).start()
            for q in range(2):
                send_piece(q).start()

            @pl.loop(0, rows_here)
            def _(i):
                for k in (UNIT_C, UNIT_D):
                    result[k, i] = patches[order[k], i]

    weights[1].wait()
    weights[2].wait()

    def mix(k, at, q_regions, k_regions):
        kv_other = jnp.dot(far[k, at], w_qkv[:, D:], preferred_element_type=jnp.float32)
        mixed = attend_slot(
            own_qkv[k, at, :D],
            own_qkv[k, at, D:],
            kv_other.astype(jnp.bfloat16),
            q_regions,
            k_regions,
        )
        return finish_part(embedded[k, at], mixed, w_out[...], o_gain_ref[...])

    wholes = UNIT_B if relayed else UNIT_D

    @pl.loop(0, wholes + 2)
    def _(step):
        k = step
        if relayed:
            swapped = jnp.where(step == UNIT_D, wholes, jnp.where(step == wholes, UNIT_D, step))
            k = jnp.where(near, step, swapped)

        @pl.when(jnp.logical_and(k < wholes, jnp.logical_or(heavy, k == UNIT_A)))
        def _():
            for h in range(2):
                arrival(k, h).wait_recv()

            mixed = mix(k, pl.ds(0, tokens), q_table[...], k_table[...])
            final = from_windows(mixed).astype(jnp.bfloat16)
            place = jnp.where(
                k == UNIT_A, order[UNIT_A], jnp.where(k == UNIT_C, order[UNIT_C], order[UNIT_D])
            )
            flat = patches[place].reshape(tokens, patch_len)
            result[k] = decode_slot(flat, final, w_dec[...]).reshape(rows_here, cols, patch_len)

            turn = jnp.logical_and(near, heavy) if relayed else jnp.logical_not(near)

            @pl.when(jnp.logical_and(k == UNIT_A, turn))
            def _():
                for q in range(2):
                    send_piece(q).start()

        @pl.when(k >= wholes)
        def _():
            q = k - wholes
            send_piece(q).wait_recv()
            finals[part(q)] = mix(UNIT_B, part(q), q_parts[q], k_parts[q])

    for h in range(2):
        send_half(UNIT_A, h).wait_send()
        send_piece(h).wait_send()

    @pl.when(heavy)
    def _():
        for h in range(2):
            send_half(UNIT_C, h).wait_send()
            if relayed:
                relay_half(h).wait_send()

    if relayed:

        @pl.when(jnp.logical_not(heavy))
        def _():
            for h in range(2):
                forward(h).wait_send()


def last_kernel(sample_ref, result, w_dec, finals, new_ref, decoded, sems, row_sems):
    slots, rows_here, cols, patch_len = result.shape
    samples = sample_ref[...]
    order, _ = slot_order([samples[0, b] for b in range(samples.shape[1])], slots)
    copies = [
        pltpu.make_async_copy(result.at[k], new_ref.at[order[k]], sems.at[k])
        for k in (UNIT_A, UNIT_C, UNIT_D)
    ]
    for copy in copies:
        copy.start()
    half = rows_here * cols // 2
    final = from_windows(finals[...]).astype(jnp.bfloat16)
    rows = rows_here // 2
    for h in range(2):
        here = slice(rows * h, rows * (h + 1))
        decoded[here] = decode_slot(
            result[UNIT_B, here].reshape(half, patch_len),
            final[half * h : half * (h + 1)],
            w_dec[...],
        ).reshape(rows, cols, patch_len)
        copies.append(
            pltpu.make_async_copy(
                decoded.at[here], new_ref.at[order[UNIT_B], here], row_sems.at[h]
            )
        )
        copies[-1].start()
    for copy in copies:
        copy.wait()


def local_strips(
    store, sample_index, region_ids, w_embed, attn_gain, w_qkv, w_out, out_gain, w_dec
):
    slots, rows_here, cols, patch_len = store.shape
    tokens = rows_here * cols
    windows = tokens // PER
    held = lambda *shape: pltpu.VMEM(shape, jnp.bfloat16)
    wide = lambda *shape: pltpu.VMEM(shape, jnp.float32)
    vmem = pl.BlockSpec(memory_space=pltpu.VMEM)
    hbm = pl.BlockSpec(memory_space=pltpu.HBM)
    in_hbm = lambda array: pltpu.with_memory_space_constraint(array, pltpu.HBM)
    samples, sample_index, store = sample_index, in_hbm(sample_index), in_hbm(store)
    w_embed, w_qkv, w_out = in_hbm(w_embed), in_hbm(w_qkv), in_hbm(w_out)
    w_dec_t = in_hbm(w_dec.T)
    *first, branch = pl.pallas_call(
        first_kernel,
        in_specs=[hbm] * 4,
        out_specs=[vmem] * 4 + [pl.BlockSpec(memory_space=pltpu.SMEM)],
        out_shape=[
            held(*w_embed.shape),
            held(2, *store.shape[1:]),
            held(tokens, D),
            held(tokens, D),
            pltpu.SMEM((1,), jnp.int32),
        ],
        scratch_shapes=[
            pltpu.SMEM(sample_index.shape, jnp.int32),
            wide(1, D),
            pltpu.SemaphoreType.DMA((5,)),
        ],
        compiler_params=pltpu.CompilerParams(vmem_limit_bytes=FIRST_LIMIT),
    )(sample_index, in_hbm(attn_gain[None]), store, w_embed)
    def exchange_and_place(heavy_owner, *first):
        carried = pl.pallas_call(
            functools.partial(exchange_kernel, heavy_owner),
            in_specs=[hbm] + [vmem] * 7 + [hbm] * 4,
            out_specs=[vmem] * 3,
            out_shape=[
                held(*store.shape),
                held(*w_dec_t.shape),
                wide(tokens, D),
            ],
            scratch_shapes=[
                pltpu.SMEM(sample_index.shape, jnp.int32),
                held(*w_qkv.shape),
                held(*w_out.shape),
                wide(windows, GROUP * PER),
                wide(2 * PER, windows),
                wide(2, windows // 2, GROUP * PER),
                wide(2, 2 * PER, windows // 2),
                held(*store.shape),
                held(slots, tokens, D),
                held(slots, tokens, D),
                held(tokens, D),
                held(slots, tokens, D),
                held(slots, tokens, 3 * D),
                pltpu.SemaphoreType.DMA((slots + 1,)),
                pltpu.SemaphoreType.DMA((3,)),
                pltpu.SemaphoreType.DMA((2,)),
                pltpu.SemaphoreType.DMA((2,)),
                pltpu.SemaphoreType.DMA((slots, 2)),
                pltpu.SemaphoreType.DMA((slots, 2)),
            ],
            compiler_params=pltpu.CompilerParams(
                vmem_limit_bytes=VMEM_LIMIT,
                collective_id=0 if heavy_owner is None else 1 + heavy_owner,
                has_side_effects=True,
            ),
        )(
            sample_index,
            region_ids,
            attn_gain[None],
            out_gain[None],
            *first,
            store,
            w_qkv,
            w_out,
            w_dec_t,
        )
        return pl.pallas_call(
            last_kernel,
            in_specs=[vmem] * 4,
            out_specs=hbm,
            out_shape=pltpu.HBM(store.shape, store.dtype),
            scratch_shapes=[
                held(*store.shape[1:]),
                pltpu.SemaphoreType.DMA((slots,)),
                pltpu.SemaphoreType.DMA((2,)),
            ],
            compiler_params=pltpu.CompilerParams(vmem_limit_bytes=LAST_LIMIT),
        )(samples[None], *carried)

    branches = [functools.partial(exchange_and_place, owner) for owner in (None, 0, 1)]
    return lax.switch(branch[0], branches, *first)


def local(store, sample_index, *rest):
    slots, rows_here = store.shape[:2]
    strips = (
        rows_here == HALF
        and slots == 4
        and lax.axis_size("buf") == 2
        and sample_index.shape[0] == 6
    )
    return (local_strips if strips else local_tiles)(store, sample_index, *rest)


def solution(mesh):
    return jax.shard_map(
        local,
        mesh=mesh,
        in_specs=(P("buf", ("lat", "lon"), None, None), P(), P(), P(), P(), P(), P(), P(), P()),
        out_specs=P("buf", ("lat", "lon"), None, None),
        check_vma=False,
    )
```

```python
import functools
import math

import jax
import jax.numpy as jnp
from jax import lax
from jax.experimental import pallas as pl
from jax.experimental.pallas import tpu as pltpu
from jax.sharding import PartitionSpec as P

D = 512
HEADS = 8
HDIM = 64
WIN = 8
HALF = WIN // 2
VMEM_LIMIT = 40 * 1024 * 1024
LAST_LIMIT = 40 * 1024 * 1024
FIRST_LIMIT = 56 * 1024 * 1024


def with_halo(array, sides, width):
    for axis, dim in sides:
        devices, length = (lax.axis_size(axis), array.shape[dim])
        up = [(i, (i + 1) % devices) for i in range(devices)]
        down = [(j, i) for i, j in up]
        last = lax.slice_in_dim(array, length - width, length, axis=dim)
        leading = lax.slice_in_dim(array, 0, width, axis=dim)
        before = lax.ppermute(last, axis, up)
        after = lax.ppermute(leading, axis, down)
        array = jnp.concatenate([before, array, after], axis=dim)
    return array


def layer_norm(values, gain_row):
    center = jnp.mean(values, axis=-1, keepdims=True)
    spread = jnp.mean(jnp.square(values - center), axis=-1, keepdims=True)
    return (values - center) * lax.rsqrt(spread + 1e-05) * gain_row


def window_mix(windows, regions):
    scores = jnp.einsum(
        "bwqhd,bwkhd->bwhqk",
        windows[:, :, :, 0],
        windows[:, :, :, 1],
        preferred_element_type=jnp.float32,
    ) / math.sqrt(HDIM)
    visible = (regions[:, :, None] == regions[:, None, :])[None, :, None]
    scores = jnp.where(visible, scores, -1e30)
    highest = jnp.max(scores, axis=-1, keepdims=True)
    expo_terms = jnp.where(visible, jnp.exp(scores - highest), 0.0)
    weights = (expo_terms / jnp.sum(expo_terms, axis=-1, keepdims=True)).astype(jnp.bfloat16)
    return jnp.einsum(
        "bwhqk,bwkhd->bwqhd", weights, windows[:, :, :, 2], preferred_element_type=jnp.float32
    ).astype(jnp.bfloat16)


def local_tiles(store, sample_index, region_ids, w_embed, attn_gain, w_qkv, w_out, out_gain, w_dec):
    lon_count = lax.axis_size("lon")
    slots_here, rows_here, width_all, patch_len = store.shape
    patch_cols = width_all // lon_count
    patch_rows = rows_here * lon_count
    half_win = WIN // 2
    ext_rows = patch_rows + WIN
    ext_cols = patch_cols + WIN
    own_slots = lax.axis_index("buf") * slots_here + jnp.arange(slots_here, dtype=jnp.int32)
    matches = own_slots[:, None] == sample_index[None, :]
    occupied = jnp.any(matches, axis=1)
    local_rows = store.reshape(slots_here, 1, rows_here, lon_count, patch_cols, patch_len)
    tile_data = lax.all_to_all(local_rows, "lon", split_axis=3, concat_axis=1, tiled=True)
    patches = tile_data.reshape(-1, patch_len)
    embedded = jnp.dot(patches, w_embed, preferred_element_type=jnp.float32).astype(jnp.bfloat16)
    normed = layer_norm(embedded.astype(jnp.float32), attn_gain).astype(jnp.bfloat16)
    normed = normed.reshape(slots_here, patch_rows, patch_cols, D)
    widened = with_halo(normed, (("lat", 1), ("lon", 2)), half_win)
    projected = jnp.dot(widened.reshape(-1, D), w_qkv, preferred_element_type=jnp.float32).astype(
        jnp.bfloat16
    )
    windows = projected.reshape(
        slots_here, ext_rows // WIN, WIN, ext_cols // WIN, WIN, 3, HEADS, HDIM
    )
    windows = windows.transpose(0, 1, 3, 2, 4, 5, 6, 7).reshape(
        slots_here, -1, WIN * WIN, 3, HEADS, HDIM
    )
    total_rows, total_cols = region_ids.shape
    row_pick = (
        lax.axis_index("lat") * patch_rows - half_win + jnp.arange(ext_rows, dtype=jnp.int32)
    ) % total_rows
    col_pick = (
        lax.axis_index("lon") * patch_cols - half_win + jnp.arange(ext_cols, dtype=jnp.int32)
    ) % total_cols
    local_regions = jnp.take(jnp.take(region_ids, row_pick, axis=0), col_pick, axis=1)
    region_windows = (
        local_regions.reshape(ext_rows // WIN, WIN, ext_cols // WIN, WIN)
        .transpose(0, 2, 1, 3)
        .reshape(-1, WIN * WIN)
    )
    mixed_heads = window_mix(windows, region_windows)
    placed = mixed_heads.reshape(slots_here, ext_rows // WIN, ext_cols // WIN, WIN, WIN, D)
    placed = placed.transpose(0, 1, 3, 2, 4, 5).reshape(slots_here, ext_rows, ext_cols, D)
    placed = placed[:, half_win : half_win + patch_rows, half_win : half_win + patch_cols].reshape(
        -1, D
    )
    updated = embedded.astype(jnp.float32) + jnp.dot(
        placed, w_out, preferred_element_type=jnp.float32
    )
    final_norm = layer_norm(updated, out_gain).astype(jnp.bfloat16)
    predicted = (
        patches.astype(jnp.float32) + jnp.dot(final_norm, w_dec, preferred_element_type=jnp.float32)
    ).astype(jnp.bfloat16)
    outgoing = predicted.reshape(slots_here, lon_count, rows_here, 1, patch_cols, patch_len)
    returned = lax.all_to_all(outgoing, "lon", split_axis=1, concat_axis=3, tiled=True)
    strip_data = returned.reshape(slots_here, rows_here, width_all, patch_len)
    return jnp.where(occupied[:, None, None, None], strip_data, store)


def to_windows(values):
    rows, cols = HALF, values.shape[0] // HALF
    parts = [pltpu.roll(values[cols * i : cols * (i + 1)], cols - HALF, 0) for i in range(rows)]
    return jnp.concatenate(
        [parts[i][WIN * c : WIN * (c + 1)] for c in range(cols // WIN) for i in range(rows)], axis=0
    )


def from_windows(values):
    rows, cols = HALF, values.shape[0] // HALF
    parts = []
    for i in range(rows):
        line = jnp.concatenate(
            [
                values[WIN * (rows * c + i) : WIN * (rows * c + i + 1)]
                for c in range(cols // WIN)
            ],
            axis=0,
        )
        parts.append(pltpu.roll(line, HALF, 0))
    return jnp.concatenate(parts, axis=0)


def embed_slot(patches, w_embed, gain):
    embedded = jnp.dot(patches, w_embed, preferred_element_type=jnp.float32).astype(jnp.bfloat16)
    embedded = to_windows(embedded.astype(jnp.float32))
    normed = layer_norm(embedded, gain).astype(jnp.bfloat16)
    return embedded.astype(jnp.bfloat16), normed


NT = (((1,), (1,)), ((), ()))
TN = (((0,), (0,)), ((), ()))
GROUP = 4
WIDE = GROUP * HDIM
PER = WIN * HALF


def attend_slot(query, kv_own, kv_other, q_regions, k_regions):
    shape = (GROUP * PER, WIDE)
    pick = (
        lax.broadcasted_iota(jnp.int32, shape, 0) // PER
        == lax.broadcasted_iota(jnp.int32, shape, 1) // HDIM
    )
    head_mask = jnp.where(pick, 1.0, 0.0).astype(jnp.bfloat16)
    windows = query.shape[0] // PER
    kvs, scores, weights, mixed = [], [], [], []
    for c in range(windows):
        at = slice(PER * c, PER * (c + 1))
        kvs.append(jnp.concatenate([kv_own[at], kv_other[at]], axis=0))
        for g in range(HEADS // GROUP):
            cols = slice(WIDE * g, WIDE * (g + 1))
            queries = jnp.concatenate([query[at, cols]] * GROUP, axis=0) * head_mask
            scores.append(
                lax.dot_general(kvs[c][:, cols], queries, NT, preferred_element_type=jnp.float32)
            )
    for c in range(windows):
        seen = k_regions[:, c : c + 1] == q_regions[c : c + 1, :]
        for g in range(HEADS // GROUP):
            part = jnp.where(seen, scores[2 * c + g], -1e30)
            expo = jnp.exp(part - jnp.max(part, axis=0, keepdims=True))
            total = jnp.sum(expo, axis=0, keepdims=True)
            weights.append((expo * (1.0 / total)).astype(jnp.bfloat16))
    for c in range(windows):
        groups = []
        for g in range(HEADS // GROUP):
            heads = lax.dot_general(
                weights[2 * c + g],
                kvs[c][:, D + WIDE * g : D + WIDE * (g + 1)],
                TN,
                preferred_element_type=jnp.float32,
            )
            heads = jnp.where(pick, heads, 0.0)
            total = heads[:PER]
            for h in range(1, GROUP):
                total = total + heads[PER * h : PER * (h + 1)]
            groups.append(total)
        mixed.append(jnp.concatenate(groups, axis=1).astype(jnp.bfloat16))
    return jnp.concatenate(mixed, axis=0)


def region_tables(own, far):
    rows, cols = own.shape
    windows = cols // WIN
    lines = [own[i : i + 1] for i in range(rows)] + [far[i : i + 1] for i in range(rows)]
    wide = jnp.concatenate([jnp.broadcast_to(line, (WIN, cols)) for line in lines], axis=0)
    row = lax.broadcasted_iota(jnp.int32, wide.shape, 0)
    col = lax.broadcasted_iota(jnp.int32, wide.shape, 1)
    kept = jnp.where((col + WIN - HALF) % WIN == row % WIN, wide, 0.0).astype(jnp.bfloat16)
    place = (lax.broadcasted_iota(jnp.int32, (windows, cols), 1) + cols - HALF) % cols // WIN
    here = place == lax.broadcasted_iota(jnp.int32, (windows, cols), 0)
    here = jnp.where(here, 1.0, 0.0).astype(jnp.bfloat16)
    k_regions = lax.dot_general(kept, here, NT, preferred_element_type=jnp.float32)
    q_rows = jnp.concatenate([kept[:PER]] * GROUP, axis=0)
    q_regions = lax.dot_general(here, q_rows, NT, preferred_element_type=jnp.float32)
    return q_regions, k_regions


def finish_part(embedded, mixed, w_out, gain):
    updated = embedded.astype(jnp.float32) + jnp.dot(
        mixed, w_out, preferred_element_type=jnp.float32
    )
    return layer_norm(updated, gain)


def decode_slot(patches, final, w_dec_t):
    return (
        patches.astype(jnp.float32)
        + lax.dot_general(
            final, w_dec_t, (((1,), (1,)), ((), ())), preferred_element_type=jnp.float32
        )
    ).astype(jnp.bfloat16)


MESH = pl.DeviceIdType.MESH
UNIT_A, UNIT_C, UNIT_D, UNIT_B = range(4)


def slot_order(sample_ref, slots):
    first = lax.axis_index("buf") * slots
    taken = []
    samples = len(sample_ref) if isinstance(sample_ref, list) else sample_ref.shape[0]
    for s in range(slots):
        hit = sample_ref[0] == first + s
        for b in range(1, samples):
            hit = jnp.logical_or(hit, sample_ref[b] == first + s)
        taken.append(hit.astype(jnp.int32))
    count = sum(taken)
    places, before = [], jnp.int32(0)
    for s in range(slots):
        places.append(jnp.where(taken[s] == 1, before, count + s - before))
        before = before + taken[s]
    order = [
        sum(jnp.where(places[s] == j, jnp.int32(s), 0) for s in range(slots)) for j in range(slots)
    ]
    return [order[j] for j in (0, 2, 3, 1)], count


def first_kernel(
    sample_ref,
    gain_ref,
    store_ref,
    w_embed_ref,
    w_embed,
    grabbed,
    embedded,
    own,
    branch,
    sample,
    gain,
    sems,
):
    slots, rows_here, cols, patch_len = store_ref.shape
    weight = pltpu.make_async_copy(w_embed_ref, w_embed, sems.at[0])
    sample_in = pltpu.make_async_copy(sample_ref, sample, sems.at[3])
    gain_in = pltpu.make_async_copy(gain_ref, gain, sems.at[4])
    sample_in.start()
    weight.start()
    gain_in.start()
    sample_in.wait()
    order, count = slot_order(sample, slots)
    buf = lax.axis_index("buf")
    heavy = jnp.where(count == slots, buf, 1 - buf)
    branch[0] = jnp.where(2 * count == sample.shape[0], 0, 1 + heavy)
    fetch_a = pltpu.make_async_copy(store_ref.at[order[UNIT_A]], grabbed.at[0], sems.at[1])
    fetch_d = pltpu.make_async_copy(store_ref.at[order[UNIT_D]], grabbed.at[1], sems.at[2])
    fetch_a.start()
    gain_in.wait()
    weight.wait()
    fetch_d.start()
    fetch_a.wait()
    flat = grabbed[0].reshape(rows_here * cols, patch_len)
    embedded[...], own[...] = embed_slot(flat, w_embed[...], gain[...])
    fetch_d.wait()


def exchange_kernel(
    heavy_owner,
    sample_in,
    region_ref,
    a_gain_ref,
    o_gain_ref,
    w_embed,
    grabbed,
    embedded_a,
    own_a,
    store_ref,
    w_qkv_ref,
    w_out_ref,
    w_dec_ref,
    result,
    w_dec,
    finals,
    sample,
    w_qkv,
    w_out,
    q_table,
    k_table,
    q_parts,
    k_parts,
    patches,
    embedded,
    own,
    relay,
    far,
    own_qkv,
    slot_sems,
    weight_sems,
    relay_send_sems,
    relay_recv_sems,
    send_sems,
    recv_sems,
):
    slots, rows_here, cols, patch_len = store_ref.shape
    lon_count = lax.axis_size("lon")
    strips = lax.axis_size("lat") * lon_count
    mine = lax.axis_index("lat") * lon_count + lax.axis_index("lon")
    other = lax.rem(mine + 2 * lax.rem(mine, 2) - 1 + strips, strips)
    partner = {"lat": lax.div(other, lon_count), "lon": lax.rem(other, lon_count)}
    relayed = heavy_owner is not None
    buf = lax.axis_index("buf")
    heavy = buf == heavy_owner if relayed else buf >= 0
    peer = {"buf": 1 - buf}
    across = dict(partner, buf=1 - buf)
    apart = jnp.abs(lax.div(other, lon_count) - lax.axis_index("lat"))
    near = apart != 1 if heavy_owner is not None else apart == 0
    tokens = rows_here * cols
    half = tokens // 2
    windows = tokens // PER

    def part(h):
        return pl.ds(half * h if isinstance(h, int) else pl.multiple_of(half * h, half), half)

    barrier = pltpu.get_barrier_semaphore()
    pl.semaphore_signal(barrier, inc=1, device_id=partner, device_id_type=MESH)
    if relayed:
        sender = {
            "lat": jnp.where(heavy, lax.axis_index("lat"), partner["lat"]),
            "lon": jnp.where(heavy, lax.axis_index("lon"), partner["lon"]),
            "buf": 1 - buf,
        }
        pl.semaphore_signal(barrier, inc=1, device_id=sender, device_id_type=MESH)

    fetches = [
        pltpu.make_async_copy(store_ref.at[s], patches.at[s], slot_sems.at[s])
        for s in range(slots)
    ]
    fetches.append(pltpu.make_async_copy(sample_in, sample, slot_sems.at[slots]))
    for copy in reversed(fetches):
        copy.start()
    weights = [
        pltpu.make_async_copy(src, dst, weight_sems.at[i])
        for i, (src, dst) in enumerate(
            ((w_qkv_ref, w_qkv), (w_out_ref, w_out), (w_dec_ref, w_dec))
        )
    ]
    def send(k, h, at, src, device):
        return pltpu.make_async_remote_copy(
            src_ref=src.at[at],
            dst_ref=far.at[k, at],
            send_sem=send_sems.at[k, h],
            recv_sem=recv_sems.at[k, h],
            device_id=device,
            device_id_type=MESH,
        )

    def send_half(k, h):
        return send(k, h, part(h), own_a if k == UNIT_A else own.at[UNIT_C], partner)

    def send_piece(q):
        return send(UNIT_B, q, part(q), own.at[UNIT_B], partner)

    def arrival(k, h):
        return send(k, h, part(h), far.at[k], partner)

    def forward(h):
        return send(UNIT_D, h, part(h), relay, peer)

    def relay_half(h):
        return pltpu.make_async_remote_copy(
            src_ref=own.at[UNIT_D, part(h)],
            dst_ref=relay.at[part(h)],
            send_sem=relay_send_sems.at[h],
            recv_sem=relay_recv_sems.at[h],
            device_id=across,
            device_id_type=MESH,
        )

    def embed(k, values):
        flat = values.reshape(tokens, patch_len)
        embedded[k], own[k] = embed_slot(flat, w_embed[...], a_gain_ref[...])

    pl.semaphore_wait(barrier, 2 if relayed else 1)
    @pl.when(near)
    def _():
        for h in range(2):
            send_half(UNIT_A, h).start()

    if relayed:

        @pl.when(heavy)
        def _():
            embed(UNIT_D, grabbed[1])
            for h in range(2):
                relay_half(h).start()

    @pl.when(jnp.logical_not(near))
    def _():
        for h in range(2):
            send_half(UNIT_A, h).start()

    embedded[UNIT_A] = embedded_a[...]
    own[UNIT_A] = own_a[...]
    q_regions, k_regions = region_tables(
        region_ref[pl.ds(mine * HALF, HALF), :].astype(jnp.float32),
        region_ref[pl.ds(other * HALF, HALF), :].astype(jnp.float32),
    )
    q_table[...] = q_regions
    k_table[...] = k_regions
    each = windows // 2
    for q in range(2):
        q_parts[q] = q_regions[each * q : each * (q + 1)]
        k_parts[q] = k_regions[:, each * q : each * (q + 1)]
    for copy in fetches:
        copy.wait()
    for copy in weights:
        copy.start()
    order, _ = slot_order(sample, slots)

    @pl.loop(0, 2)
    def _(i):
        k = jnp.where(i == 0, UNIT_C, UNIT_B)

        @pl.when(jnp.logical_or(heavy, k == UNIT_B))
        def _():
            embed(k, patches[jnp.where(i == 0, order[UNIT_C], order[UNIT_B])])

        @pl.when(jnp.logical_and(i == 0, jnp.logical_and(near, heavy)))
        def _():
            for h in range(2):
                send_half(UNIT_C, h).start()


    if not relayed:

        @pl.when(near)
        def _():
            for q in range(2):
                send_piece(q).start()

    @pl.when(jnp.logical_and(heavy, jnp.logical_not(near)))
    def _():
        for h in range(2):
            send_half(UNIT_C, h).start()

    @pl.loop(0, rows_here)
    def _(i):
        result[UNIT_B, i] = patches[order[UNIT_B], i]
        if not relayed:
            result[UNIT_D, i] = patches[order[UNIT_D], i]

    weights[0].wait()

    def project(k):
        query = jnp.dot(own[k], w_qkv[:, :D], preferred_element_type=jnp.float32)
        own_qkv[k, :, :D] = (query * (1.0 / math.sqrt(HDIM))).astype(jnp.bfloat16)
        own_qkv[k, :, D:] = jnp.dot(
            own[k], w_qkv[:, D:], preferred_element_type=jnp.float32
        ).astype(jnp.bfloat16)

    @pl.loop(0, jnp.where(heavy, 4, 2) if relayed else 3)
    def _(i):
        project(jnp.where(i == 0, UNIT_A, jnp.where(i == 1, UNIT_B, i - 1)))

    if relayed:

        @pl.when(jnp.logical_and(heavy, jnp.logical_not(near)))
        def _():
            for q in range(2):
                send_piece(q).start()

        @pl.when(jnp.logical_not(heavy))
        def _():
            for h in range(2):
                relay_half(h).wait_recv()
                forward(h).start()
            for q in range(2):
                send_piece(q).start()

            @pl.loop(0, rows_here)
            def _(i):
                for k in (UNIT_C, UNIT_D):
                    result[k, i] = patches[order[k], i]

    weights[1].wait()
    weights[2].wait()

    def mix(k, at, q_regions, k_regions):
        kv_other = jnp.dot(far[k, at], w_qkv[:, D:], preferred_element_type=jnp.float32)
        mixed = attend_slot(
            own_qkv[k, at, :D],
            own_qkv[k, at, D:],
            kv_other.astype(jnp.bfloat16),
            q_regions,
            k_regions,
        )
        return finish_part(embedded[k, at], mixed, w_out[...], o_gain_ref[...])

    wholes = UNIT_B if relayed else UNIT_D

    @pl.loop(0, wholes + 2)
    def _(step):
        k = step
        if relayed:
            swapped = jnp.where(step == UNIT_D, wholes, jnp.where(step == wholes, UNIT_D, step))
            k = jnp.where(near, step, swapped)

        @pl.when(jnp.logical_and(k < wholes, jnp.logical_or(heavy, k == UNIT_A)))
        def _():
            for h in range(2):
                arrival(k, h).wait_recv()

            mixed = mix(k, pl.ds(0, tokens), q_table[...], k_table[...])
            final = from_windows(mixed).astype(jnp.bfloat16)
            place = jnp.where(
                k == UNIT_A, order[UNIT_A], jnp.where(k == UNIT_C, order[UNIT_C], order[UNIT_D])
            )
            flat = patches[place].reshape(tokens, patch_len)
            result[k] = decode_slot(flat, final, w_dec[...]).reshape(rows_here, cols, patch_len)

            turn = jnp.logical_and(near, heavy) if relayed else jnp.logical_not(near)

            @pl.when(jnp.logical_and(k == UNIT_A, turn))
            def _():
                for q in range(2):
                    send_piece(q).start()

        @pl.when(k >= wholes)
        def _():
            q = k - wholes
            send_piece(q).wait_recv()
            finals[part(q)] = mix(UNIT_B, part(q), q_parts[q], k_parts[q])

    for h in range(2):
        send_half(UNIT_A, h).wait_send()
        send_piece(h).wait_send()

    @pl.when(heavy)
    def _():
        for h in range(2):
            send_half(UNIT_C, h).wait_send()
            if relayed:
                relay_half(h).wait_send()

    if relayed:

        @pl.when(jnp.logical_not(heavy))
        def _():
            for h in range(2):
                forward(h).wait_send()


def last_kernel(sample_ref, result, w_dec, finals, new_ref, decoded, sems, row_sems):
    slots, rows_here, cols, patch_len = result.shape
    samples = sample_ref[...]
    order, _ = slot_order([samples[0, b] for b in range(samples.shape[1])], slots)
    copies = [
        pltpu.make_async_copy(result.at[k], new_ref.at[order[k]], sems.at[k])
        for k in (UNIT_A, UNIT_C, UNIT_D)
    ]
    for copy in copies:
        copy.start()
    half = rows_here * cols // 2
    final = from_windows(finals[...]).astype(jnp.bfloat16)
    rows = rows_here // 2
    for h in range(2):
        here = slice(rows * h, rows * (h + 1))
        decoded[here] = decode_slot(
            result[UNIT_B, here].reshape(half, patch_len),
            final[half * h : half * (h + 1)],
            w_dec[...],
        ).reshape(rows, cols, patch_len)
        copies.append(
            pltpu.make_async_copy(
                decoded.at[here], new_ref.at[order[UNIT_B], here], row_sems.at[h]
            )
        )
        copies[-1].start()
    for copy in copies:
        copy.wait()


def local_strips(
    store, sample_index, region_ids, w_embed, attn_gain, w_qkv, w_out, out_gain, w_dec
):
    slots, rows_here, cols, patch_len = store.shape
    tokens = rows_here * cols
    windows = tokens // PER
    held = lambda *shape: pltpu.VMEM(shape, jnp.bfloat16)
    wide = lambda *shape: pltpu.VMEM(shape, jnp.float32)
    vmem = pl.BlockSpec(memory_space=pltpu.VMEM)
    hbm = pl.BlockSpec(memory_space=pltpu.HBM)
    in_hbm = lambda array: pltpu.with_memory_space_constraint(array, pltpu.HBM)
    samples, sample_index, store = sample_index, in_hbm(sample_index), in_hbm(store)
    w_embed, w_qkv, w_out = in_hbm(w_embed), in_hbm(w_qkv), in_hbm(w_out)
    w_dec_t = in_hbm(w_dec.T)
    *first, branch = pl.pallas_call(
        first_kernel,
        in_specs=[hbm] * 4,
        out_specs=[vmem] * 4 + [pl.BlockSpec(memory_space=pltpu.SMEM)],
        out_shape=[
            held(*w_embed.shape),
            held(2, *store.shape[1:]),
            held(tokens, D),
            held(tokens, D),
            pltpu.SMEM((1,), jnp.int32),
        ],
        scratch_shapes=[
            pltpu.SMEM(sample_index.shape, jnp.int32),
            wide(1, D),
            pltpu.SemaphoreType.DMA((5,)),
        ],
        compiler_params=pltpu.CompilerParams(vmem_limit_bytes=FIRST_LIMIT),
    )(sample_index, in_hbm(attn_gain[None]), store, w_embed)
    def exchange_and_place(heavy_owner, *first):
        carried = pl.pallas_call(
            functools.partial(exchange_kernel, heavy_owner),
            in_specs=[hbm] + [vmem] * 7 + [hbm] * 4,
            out_specs=[vmem] * 3,
            out_shape=[
                held(*store.shape),
                held(*w_dec_t.shape),
                wide(tokens, D),
            ],
            scratch_shapes=[
                pltpu.SMEM(sample_index.shape, jnp.int32),
                held(*w_qkv.shape),
                held(*w_out.shape),
                wide(windows, GROUP * PER),
                wide(2 * PER, windows),
                wide(2, windows // 2, GROUP * PER),
                wide(2, 2 * PER, windows // 2),
                held(*store.shape),
                held(slots, tokens, D),
                held(slots, tokens, D),
                held(tokens, D),
                held(slots, tokens, D),
                held(slots, tokens, 3 * D),
                pltpu.SemaphoreType.DMA((slots + 1,)),
                pltpu.SemaphoreType.DMA((3,)),
                pltpu.SemaphoreType.DMA((2,)),
                pltpu.SemaphoreType.DMA((2,)),
                pltpu.SemaphoreType.DMA((slots, 2)),
                pltpu.SemaphoreType.DMA((slots, 2)),
            ],
            compiler_params=pltpu.CompilerParams(
                vmem_limit_bytes=VMEM_LIMIT,
                collective_id=0 if heavy_owner is None else 1 + heavy_owner,
                has_side_effects=True,
            ),
        )(
            sample_index,
            region_ids,
            attn_gain[None],
            out_gain[None],
            *first,
            store,
            w_qkv,
            w_out,
            w_dec_t,
        )
        return pl.pallas_call(
            last_kernel,
            in_specs=[vmem] * 4,
            out_specs=hbm,
            out_shape=pltpu.HBM(store.shape, store.dtype),
            scratch_shapes=[
                held(*store.shape[1:]),
                pltpu.SemaphoreType.DMA((slots,)),
                pltpu.SemaphoreType.DMA((2,)),
            ],
            compiler_params=pltpu.CompilerParams(vmem_limit_bytes=LAST_LIMIT),
        )(samples[None], *carried)

    branches = [functools.partial(exchange_and_place, owner) for owner in (None, 0, 1)]
    return lax.switch(branch[0], branches, *first)


def local(store, sample_index, *rest):
    slots, rows_here = store.shape[:2]
    strips = (
        rows_here == HALF
        and slots == 4
        and lax.axis_size("buf") == 2
        and sample_index.shape[0] == 6
    )
    return (local_strips if strips else local_tiles)(store, sample_index, *rest)


def solution(mesh):
    return jax.shard_map(
        local,
        mesh=mesh,
        in_specs=(P("buf", ("lat", "lon"), None, None), P(), P(), P(), P(), P(), P(), P(), P()),
        out_specs=P("buf", ("lat", "lon"), None, None),
        check_vma=False,
    )
```
